32 devices in a mesh: clips: 2 (over y), seq: 4 (over z), tp: 2 (over x), dp: 2 (over core).
Axes of the slice: x: 2, y: 2, z: 4, core: 2. Of those that a mesh axis runs over, the one named last changes fastest.
Arguments:
- video_query: bfloat16 [4, 512, 4096], P(('clips', 'dp'), 'seq', 'tp'), parts along dimension 0, may hold values from -384 to 384
- video_key: bfloat16 [4, 512, 4096], P(('clips', 'dp'), 'seq', 'tp'), parts along dimension 0, may hold values from -384 to 384
- video_value: bfloat16 [4, 512, 4096], P(('clips', 'dp'), 'seq', 'tp'), parts along dimension 0, may hold values from -6 to 6
- cross_query: bfloat16 [4, 512, 2048], P(('clips', 'dp'), 'seq', 'tp'), parts along dimension 0, may hold values from -384 to 384
- audio_key: bfloat16 [4, 32, 2048], P(('clips', 'dp'), 'seq', 'tp'), parts along dimension 0, may hold values from -384 to 384
- audio_value: bfloat16 [4, 32, 2048], P(('clips', 'dp'), 'seq', 'tp'), parts along dimension 0, may hold values from -6 to 6
- audio_query: bfloat16 [4, 32, 2048], P(('clips', 'dp'), 'seq', 'tp'), parts along dimension 0, may hold values from -384 to 384
- cross_key: bfloat16 [4, 512, 2048], P(('clips', 'dp'), 'seq', 'tp'), parts along dimension 0, may hold values from -384 to 384
- cross_value: bfloat16 [4, 512, 2048], P(('clips', 'dp'), 'seq', 'tp'), parts along dimension 0, may hold values from -6 to 6
- audio_input: bfloat16 [4, 32, 2048], P(('clips', 'dp'), 'seq'), parts along dimension 0, may hold values from -0.29882812 to 0.29882812
- norm_gain: float32 [2048], replicated, may hold values from 0.1 to 1.9
- up_weight: bfloat16 [2048, 8192], P('tp', 'seq'), may hold values from -0.125 to 0.125
- down_weight: bfloat16 [8192, 2048], P('seq', 'tp'), may hold values from -0.0625 to 0.0625
Outputs:
- video_mixed: bfloat16 [4, 512, 4096], P(('clips', 'dp'), 'seq', 'tp'), parts along dimension 0
- video_heard: bfloat16 [4, 512, 2048], P(('clips', 'dp'), 'seq', 'tp'), parts along dimension 0
- audio_seen: bfloat16 [4, 32, 2048], P(('clips', 'dp'), 'seq', 'tp'), parts along dimension 0
- audio_mlp: bfloat16 [4, 32, 2048], P(('clips', 'dp'), 'seq', 'tp'), parts along dimension 0
The draws below stay inside these ranges and needn't reach their ends.
There are 2 independent parts, one for each index of `clips`. The reference program is written for one: setup_inputs(seed, part) draws one part's arguments, and reference() takes and returns one part's arrays. A program takes and returns all parts, laid end to end along the dimension named above; an argument that names none is the same for every part. Nothing has to cross between parts.
All inputs are finite; a program needn't handle non-finite values.
Results may differ from the reference program's by a relative error of at most 0.013.
Values may be sent and summed in bfloat16 or wider, within the bound.
No kernel may reach another device: no remote copies, remote signals or barrier semaphores. Data moves between devices by JAX's collectives and lax.ppermute only.
A program may use at most 64 MiB of HBM per device.

```python
import math
import jax
import jax.numpy as jnp
from jax import lax

VHEADS = 32
VHEAD = 128
CHEADS = 32
CHEAD = 64
FFA = 8192
BATCH = 2
VWIDTH = 4096
AUDIO_D = 2048
VIDEO_LEN = 512
AUDIO_LEN = 32


def make_pair(base_key, query_rows, key_rows, head_count, head_size):
    key_query, key_keys = jax.random.split(base_key, 2)
    queries = jnp.clip(jax.random.normal(key_query, (BATCH, query_rows, head_count, head_size), jnp.float32), -4.0, 4.0)
    keys_out = 2.0 * jnp.clip(jax.random.normal(key_keys, (BATCH, key_rows, head_count, head_size), jnp.float32), -4.0, 4.0)
    return (queries.reshape(BATCH, query_rows, head_count * head_size), keys_out.reshape(BATCH, key_rows, head_count * head_size))


def draw_video_query(key, part):
    return make_pair(jax.random.fold_in(key, 11), VIDEO_LEN, VIDEO_LEN, VHEADS, VHEAD)[0].astype(jnp.bfloat16)


def draw_video_key(key, part):
    return make_pair(jax.random.fold_in(key, 11), VIDEO_LEN, VIDEO_LEN, VHEADS, VHEAD)[1].astype(jnp.bfloat16)


def draw_cross_query(key, part):
    return make_pair(jax.random.fold_in(key, 12), VIDEO_LEN, AUDIO_LEN, CHEADS, CHEAD)[0].astype(jnp.bfloat16)


def draw_audio_key(key, part):
    return make_pair(jax.random.fold_in(key, 12), VIDEO_LEN, AUDIO_LEN, CHEADS, CHEAD)[1].astype(jnp.bfloat16)


def draw_audio_query(key, part):
    return make_pair(jax.random.fold_in(key, 13), AUDIO_LEN, VIDEO_LEN, CHEADS, CHEAD)[0].astype(jnp.bfloat16)


def draw_cross_key(key, part):
    return make_pair(jax.random.fold_in(key, 13), AUDIO_LEN, VIDEO_LEN, CHEADS, CHEAD)[1].astype(jnp.bfloat16)


def steps_of(key, shape, shards, least, largest):
    factor_of = 1.0
    for axis_at, shards_of in shards:
        steps = jax.random.uniform(jax.random.fold_in(jax.random.fold_in(key, 6), axis_at), (shards_of,), jnp.float32, least / len(shards), largest / len(shards))
        factor_of = factor_of * jnp.repeat(jnp.exp(steps), shape[axis_at] // shards_of).reshape((-1,) + (1,) * (len(shape) - 1 - axis_at))
    return factor_of


def bell_draw(rng, shape, spread, limit, shards=(), kind=jnp.bfloat16):
    factor_of = steps_of(rng, shape, shards, -0.22, 0.18) if shards else 1.0
    values = jax.random.normal(rng, shape, jnp.float32) * spread * factor_of
    return jnp.minimum(jnp.maximum(values, -limit), limit).astype(kind)


def setup_inputs(seed: int = 0, part: int = 0) -> dict:
    arg_keys = jax.random.split(jax.random.key(seed), 14)
    part_splits = jax.random.split(jax.random.fold_in(arg_keys[13], part), 14)
    video_query = draw_video_query(jax.random.fold_in(jax.random.fold_in(arg_keys[13], part), 71), part)
    video_key = draw_video_key(jax.random.fold_in(jax.random.fold_in(arg_keys[13], part), 71), part)
    video_value = bell_draw(part_splits[2], (BATCH, VIDEO_LEN, VWIDTH), 1.0, 6.0, ((0, 2), (1, 4), (2, 2)))
    cross_query = draw_cross_query(jax.random.fold_in(jax.random.fold_in(arg_keys[13], part), 71), part)
    audio_key = draw_audio_key(jax.random.fold_in(jax.random.fold_in(arg_keys[13], part), 71), part)
    audio_value = bell_draw(part_splits[5], (BATCH, AUDIO_LEN, AUDIO_D), 1.0, 6.0, ((0, 2), (1, 4), (2, 2)))
    audio_query = draw_audio_query(jax.random.fold_in(jax.random.fold_in(arg_keys[13], part), 71), part)
    cross_key = draw_cross_key(jax.random.fold_in(jax.random.fold_in(arg_keys[13], part), 71), part)
    cross_value = bell_draw(part_splits[8], (BATCH, VIDEO_LEN, AUDIO_D), 1.0, 6.0, ((0, 2), (1, 4), (2, 2)))
    audio_input = jnp.clip(jax.random.uniform(part_splits[9], (BATCH, AUDIO_LEN, AUDIO_D), jnp.float32, -0.29882812, 0.29882812) * steps_of(part_splits[9], (BATCH, AUDIO_LEN, AUDIO_D), ((0, 2), (1, 4)), -0.4, 0.0), -0.29882812, 0.29882812).astype(jnp.bfloat16)
    norm_gain = jnp.clip(1.0 + 0.18 * jax.random.normal(arg_keys[10], (AUDIO_D,), jnp.float32), 0.1, 1.9)
    up_weight = bell_draw(arg_keys[11], (AUDIO_D, FFA), AUDIO_D ** -0.5, 0.125, ((0, 2), (1, 4)))
    down_weight = bell_draw(arg_keys[12], (FFA, AUDIO_D), FFA ** -0.5, 0.0625, ((0, 4), (1, 2)))
    return dict(video_query=video_query, video_key=video_key, video_value=video_value, cross_query=cross_query, audio_key=audio_key, audio_value=audio_value, audio_query=audio_query, cross_key=cross_key, cross_value=cross_value, audio_input=audio_input, norm_gain=norm_gain, up_weight=up_weight, down_weight=down_weight)


def attend_rows(queries, keys_in, values_in, head_count):
    head_size = queries.shape[1] // head_count
    query_heads = queries.reshape(queries.shape[0], head_count, head_size).astype(jnp.float32)
    key_heads = keys_in.reshape(keys_in.shape[0], head_count, head_size).astype(jnp.float32)
    value_heads = values_in.reshape(values_in.shape[0], head_count, head_size).astype(jnp.float32)
    scores = jnp.einsum('qhd,khd->qhk', query_heads, key_heads) / math.sqrt(head_size)
    peak_value = lax.optimization_barrier(jnp.max(scores, axis=2, keepdims=True))
    weights = jnp.exp(scores - peak_value)
    totals = lax.optimization_barrier(jnp.sum(weights, axis=2))
    rounded = lax.optimization_barrier(weights.astype(jnp.bfloat16)).astype(jnp.float32)
    weighted = jnp.einsum('qhk,khd->qhd', rounded, value_heads)
    result = weighted / totals[:, :, None]
    return result.reshape(queries.shape[0], head_count * head_size).astype(jnp.bfloat16)

def attend(queries, keys_in, values_in, head_count):
    row_total = queries.shape[0]
    block_rows = 512 if row_total % 512 == 0 else row_total
    pieces = queries.reshape(row_total // block_rows, block_rows, queries.shape[1])
    result = lax.map(lambda row_piece: attend_rows(row_piece, keys_in, values_in, head_count), pieces)
    return result.reshape(row_total, queries.shape[1])

def reference(video_query, video_key, video_value, cross_query, audio_key, audio_value, audio_query, cross_key, cross_value, audio_input, norm_gain, up_weight, down_weight):
    mixed_list, heard_list, seen_list, output_list = ([], [], [], [])
    for sample in range(BATCH):
        mixed_list.append(attend(video_query[sample], video_key[sample], video_value[sample], VHEADS))
        heard_list.append(attend(cross_query[sample], audio_key[sample], audio_value[sample], CHEADS))
        audio_seen = attend(audio_query[sample], cross_key[sample], cross_value[sample], CHEADS)
        seen_list.append(audio_seen)
        residual = audio_input[sample].astype(jnp.float32) + audio_seen.astype(jnp.float32)
        scale_factor = lax.rsqrt(lax.optimization_barrier(jnp.mean(residual * residual, axis=1, keepdims=True)) + 1e-06)
        normed = (residual * scale_factor * norm_gain.astype(jnp.float32)).astype(jnp.bfloat16)
        hidden = jax.nn.gelu(jnp.dot(normed, up_weight, preferred_element_type=jnp.float32)).astype(jnp.bfloat16)
        output_list.append(jnp.dot(hidden, down_weight, preferred_element_type=jnp.float32).astype(jnp.bfloat16))
    return (jnp.stack(mixed_list), jnp.stack(heard_list), jnp.stack(seen_list), jnp.stack(output_list))
```

```python
import functools
import math

import jax
import jax.numpy as jnp
from jax import lax
from jax.experimental import pallas as pl
from jax.experimental.pallas import tpu as pltpu
from jax.sharding import PartitionSpec as P

VHEAD = 128
CHEAD = 64
LANES = 128
F32 = jnp.float32
BF16 = jnp.bfloat16
LOG2E = math.log2(math.e)
MIB = 1024 * 1024
NT = (((1,), (1,)), ((), ()))
TN = (((0,), (0,)), ((), ()))


def attend_rows(queries, keys_in, values_in, head_count):
    head_size = queries.shape[1] // head_count
    query_heads = queries.reshape(queries.shape[0], head_count, head_size)
    key_heads = keys_in.reshape(keys_in.shape[0], head_count, head_size)
    value_heads = values_in.reshape(values_in.shape[0], head_count, head_size)
    scores = jnp.einsum(
        "qhd,khd->qhk", query_heads, key_heads, preferred_element_type=jnp.float32
    ) / math.sqrt(head_size)
    peak_value = jnp.max(scores, axis=2, keepdims=True)
    weights = jnp.exp(scores - peak_value)
    totals = jnp.sum(weights, axis=2)
    weighted = jnp.einsum(
        "qhk,khd->qhd",
        weights.astype(jnp.bfloat16),
        value_heads,
        preferred_element_type=jnp.float32,
    )
    result = weighted / totals[:, :, None]
    return result.reshape(queries.shape[0], head_count * head_size).astype(jnp.bfloat16)


def attend(queries, keys_in, values_in, head_count):
    row_total = queries.shape[0]
    block_rows = 512 if row_total % 512 == 0 else row_total
    pieces = queries.reshape(row_total // block_rows, block_rows, queries.shape[1])
    result = lax.map(
        lambda row_piece: attend_rows(row_piece, keys_in, values_in, head_count), pieces
    )
    return result.reshape(row_total, queries.shape[1])


def video_self(queries, keys_in, values_in):
    seq_count = lax.axis_size("seq")
    local_heads = queries.shape[1] // VHEAD
    dest_heads = max(local_heads // seq_count, 1)
    blocks = seq_count * dest_heads // local_heads
    groups = local_heads // dest_heads
    group_width = dest_heads * VHEAD
    token_count = queries.shape[0]
    block_tokens = token_count // blocks

    def spread(tensor):
        shaped = tensor.reshape(token_count, groups, group_width).transpose(1, 0, 2)
        shaped = jnp.broadcast_to(shaped[:, None], (groups, blocks, token_count, group_width))
        return shaped.reshape(seq_count, token_count, group_width)

    shaped = queries.reshape(blocks, block_tokens, groups, group_width).transpose(2, 0, 1, 3)
    own_queries = lax.all_to_all(
        shaped.reshape(seq_count, block_tokens, group_width),
        "seq",
        split_axis=0,
        concat_axis=0,
        tiled=True,
    )
    keys_all = lax.all_to_all(spread(keys_in), "seq", split_axis=0, concat_axis=0, tiled=True)
    values_all = lax.all_to_all(spread(values_in), "seq", split_axis=0, concat_axis=0, tiled=True)
    keys_all = keys_all.reshape(-1, group_width)
    values_all = values_all.reshape(-1, group_width)
    own_queries = own_queries.reshape(-1, group_width)
    attended = attend(own_queries, keys_all, values_all, dest_heads)
    returned = lax.all_to_all(
        attended.reshape(seq_count, block_tokens, group_width),
        "seq",
        split_axis=0,
        concat_axis=0,
        tiled=True,
    )
    returned = returned.reshape(groups, blocks, block_tokens, group_width).transpose(1, 2, 0, 3)
    return returned.reshape(token_count, groups * group_width)


def audio_listen(queries, keys_in, values_in, head_count):
    head_size = queries.shape[1] // head_count
    query_heads = queries.reshape(queries.shape[0], head_count, head_size)
    key_heads = keys_in.reshape(keys_in.shape[0], head_count, head_size)
    value_heads = values_in.reshape(values_in.shape[0], head_count, head_size)
    scores = jnp.einsum(
        "qhd,khd->qhk", query_heads, key_heads, preferred_element_type=jnp.float32
    ) / math.sqrt(head_size)
    local_peak = jnp.max(scores, axis=2)
    peak_value = lax.pmax(local_peak, "seq")
    weights = jnp.exp(scores - peak_value[:, :, None])
    totals = jnp.sum(weights, axis=2)
    weighted = jnp.einsum(
        "qhk,khd->qhd",
        weights.astype(jnp.bfloat16),
        value_heads,
        preferred_element_type=jnp.float32,
    )
    weighted = weighted.reshape(queries.shape[0], head_count * head_size)
    totals = lax.psum_scatter(totals, "seq", scatter_dimension=0, tiled=True)
    weighted = lax.psum_scatter(weighted, "seq", scatter_dimension=0, tiled=True)
    return (weighted / jnp.repeat(totals, head_size, axis=1)).astype(jnp.bfloat16)


def audio_block(audio_rows, audio_seen, norm_gain, up_weight, down_weight):
    features = lax.all_gather(audio_seen, "tp", axis=1, tiled=True)
    residual = audio_rows.astype(jnp.float32) + features.astype(jnp.float32)
    scale_factor = lax.rsqrt(jnp.mean(residual * residual, axis=1, keepdims=True) + 1e-06)
    normed = (residual * scale_factor * norm_gain).astype(jnp.bfloat16)
    slice_width = up_weight.shape[0]
    own_features = lax.dynamic_slice_in_dim(
        normed, lax.axis_index("tp") * slice_width, slice_width, 1
    )
    partial_sum = jnp.dot(
        lax.all_gather(own_features, "seq", axis=0, tiled=True),
        up_weight,
        preferred_element_type=jnp.float32,
    )
    hidden = jax.nn.gelu(lax.psum(partial_sum, "tp")).astype(jnp.bfloat16)
    return lax.psum_scatter(
        jnp.dot(hidden, down_weight, preferred_element_type=jnp.float32),
        "seq",
        scatter_dimension=0,
        tiled=True,
    ).astype(jnp.bfloat16)


def general_body(vq, vk, vv, cq, ak, av, aq, ck, cv, ai, gain, up, down):
    cross_heads = cq.shape[1] // CHEAD
    mixed = video_self(vq, vk, vv)
    gathered_query = lax.all_gather(aq, "seq", axis=0, tiled=True)
    gathered_key = lax.all_gather(ak, "seq", axis=0, tiled=True)
    gathered_value = lax.all_gather(av, "seq", axis=0, tiled=True)
    heard = attend(cq, gathered_key, gathered_value, cross_heads)
    seen = audio_listen(gathered_query, ck, cv, cross_heads)
    mlp = audio_block(ai, seen, gain, up, down)
    return mixed, heard, seen, mlp


def vmem():
    return pl.BlockSpec(memory_space=pltpu.VMEM)


def smem():
    return pl.BlockSpec(memory_space=pltpu.SMEM)


def sds(shape, dtype=BF16):
    return jax.ShapeDtypeStruct(shape, dtype)


def call(kernel, ins, outs, flops=0, moved=0, limit=32, scalars=0):
    return pl.pallas_call(
        kernel,
        out_shape=tuple(outs),
        in_specs=[smem()] * scalars + [vmem()] * (len(ins) - scalars),
        out_specs=tuple(vmem() for _ in outs),
        compiler_params=pltpu.CompilerParams(vmem_limit_bytes=limit * MIB),
        cost_estimate=pl.CostEstimate(flops=flops, bytes_accessed=moved, transcendentals=0),
    )(*ins)


def shift(value, by):
    n = lax.axis_size("seq")
    return lax.ppermute(value, "seq", [(i, (i + by) % n) for i in range(n)])


def parts3(value):
    first = value.astype(BF16).astype(F32)
    second = (value - first).astype(BF16).astype(F32)
    return first, second, value - first - second


def pack_kernel(n, first, width, with_audio, place, q, k, v, *rest):
    audio, outs = (rest[:3], rest[3:]) if with_audio else ((), rest)
    tokens = q.shape[0]
    group = q.shape[1] // n
    me = place[0]
    if with_audio:
        key, value, line = audio
        half = key.shape[1]
        mine = line[:, pl.ds(pl.multiple_of(place[1] * half, LANES), half)].astype(F32)
        rows = []
        for part in (key[...].astype(F32), value[...].astype(F32), mine):
            rows += [part[:, c : c + width] for c in range(0, half, width)]
        extra = jnp.concatenate(rows, axis=0).astype(BF16)
    for s in range(n):
        dest = lax.rem(me + s, n)
        at = pl.ds(pl.multiple_of(dest * group + first, LANES), width)
        for i, ref in enumerate((q, k, v)):
            outs[s][i * tokens : (i + 1) * tokens, :] = ref[:, at]
        if with_audio:
            outs[s][3 * tokens :, :] = extra


def unfold(tail, index, rows, columns, width):
    per = columns // width
    return jnp.concatenate(
        [tail[(index * per + c) * rows : (index * per + c + 1) * rows] for c in range(per)], axis=1
    )


def attend_kernel(n, tokens, *refs):
    pieces, outs = refs[:n], refs[n:]
    width = pieces[0].shape[1]
    scale = LOG2E / math.sqrt(VHEAD)
    for h in range(width // VHEAD):
        cols = slice(h * VHEAD, (h + 1) * VHEAD)
        keys = jnp.concatenate([p[tokens : 2 * tokens, cols] for p in pieces], axis=0)
        values = jnp.concatenate([p[2 * tokens : 3 * tokens, cols] for p in pieces], axis=0)
        for p, out in zip(pieces, outs):
            s = lax.dot_general(p[0:tokens, cols], keys, NT, preferred_element_type=F32)
            s = s * scale
            w = jnp.exp2(s - jnp.max(s, axis=1, keepdims=True))
            total = jnp.sum(w, axis=1, keepdims=True)
            o = jnp.dot(w.astype(BF16), values, preferred_element_type=F32)
            out[:, cols] = (o / total).astype(BF16)


def unpack_kernel(n, widths, place, *refs):
    pieces, out = refs[:-1], refs[-1]
    me = place[0]
    group = sum(widths)
    first = 0
    for c, width in enumerate(widths):
        for s in range(n):
            dest = lax.rem(me + s, n)
            at = pl.ds(pl.multiple_of(dest * group + first, LANES), width)
            out[:, at] = pieces[c * n + s][...]
        first += width


def low_half(shape):
    return lax.broadcasted_iota(jnp.int32, shape, 1) < CHEAD


def listen_kernel(n, *refs):
    queries, keys, values, out = refs[:n], refs[n], refs[n + 1], refs[n + 2]
    columns = keys.shape[1]
    q = jnp.concatenate([p[...].astype(F32) for p in queries], axis=0)
    rows = q.shape[0]
    scale = LOG2E / math.sqrt(CHEAD)
    low = low_half((rows, LANES))
    lane = lax.broadcasted_iota(jnp.int32, (rows, LANES), 1)
    stats = jnp.zeros((rows, LANES), F32)
    heads = columns // CHEAD
    for pair in range(columns // LANES):
        cols = slice(pair * LANES, (pair + 1) * LANES)
        qp = q[:, cols]
        both = jnp.concatenate([jnp.where(low, qp, 0.0), jnp.where(low, 0.0, qp)], axis=0)
        s = lax.dot_general(both.astype(BF16), keys[:, cols], NT, preferred_element_type=F32)
        s = s * scale
        peak = jnp.max(s, axis=1, keepdims=True)
        w = jnp.exp2(s - peak)
        total = jnp.sum(w, axis=1, keepdims=True)
        o = jnp.dot(w.astype(BF16), values[:, cols], preferred_element_type=F32) / total
        out[:, cols] = jnp.where(low, o[:rows], o[rows:]).astype(BF16)
        for i in range(2):
            head = 2 * pair + i
            sel = slice(i * rows, (i + 1) * rows)
            for j, part in enumerate(parts3(peak[sel]) + parts3(total[sel])):
                stats = jnp.where(lane == j * heads + head, part, stats)
    out[:, columns:] = stats.astype(BF16)


def combine_kernel(n, tokens, rows, *refs):
    got, pieces = refs[:n], refs[n : 2 * n]
    gain, up = refs[2 * n], refs[2 * n + 1]
    own_sum, sent_sum, seen, x_ref = refs[2 * n + 2 :]

    @pl.when(pl.program_id(0) == 0)
    def _():
        columns = seen.shape[1]
        heads = columns // CHEAD
        width = pieces[0].shape[1]
        peaks, totals, parts = [], [], []
        for s in range(n):
            whole = got[s][...].astype(F32)
            if s:
                whole = jnp.concatenate([whole[-s * rows :], whole[: -s * rows]], axis=0)
            whole, stats = whole[:, :columns], whole[:, columns:]
            piece = [stats[:, j * heads : (j + 1) * heads] for j in range(6)]
            peaks.append(piece[0] + piece[1] + piece[2])
            totals.append(piece[3] + piece[4] + piece[5])
            parts.append(whole)
        top = functools.reduce(jnp.maximum, peaks)
        weight = [t * jnp.exp2(p - top) for t, p in zip(totals, peaks)]
        every = functools.reduce(jnp.add, weight)
        weight = [w / every for w in weight]
        tails = [p[3 * tokens :, :].astype(F32) for p in pieces]
        line = jnp.concatenate([unfold(t, 2, rows, columns, width) for t in tails], axis=0)
        low = low_half((n * rows, LANES))
        square = jnp.zeros((n * rows, 1), F32)
        for pair in range(columns // LANES):
            cols = slice(pair * LANES, (pair + 1) * LANES)
            o = jnp.zeros((n * rows, LANES), F32)
            for w, part in zip(weight, parts):
                a, b = w[:, 2 * pair : 2 * pair + 1], w[:, 2 * pair + 1 : 2 * pair + 2]
                o = o + jnp.where(low, a, b) * part[:, cols]
            o = o.astype(BF16)
            seen[:, cols] = o[:rows]
            residual = line[:, cols] + o.astype(F32)
            square = square + jnp.sum(residual * residual, axis=1, keepdims=True)
            x_ref[:, cols] = (residual * gain[:, cols]).astype(BF16)
        lane = lax.broadcasted_iota(jnp.int32, (n * rows, LANES), 1)
        first, second, third = parts3(square)
        spread = jnp.where(lane == 0, first, jnp.where(lane == 1, second, third))
        spread = jnp.where(lane < 3, spread, 0.0)
        own_sum[0, :, :LANES] = spread
        sent_sum[0, :, :LANES] = spread.astype(BF16)

    @pl.when(pl.program_id(0) > 0)
    def _():
        product = jnp.dot(x_ref[...], up[...], preferred_element_type=F32)
        own_sum[0] = product
        sent_sum[0] = product.astype(BF16)


def combine(got, pieces, gain, up, tokens, rows, block):
    n = len(got)
    columns, units = up.shape
    steps = units // block + 1
    held = lambda ref: pl.BlockSpec(ref.shape, lambda i: (0,) * ref.ndim)
    moved = pl.BlockSpec((1, n * rows, block), lambda i: (i, 0, 0))
    return pl.pallas_call(
        functools.partial(combine_kernel, n, tokens, rows),
        grid=(steps,),
        out_shape=(
            sds((steps, n * rows, block), F32),
            sds((steps, n * rows, block)),
            sds((rows, columns)),
        ),
        in_specs=[held(r) for r in (*got, *pieces, gain)]
        + [pl.BlockSpec((columns, block), lambda i: (0, jnp.maximum(i - 1, 0)))],
        out_specs=(moved, moved, pl.BlockSpec((rows, columns), lambda i: (0, 0))),
        scratch_shapes=[pltpu.VMEM((n * rows, columns), BF16)],
        compiler_params=pltpu.CompilerParams(vmem_limit_bytes=32 * MIB),
        cost_estimate=pl.CostEstimate(
            flops=8 * n * rows * columns * units, bytes_accessed=4 * columns * units, transcendentals=0
        ),
    )(*got, *pieces, gain, up)


def finish_kernel(n, features, own, other, down, *refs):
    outs, hidden = refs[:n], refs[n]
    rows = outs[0].shape[0]

    @pl.when(pl.program_id(0) == 0)
    def _():
        square = own[0, :, :LANES] + other[0, :, :LANES].astype(F32)
        square = jnp.sum(square, axis=1, keepdims=True)
        scale = lax.rsqrt(square / features + 1e-6)
        block = own.shape[2]
        for i in range(1, own.shape[0]):
            total = (own[i] + other[i].astype(F32)) * scale
            hidden[:, (i - 1) * block : i * block] = jax.nn.gelu(total).astype(BF16)

    product = jnp.dot(hidden[...], down[...], preferred_element_type=F32)
    for s in range(n):
        outs[s][...] = product[s * rows : (s + 1) * rows].astype(outs[s].dtype)


def finish(own, other, down, n, rows, features, block):
    units, columns = down.shape
    held = lambda ref: pl.BlockSpec(ref.shape, lambda i: (0,) * ref.ndim)
    return pl.pallas_call(
        functools.partial(finish_kernel, n, features),
        grid=(columns // block,),
        out_shape=(sds((rows, columns), F32),) + (sds((rows, columns)),) * (n - 1),
        in_specs=[held(own), held(other), pl.BlockSpec((units, block), lambda i: (0, i))],
        out_specs=(pl.BlockSpec((rows, block), lambda i: (0, i)),) * n,
        scratch_shapes=[pltpu.VMEM((n * rows, units), BF16)],
        compiler_params=pltpu.CompilerParams(vmem_limit_bytes=32 * MIB),
        cost_estimate=pl.CostEstimate(
            flops=8 * n * rows * columns * units, bytes_accessed=4 * columns * units, transcendentals=0
        ),
    )(own, other, down)


def heard_kernel(n, tokens, rows, q, *refs):
    pieces, out = refs[:n], refs[n]
    columns = q.shape[1]
    width = pieces[0].shape[1]
    tails = [p[3 * tokens :, :].astype(F32) for p in pieces]
    keys = jnp.concatenate([unfold(t, 0, rows, columns, width) for t in tails], axis=0)
    values = jnp.concatenate([unfold(t, 1, rows, columns, width) for t in tails], axis=0)
    count = n * rows
    low = low_half((count, LANES))
    scale = LOG2E / math.sqrt(CHEAD)
    for pair in range(columns // LANES):
        cols = slice(pair * LANES, (pair + 1) * LANES)

        def both(x):
            x = x[:, cols]
            return jnp.concatenate([jnp.where(low, x, 0.0), jnp.where(low, 0.0, x)], axis=0).astype(BF16)

        s = lax.dot_general(both(keys), q[:, cols], NT, preferred_element_type=F32) * scale
        probs = []
        for i in range(2):
            t = s[i * count : (i + 1) * count]
            w = jnp.exp2(t - jnp.max(t, axis=0, keepdims=True))
            probs.append(w / jnp.sum(w, axis=0, keepdims=True))
        w = jnp.concatenate(probs, axis=0).astype(BF16)
        out[:, cols] = lax.dot_general(w, both(values), TN, preferred_element_type=F32).astype(BF16)


def add_kernel(own, *refs):
    total = own[...]
    for ref in refs[:-1]:
        total = total + ref[...].astype(F32)
    refs[-1][...] = total.astype(BF16)


def short_body(vq, vk, vv, cq, ak, av, aq, ck, cv, ai, gain, up, down):
    n = lax.axis_size("seq")
    tokens = vq.shape[0]
    rows = aq.shape[0]
    columns = aq.shape[1]
    features = ai.shape[1]
    tp = lax.axis_index("tp")
    place = jnp.stack([lax.axis_index("seq"), tp]).astype(jnp.int32)
    group = vq.shape[1] // n
    head_split = [group // VHEAD // 2 * VHEAD, group - group // VHEAD // 2 * VHEAD]
    video_bytes = 6 * vq.size

    queries = [aq] + [shift(aq, s) for s in range(1, n)]

    wide = head_split[0]
    extra = 3 * rows * columns // wide
    packed = call(
        functools.partial(pack_kernel, n, 0, wide, True),
        (place, vq, vk, vv, ak, av, ai),
        [sds((3 * tokens + extra, wide))] * n,
        moved=video_bytes,
        scalars=1,
    )
    chunk_a = [packed[0]] + [shift(packed[s], s) for s in range(1, n)]

    (share,) = call(
        functools.partial(listen_kernel, n),
        (*queries, ck, cv),
        [sds((n * rows, columns + LANES))],
        flops=8 * n * rows * tokens * columns,
        moved=4 * ck.size,
    )
    shares = [share] + [shift(share, s) for s in range(1, n)]

    wide_b = head_split[1]
    packed_b = call(
        functools.partial(pack_kernel, n, wide, wide_b, False),
        (place, vq, vk, vv),
        [sds((3 * tokens, wide_b))] * n,
        moved=video_bytes,
        scalars=1,
    )
    chunk_b = [packed_b[0]] + [shift(packed_b[s], s) for s in range(1, n)]

    own_gain = lax.dynamic_slice_in_dim(gain.reshape(1, -1), tp * columns, columns, 1)
    own_sum, sent_sum, seen = combine(shares, chunk_a, own_gain, up, tokens, rows, 512)
    other_sum = lax.ppermute(sent_sum, "tp", [(0, 1), (1, 0)])
    results = finish(own_sum, other_sum, down, n, rows, features, 512)
    back = [results[0]] + [shift(results[s], -s) for s in range(1, n)]
    (mlp,) = call(add_kernel, back, [sds((rows, columns))])

    flops = 8 * n * n * tokens * tokens
    def attended(chunk, width):
        outs = call(
            functools.partial(attend_kernel, n, tokens),
            chunk,
            [sds((tokens, width))] * n,
            flops=flops * width,
            moved=4 * n * tokens * width * 2,
        )
        return [outs[0]] + [shift(outs[s], -s) for s in range(1, n)]

    mixed_a = attended(chunk_a, wide)
    (heard,) = call(
        functools.partial(heard_kernel, n, tokens, rows),
        (cq, *chunk_a),
        [sds(cq.shape)],
        flops=8 * n * rows * cq.size,
        moved=4 * cq.size,
    )
    mixed_b = attended(chunk_b, wide_b)
    (mixed,) = call(
        functools.partial(unpack_kernel, n, head_split),
        (place, *mixed_a, *mixed_b),
        [sds(vq.shape)],
        moved=4 * vq.size,
        scalars=1,
    )
    return mixed, heard, seen, mlp


def fits(vq, cq, aq, up, down):
    n = lax.axis_size("seq")
    heads = vq.shape[1] // VHEAD
    return (
        1 < n <= 8
        and lax.axis_size("tp") == 2
        and heads % (2 * n) == 0
        and vq.shape[0] == LANES
        and n * vq.shape[0] <= 1024
        and aq.shape[0] % 8 == 0
        and n * aq.shape[0] <= 64
        and 6 * (aq.shape[1] // CHEAD) <= LANES
        and aq.shape[1] % (heads // n // 2 * VHEAD) == 0
        and up.shape[1] % 512 == 0
        and down.shape[1] % 512 == 0
    )


def body(*args):
    *arrays, gain, up, down = args
    arrays = [a[0] for a in arrays]
    path = short_body if fits(arrays[0], arrays[3], arrays[6], up, down) else general_body
    return tuple(out[None] for out in path(*arrays, gain, up, down))


def solution(mesh):
    rows = P(("clips", "dp"), "seq", "tp")
    placed = (rows,) * 9 + (P(("clips", "dp"), "seq", None), P(), P("tp", "seq"), P("seq", "tp"))
    return jax.shard_map(
        body, mesh=mesh, in_specs=placed, out_specs=(rows,) * 4, check_vma=False
    )
```

```python
import functools
import math

import jax
import jax.numpy as jnp
from jax import lax
from jax.experimental import pallas as pl
from jax.experimental.pallas import tpu as pltpu
from jax.sharding import PartitionSpec as P

VHEAD = 128
CHEAD = 64
LANES = 128
F32 = jnp.float32
BF16 = jnp.bfloat16
LOG2E = math.log2(math.e)
MIB = 1024 * 1024
NT = (((1,), (1,)), ((), ()))
TN = (((0,), (0,)), ((), ()))


def attend_rows(queries, keys_in, values_in, head_count):
    head_size = queries.shape[1] // head_count
    query_heads = queries.reshape(queries.shape[0], head_count, head_size)
    key_heads = keys_in.reshape(keys_in.shape[0], head_count, head_size)
    value_heads = values_in.reshape(values_in.shape[0], head_count, head_size)
    scores = jnp.einsum(
        "qhd,khd->qhk", query_heads, key_heads, preferred_element_type=jnp.float32
    ) / math.sqrt(head_size)
    peak_value = jnp.max(scores, axis=2, keepdims=True)
    weights = jnp.exp(scores - peak_value)
    totals = jnp.sum(weights, axis=2)
    weighted = jnp.einsum(
        "qhk,khd->qhd",
        weights.astype(jnp.bfloat16),
        value_heads,
        preferred_element_type=jnp.float32,
    )
    result = weighted / totals[:, :, None]
    return result.reshape(queries.shape[0], head_count * head_size).astype(jnp.bfloat16)


def attend(queries, keys_in, values_in, head_count):
    row_total = queries.shape[0]
    block_rows = 512 if row_total % 512 == 0 else row_total
    pieces = queries.reshape(row_total // block_rows, block_rows, queries.shape[1])
    result = lax.map(
        lambda row_piece: attend_rows(row_piece, keys_in, values_in, head_count), pieces
    )
    return result.reshape(row_total, queries.shape[1])


def video_self(queries, keys_in, values_in):
    seq_count = lax.axis_size("seq")
    local_heads = queries.shape[1] // VHEAD
    dest_heads = max(local_heads // seq_count, 1)
    blocks = seq_count * dest_heads // local_heads
    groups = local_heads // dest_heads
    group_width = dest_heads * VHEAD
    token_count = queries.shape[0]
    block_tokens = token_count // blocks

    def spread(tensor):
        shaped = tensor.reshape(token_count, groups, group_width).transpose(1, 0, 2)
        shaped = jnp.broadcast_to(shaped[:, None], (groups, blocks, token_count, group_width))
        return shaped.reshape(seq_count, token_count, group_width)

    shaped = queries.reshape(blocks, block_tokens, groups, group_width).transpose(2, 0, 1, 3)
    own_queries = lax.all_to_all(
        shaped.reshape(seq_count, block_tokens, group_width),
        "seq",
        split_axis=0,
        concat_axis=0,
        tiled=True,
    )
    keys_all = lax.all_to_all(spread(keys_in), "seq", split_axis=0, concat_axis=0, tiled=True)
    values_all = lax.all_to_all(spread(values_in), "seq", split_axis=0, concat_axis=0, tiled=True)
    keys_all = keys_all.reshape(-1, group_width)
    values_all = values_all.reshape(-1, group_width)
    own_queries = own_queries.reshape(-1, group_width)
    attended = attend(own_queries, keys_all, values_all, dest_heads)
    returned = lax.all_to_all(
        attended.reshape(seq_count, block_tokens, group_width),
        "seq",
        split_axis=0,
        concat_axis=0,
        tiled=True,
    )
    returned = returned.reshape(groups, blocks, block_tokens, group_width).transpose(1, 2, 0, 3)
    return returned.reshape(token_count, groups * group_width)


def audio_listen(queries, keys_in, values_in, head_count):
    head_size = queries.shape[1] // head_count
    query_heads = queries.reshape(queries.shape[0], head_count, head_size)
    key_heads = keys_in.reshape(keys_in.shape[0], head_count, head_size)
    value_heads = values_in.reshape(values_in.shape[0], head_count, head_size)
    scores = jnp.einsum(
        "qhd,khd->qhk", query_heads, key_heads, preferred_element_type=jnp.float32
    ) / math.sqrt(head_size)
    local_peak = jnp.max(scores, axis=2)
    peak_value = lax.pmax(local_peak, "seq")
    weights = jnp.exp(scores - peak_value[:, :, None])
    totals = jnp.sum(weights, axis=2)
    weighted = jnp.einsum(
        "qhk,khd->qhd",
        weights.astype(jnp.bfloat16),
        value_heads,
        preferred_element_type=jnp.float32,
    )
    weighted = weighted.reshape(queries.shape[0], head_count * head_size)
    totals = lax.psum_scatter(totals, "seq", scatter_dimension=0, tiled=True)
    weighted = lax.psum_scatter(weighted, "seq", scatter_dimension=0, tiled=True)
    return (weighted / jnp.repeat(totals, head_size, axis=1)).astype(jnp.bfloat16)


def audio_block(audio_rows, audio_seen, norm_gain, up_weight, down_weight):
    features = lax.all_gather(audio_seen, "tp", axis=1, tiled=True)
    residual = audio_rows.astype(jnp.float32) + features.astype(jnp.float32)
    scale_factor = lax.rsqrt(jnp.mean(residual * residual, axis=1, keepdims=True) + 1e-06)
    normed = (residual * scale_factor * norm_gain).astype(jnp.bfloat16)
    slice_width = up_weight.shape[0]
    own_features = lax.dynamic_slice_in_dim(
        normed, lax.axis_index("tp") * slice_width, slice_width, 1
    )
    partial_sum = jnp.dot(
        lax.all_gather(own_features, "seq", axis=0, tiled=True),
        up_weight,
        preferred_element_type=jnp.float32,
    )
    hidden = jax.nn.gelu(lax.psum(partial_sum, "tp")).astype(jnp.bfloat16)
    return lax.psum_scatter(
        jnp.dot(hidden, down_weight, preferred_element_type=jnp.float32),
        "seq",
        scatter_dimension=0,
        tiled=True,
    ).astype(jnp.bfloat16)


def general_body(vq, vk, vv, cq, ak, av, aq, ck, cv, ai, gain, up, down):
    cross_heads = cq.shape[1] // CHEAD
    mixed = video_self(vq, vk, vv)
    gathered_query = lax.all_gather(aq, "seq", axis=0, tiled=True)
    gathered_key = lax.all_gather(ak, "seq", axis=0, tiled=True)
    gathered_value = lax.all_gather(av, "seq", axis=0, tiled=True)
    heard = attend(cq, gathered_key, gathered_value, cross_heads)
    seen = audio_listen(gathered_query, ck, cv, cross_heads)
    mlp = audio_block(ai, seen, gain, up, down)
    return mixed, heard, seen, mlp


def whole():
    return pl.BlockSpec()


def after(value, *others):
    return lax.optimization_barrier((value, *others))[0]


def sds(shape, dtype=BF16):
    return jax.ShapeDtypeStruct(shape, dtype)


def call(kernel, ins, outs, flops=0, moved=0, limit=32):
    return pl.pallas_call(
        kernel,
        out_shape=tuple(outs),
        in_specs=[whole()] * len(ins),
        out_specs=tuple(whole() for _ in outs),
        compiler_params=pltpu.CompilerParams(vmem_limit_bytes=limit * MIB),
        cost_estimate=pl.CostEstimate(flops=flops, bytes_accessed=moved, transcendentals=0),
    )(*ins)


def shift(value, by):
    n = lax.axis_size("seq")
    return lax.ppermute(value, "seq", [(i, (i + by) % n) for i in range(n)])


def parts3(value):
    first = value.astype(BF16).astype(F32)
    second = (value - first).astype(BF16).astype(F32)
    return first, second, value - first - second


def pack_kernel(n, first, widths, audio_count, kept, q, k, v, *refs):
    audio, refs = refs[:audio_count], refs[audio_count:]
    keep, outs, sem = refs[:kept], refs[kept:-1], refs[-1]
    me = lax.axis_index("seq")
    tokens = q.shape[0]
    group = q.shape[1] // n
    copies = []
    for c, width in enumerate(widths):
        for s in range(n):
            dest = lax.rem(me + s, n)
            at = pl.ds(pl.multiple_of(dest * group + first, LANES), width)
            for i, ref in enumerate((q, k, v)):
                to = outs[c * n + s].at[pl.ds(i * tokens, tokens), :]
                copies.append(pltpu.make_async_copy(ref.at[:, at], to, sem.at[len(copies)]))
                copies[-1].start()
        first += width
    for ref, to in zip(keep, outs[n * len(widths) :]):
        copies.append(pltpu.make_async_copy(ref, to, sem.at[len(copies)]))
        copies[-1].start()
    if audio:
        half = audio[0].shape[1]
        mine = pl.ds(pl.multiple_of(lax.axis_index("tp") * half, LANES), half)
        parts = [ref[...].astype(F32) for ref in audio[:3]] + [audio[3][:, mine].astype(F32)]
        blocks = [part[:, c : c + LANES] for part in parts for c in range(0, half, LANES)]
        extra = jnp.concatenate(blocks, axis=0).astype(BF16)
        for s in range(n):
            outs[s][3 * tokens :, :] = extra
    for copy in copies:
        copy.wait()


def pack(video, audio, keep, n, first, widths, limit, moved):
    tokens = video[0].shape[0]
    extra = 4 * audio[0].size // LANES if audio else 0
    shapes = [sds((3 * tokens + extra, w)) for w in widths for _ in range(n)]
    stay = pl.BlockSpec(memory_space=pl.ANY)
    return pl.pallas_call(
        functools.partial(pack_kernel, n, first, widths, len(audio), len(keep)),
        out_shape=tuple(shapes) + tuple(sds(x.shape) for x in keep),
        in_specs=[stay] * 3 + [whole()] * len(audio) + [stay] * len(keep),
        out_specs=(whole(),) * (len(shapes) + len(keep)),
        scratch_shapes=[pltpu.SemaphoreType.DMA((3 * len(shapes) + len(keep),))],
        compiler_params=pltpu.CompilerParams(vmem_limit_bytes=limit * MIB),
        cost_estimate=pl.CostEstimate(flops=0, bytes_accessed=moved, transcendentals=0),
    )(*video, *audio, *keep)


def audio_rows(tails, part, pair, rows, pairs):
    at = (part * pairs + pair) * rows
    return jnp.concatenate([t[at : at + rows] for t in tails], axis=0)


def attend_kernel(n, tokens, *refs):
    inputs, outs = refs[:-n], refs[-n:]
    scale = LOG2E / math.sqrt(VHEAD)
    first = 0
    for c in range(0, len(inputs), n):
        pieces = inputs[c : c + n]
        for h in range(pieces[0].shape[1] // VHEAD):
            cols = slice(h * VHEAD, (h + 1) * VHEAD)
            keys = jnp.concatenate([p[tokens : 2 * tokens, cols] for p in pieces], axis=0)
            values = jnp.concatenate([p[2 * tokens : 3 * tokens, cols] for p in pieces], axis=0)
            for p, out in zip(pieces, outs):
                s = lax.dot_general(p[0:tokens, cols], keys, NT, preferred_element_type=F32)
                s = s * scale
                w = jnp.exp2(s - jnp.max(s, axis=1, keepdims=True))
                total = jnp.sum(w, axis=1, keepdims=True)
                o = jnp.dot(w.astype(BF16), values, preferred_element_type=F32)
                out[:, first + h * VHEAD : first + (h + 1) * VHEAD] = (o / total).astype(BF16)
        first += pieces[0].shape[1]


def unpack_kernel(n, widths, *refs):
    pieces, out, sem = refs[: n * len(widths)], refs[-2], refs[-1]
    me = lax.axis_index("seq")
    group = sum(widths)
    first = 0
    copies = []
    for c, width in enumerate(widths):
        for s in range(n):
            dest = lax.rem(me + s, n)
            at = pl.ds(pl.multiple_of(dest * group + first, LANES), width)
            copies.append(pltpu.make_async_copy(pieces[c * n + s], out.at[:, at], sem.at[len(copies)]))
            copies[-1].start()
        first += width
    for copy in copies:
        copy.wait()


def unpack(pieces, n, widths):
    tokens = pieces[0].shape[0]
    return pl.pallas_call(
        functools.partial(unpack_kernel, n, widths),
        out_shape=sds((tokens, n * sum(widths))),
        in_specs=[pl.BlockSpec(memory_space=pltpu.VMEM)] * len(pieces),
        out_specs=pl.BlockSpec(memory_space=pl.ANY),
        scratch_shapes=[pltpu.SemaphoreType.DMA((len(pieces),))],
        compiler_params=pltpu.CompilerParams(vmem_limit_bytes=16 * MIB),
    )(*pieces)


def low_half(shape):
    return lax.broadcasted_iota(jnp.int32, shape, 1) < CHEAD


def listen_kernel(n, tokens, rows, *refs):
    pieces, keys, values, out = refs[:n], refs[n], refs[n + 1], refs[n + 2]
    columns = keys.shape[1]
    pairs = columns // LANES
    tails = [p[3 * tokens : 3 * tokens + rows * pairs, :].astype(F32) for p in pieces]
    count = n * rows
    scale = LOG2E / math.sqrt(CHEAD)
    low = low_half((count, LANES))
    lane = lax.broadcasted_iota(jnp.int32, (count, LANES), 1)
    stats = jnp.zeros((count, LANES), F32)
    heads = columns // CHEAD
    for pair in range(pairs):
        cols = slice(pair * LANES, (pair + 1) * LANES)
        qp = audio_rows(tails, 0, pair, rows, pairs)
        both = jnp.concatenate([jnp.where(low, qp, 0.0), jnp.where(low, 0.0, qp)], axis=0)
        s = lax.dot_general(both.astype(BF16), keys[:, cols], NT, preferred_element_type=F32)
        s = s * scale
        peak = jnp.max(s, axis=1, keepdims=True)
        w = jnp.exp2(s - peak)
        total = jnp.sum(w, axis=1, keepdims=True)
        o = jnp.dot(w.astype(BF16), values[:, cols], preferred_element_type=F32) / total
        out[:, cols] = jnp.where(low, o[:count], o[count:]).astype(BF16)
        for i in range(2):
            head = 2 * pair + i
            sel = slice(i * count, (i + 1) * count)
            for j, part in enumerate(parts3(peak[sel]) + parts3(total[sel])):
                stats = jnp.where(lane == j * heads + head, part, stats)
    out[:, columns:] = stats.astype(BF16)


def combine_kernel(n, tokens, rows, *refs):
    got, pieces = refs[:n], refs[n : 2 * n]
    gain, up = refs[2 * n], refs[2 * n + 1]
    own_sum, sent_sum, seen, x_ref = refs[2 * n + 2 :]

    @pl.when(pl.program_id(0) == 0)
    def _():
        columns = seen.shape[1]
        heads = columns // CHEAD
        peaks, totals, parts = [], [], []
        for s in range(n):
            whole = got[s][...].astype(F32)
            if s:
                whole = jnp.concatenate([whole[-s * rows :], whole[: -s * rows]], axis=0)
            whole, stats = whole[:, :columns], whole[:, columns:]
            piece = [stats[:, j * heads : (j + 1) * heads] for j in range(6)]
            peaks.append(piece[0] + piece[1] + piece[2])
            totals.append(piece[3] + piece[4] + piece[5])
            parts.append(whole)
        top = functools.reduce(jnp.maximum, peaks)
        weight = [t * jnp.exp2(p - top) for t, p in zip(totals, peaks)]
        every = functools.reduce(jnp.add, weight)
        weight = [w / every for w in weight]
        tails = [p[3 * tokens :, :].astype(F32) for p in pieces]
        low = low_half((n * rows, LANES))
        square = jnp.zeros((n * rows, 1), F32)
        for pair in range(columns // LANES):
            cols = slice(pair * LANES, (pair + 1) * LANES)
            o = jnp.zeros((n * rows, LANES), F32)
            for w, part in zip(weight, parts):
                a, b = w[:, 2 * pair : 2 * pair + 1], w[:, 2 * pair + 1 : 2 * pair + 2]
                o = o + jnp.where(low, a, b) * part[:, cols]
            o = o.astype(BF16)
            seen[:, cols] = o[:rows]
            residual = audio_rows(tails, 3, pair, rows, columns // LANES) + o.astype(F32)
            square = square + jnp.sum(residual * residual, axis=1, keepdims=True)
            at = pl.ds(pl.multiple_of(lax.axis_index("tp") * columns + pair * LANES, LANES), LANES)
            x_ref[:, cols] = (residual * gain[:, at]).astype(BF16)
        lane = lax.broadcasted_iota(jnp.int32, (n * rows, LANES), 1)
        first, second, third = parts3(square)
        spread = jnp.where(lane == 0, first, jnp.where(lane == 1, second, third))
        spread = jnp.where(lane < 3, spread, 0.0)
        own_sum[0, :, :LANES] = spread
        sent_sum[0, :, :LANES] = spread.astype(BF16)

    @pl.when(pl.program_id(0) > 0)
    def _():
        product = jnp.dot(x_ref[...], up[...], preferred_element_type=F32)
        own_sum[0] = product
        sent_sum[0] = product.astype(BF16)


def combine(got, pieces, gain, up, tokens, rows, block):
    n = len(got)
    columns, units = up.shape
    steps = units // block + 1
    held = lambda ref: pl.BlockSpec(ref.shape, lambda i: (0,) * ref.ndim)
    moved = pl.BlockSpec((1, n * rows, block), lambda i: (i, 0, 0))
    return pl.pallas_call(
        functools.partial(combine_kernel, n, tokens, rows),
        grid=(steps,),
        out_shape=(
            sds((steps, n * rows, block), F32),
            sds((steps, n * rows, block)),
            sds((rows, columns)),
        ),
        in_specs=[held(r) for r in (*got, *pieces, gain)]
        + [pl.BlockSpec((columns, block), lambda i: (0, jnp.maximum(i - 1, 0)))],
        out_specs=(moved, moved, pl.BlockSpec((rows, columns), lambda i: (0, 0))),
        scratch_shapes=[pltpu.VMEM((n * rows, columns), BF16)],
        compiler_params=pltpu.CompilerParams(vmem_limit_bytes=32 * MIB),
        cost_estimate=pl.CostEstimate(
            flops=0, bytes_accessed=0 * MIB, transcendentals=0
        ),
    )(*got, *pieces, gain, up)


def finish_kernel(n, features, own, other, down, *refs):
    outs, hidden = refs[:n], refs[n]
    rows = outs[0].shape[0]

    @pl.when(pl.program_id(0) == 0)
    def _():
        square = own[0, :, :LANES] + other[0, :, :LANES].astype(F32)
        square = jnp.sum(square, axis=1, keepdims=True)
        scale = lax.rsqrt(square / features + 1e-6)
        block = own.shape[2]
        for i in range(1, own.shape[0]):
            total = (own[i] + other[i].astype(F32)) * scale
            hidden[:, (i - 1) * block : i * block] = jax.nn.gelu(total).astype(BF16)

    product = jnp.dot(hidden[...], down[...], preferred_element_type=F32)
    for s in range(n):
        outs[s][...] = product[s * rows : (s + 1) * rows].astype(outs[s].dtype)


def finish(own, other, down, n, rows, features, block):
    units, columns = down.shape
    held = lambda ref: pl.BlockSpec(ref.shape, lambda i: (0,) * ref.ndim)
    return pl.pallas_call(
        functools.partial(finish_kernel, n, features),
        grid=(columns // block,),
        out_shape=(sds((rows, columns), F32),) + (sds((rows, columns)),) * (n - 1),
        in_specs=[held(own), held(other), pl.BlockSpec((units, block), lambda i: (0, i))],
        out_specs=(pl.BlockSpec((rows, block), lambda i: (0, i)),) * n,
        scratch_shapes=[pltpu.VMEM((n * rows, units), BF16)],
        compiler_params=pltpu.CompilerParams(vmem_limit_bytes=32 * MIB),
        cost_estimate=pl.CostEstimate(
            flops=0, bytes_accessed=0 * MIB, transcendentals=0
        ),
    )(own, other, down)


def heard_kernel(n, tokens, rows, q, *refs):
    pieces, out = refs[:n], refs[n]
    pairs = q.shape[1] // LANES
    tails = [p[3 * tokens :, :].astype(F32) for p in pieces]
    count = n * rows
    low = low_half((count, LANES))
    scale = LOG2E / math.sqrt(CHEAD)

    def both(part, pair):
        x = audio_rows(tails, part, pair, rows, pairs)
        return jnp.concatenate([jnp.where(low, x, 0.0), jnp.where(low, 0.0, x)], axis=0).astype(BF16)

    for pair in range(pairs):
        cols = slice(pair * LANES, (pair + 1) * LANES)
        s = lax.dot_general(both(1, pair), q[:, cols], NT, preferred_element_type=F32) * scale
        probs = []
        for i in range(2):
            t = s[i * count : (i + 1) * count]
            w = jnp.exp2(t - jnp.max(t, axis=0, keepdims=True))
            probs.append(w / jnp.sum(w, axis=0, keepdims=True))
        w = jnp.concatenate(probs, axis=0).astype(BF16)
        out[:, cols] = lax.dot_general(w, both(2, pair), TN, preferred_element_type=F32).astype(BF16)


def add_kernel(own, *refs):
    total = own[...]
    for ref in refs[:-1]:
        total = total + ref[...].astype(F32)
    refs[-1][...] = total.astype(BF16)


def short_body(vq, vk, vv, cq, ak, av, aq, ck, cv, ai, gain, up, down):
    n = lax.axis_size("seq")
    tokens = vq.shape[0]
    rows, columns = aq.shape
    features = ai.shape[1]
    heads = vq.shape[1] // n // VHEAD
    widths = [c * VHEAD for c in (1, 1, heads - 2)]
    video = (vq, vk, vv)

    def send(own, *first):
        return [own[0]] + [shift(after(own[s], *first), s) for s in range(1, n)]

    def give_back(own):
        return [own[0]] + [shift(own[s], -s) for s in range(1, n)]

    def attended(chunks, moved):
        width = sum(c[0].shape[1] for c in chunks)
        return call(
            functools.partial(attend_kernel, n, tokens),
            [p for c in chunks for p in c],
            [sds((tokens, width))] * n,
            moved=moved,
            limit=16,
        )

    wait = 16 * MIB
    packed = pack(video, (aq, ak, av, ai), (), n, 0, widths[:1], 60, 6 * vq.size)
    chunk_0 = send(packed)
    packed = pack(video, (), (packed[0], ck, cv), n, widths[0], widths[1:], 16, wait)
    *packed, chunk_0[0], ck, cv = packed
    chunk_1 = send(packed[:n])
    (share,) = call(
        functools.partial(listen_kernel, n, tokens, rows),
        (*chunk_0, ck, cv),
        [sds((n * rows, columns + LANES))],
        moved=4 * vq.size,
        limit=16,
    )
    shares = send([share] * n)
    chunk_2 = send(packed[n:], *chunk_1[1:])
    first = attended([chunk_0, chunk_1], 1 * MIB)
    (heard,) = call(
        functools.partial(heard_kernel, n, tokens, rows),
        (cq, *chunk_0),
        [sds(cq.shape)],
        moved=1 * MIB,
        limit=16,
    )
    gain = after(gain.reshape(1, -1), first[0], heard)
    own_sum, sent_sum, seen = combine(shares, chunk_0, gain, up, tokens, rows, 512)
    other_sum = lax.ppermute(sent_sum, "tp", [(0, 1), (1, 0)])
    mixed_a = give_back(first)
    results = finish(own_sum, other_sum, down, n, rows, features, 512)
    (mlp,) = call(add_kernel, give_back(results), [sds((rows, columns))])
    mixed_b = give_back(attended([chunk_2], 0 * MIB))
    mixed = unpack((after(mixed_a[0], mlp), *mixed_a[1:], *mixed_b), n, (widths[0] + widths[1], widths[2]))
    return mixed, heard, seen, mlp


def fits(vq, cq, aq, up, down):
    n = lax.axis_size("seq")
    heads = vq.shape[1] // VHEAD
    return (
        1 < n <= 8
        and lax.axis_size("tp") == 2
        and heads % n == 0
        and heads // n > 2
        and vq.shape[0] == LANES
        and n * vq.shape[0] <= 1024
        and aq.shape[0] % 8 == 0
        and n * aq.shape[0] <= 64
        and 6 * (aq.shape[1] // CHEAD) <= LANES
        and aq.shape[1] % VHEAD == 0
        and up.shape[1] % 512 == 0
        and down.shape[1] % 512 == 0
    )


def body(*args):
    *arrays, gain, up, down = args
    arrays = [a[0] for a in arrays]
    path = short_body if fits(arrays[0], arrays[3], arrays[6], up, down) else general_body
    return tuple(out[None] for out in path(*arrays, gain, up, down))


def solution(mesh):
    rows = P(("clips", "dp"), "seq", "tp")
    placed = (rows,) * 9 + (P(("clips", "dp"), "seq", None), P(), P("tp", "seq"), P("seq", "tp"))
    return jax.shard_map(
        body, mesh=mesh, in_specs=placed, out_specs=(rows,) * 4, check_vma=False
    )
```

```python
import functools
import math

import jax
import jax.numpy as jnp
from jax import lax
from jax.experimental import pallas as pl
from jax.experimental.pallas import tpu as pltpu
from jax.sharding import PartitionSpec as P

VHEAD = 128
CHEAD = 64
LANES = 128
F32 = jnp.float32
BF16 = jnp.bfloat16
LOG2E = math.log2(math.e)
MIB = 1024 * 1024
NT = (((1,), (1,)), ((), ()))
TN = (((0,), (0,)), ((), ()))


def attend_rows(queries, keys_in, values_in, head_count):
    head_size = queries.shape[1] // head_count
    query_heads = queries.reshape(queries.shape[0], head_count, head_size)
    key_heads = keys_in.reshape(keys_in.shape[0], head_count, head_size)
    value_heads = values_in.reshape(values_in.shape[0], head_count, head_size)
    scores = jnp.einsum(
        "qhd,khd->qhk", query_heads, key_heads, preferred_element_type=jnp.float32
    ) / math.sqrt(head_size)
    peak_value = jnp.max(scores, axis=2, keepdims=True)
    weights = jnp.exp(scores - peak_value)
    totals = jnp.sum(weights, axis=2)
    weighted = jnp.einsum(
        "qhk,khd->qhd",
        weights.astype(jnp.bfloat16),
        value_heads,
        preferred_element_type=jnp.float32,
    )
    result = weighted / totals[:, :, None]
    return result.reshape(queries.shape[0], head_count * head_size).astype(jnp.bfloat16)


def attend(queries, keys_in, values_in, head_count):
    row_total = queries.shape[0]
    block_rows = 512 if row_total % 512 == 0 else row_total
    pieces = queries.reshape(row_total // block_rows, block_rows, queries.shape[1])
    result = lax.map(
        lambda row_piece: attend_rows(row_piece, keys_in, values_in, head_count), pieces
    )
    return result.reshape(row_total, queries.shape[1])


def video_self(queries, keys_in, values_in):
    seq_count = lax.axis_size("seq")
    local_heads = queries.shape[1] // VHEAD
    dest_heads = max(local_heads // seq_count, 1)
    blocks = seq_count * dest_heads // local_heads
    groups = local_heads // dest_heads
    group_width = dest_heads * VHEAD
    token_count = queries.shape[0]
    block_tokens = token_count // blocks

    def spread(tensor):
        shaped = tensor.reshape(token_count, groups, group_width).transpose(1, 0, 2)
        shaped = jnp.broadcast_to(shaped[:, None], (groups, blocks, token_count, group_width))
        return shaped.reshape(seq_count, token_count, group_width)

    shaped = queries.reshape(blocks, block_tokens, groups, group_width).transpose(2, 0, 1, 3)
    own_queries = lax.all_to_all(
        shaped.reshape(seq_count, block_tokens, group_width),
        "seq",
        split_axis=0,
        concat_axis=0,
        tiled=True,
    )
    keys_all = lax.all_to_all(spread(keys_in), "seq", split_axis=0, concat_axis=0, tiled=True)
    values_all = lax.all_to_all(spread(values_in), "seq", split_axis=0, concat_axis=0, tiled=True)
    keys_all = keys_all.reshape(-1, group_width)
    values_all = values_all.reshape(-1, group_width)
    own_queries = own_queries.reshape(-1, group_width)
    attended = attend(own_queries, keys_all, values_all, dest_heads)
    returned = lax.all_to_all(
        attended.reshape(seq_count, block_tokens, group_width),
        "seq",
        split_axis=0,
        concat_axis=0,
        tiled=True,
    )
    returned = returned.reshape(groups, blocks, block_tokens, group_width).transpose(1, 2, 0, 3)
    return returned.reshape(token_count, groups * group_width)


def audio_listen(queries, keys_in, values_in, head_count):
    head_size = queries.shape[1] // head_count
    query_heads = queries.reshape(queries.shape[0], head_count, head_size)
    key_heads = keys_in.reshape(keys_in.shape[0], head_count, head_size)
    value_heads = values_in.reshape(values_in.shape[0], head_count, head_size)
    scores = jnp.einsum(
        "qhd,khd->qhk", query_heads, key_heads, preferred_element_type=jnp.float32
    ) / math.sqrt(head_size)
    local_peak = jnp.max(scores, axis=2)
    peak_value = lax.pmax(local_peak, "seq")
    weights = jnp.exp(scores - peak_value[:, :, None])
    totals = jnp.sum(weights, axis=2)
    weighted = jnp.einsum(
        "qhk,khd->qhd",
        weights.astype(jnp.bfloat16),
        value_heads,
        preferred_element_type=jnp.float32,
    )
    weighted = weighted.reshape(queries.shape[0], head_count * head_size)
    totals = lax.psum_scatter(totals, "seq", scatter_dimension=0, tiled=True)
    weighted = lax.psum_scatter(weighted, "seq", scatter_dimension=0, tiled=True)
    return (weighted / jnp.repeat(totals, head_size, axis=1)).astype(jnp.bfloat16)


def audio_block(audio_rows, audio_seen, norm_gain, up_weight, down_weight):
    features = lax.all_gather(audio_seen, "tp", axis=1, tiled=True)
    residual = audio_rows.astype(jnp.float32) + features.astype(jnp.float32)
    scale_factor = lax.rsqrt(jnp.mean(residual * residual, axis=1, keepdims=True) + 1e-06)
    normed = (residual * scale_factor * norm_gain).astype(jnp.bfloat16)
    slice_width = up_weight.shape[0]
    own_features = lax.dynamic_slice_in_dim(
        normed, lax.axis_index("tp") * slice_width, slice_width, 1
    )
    partial_sum = jnp.dot(
        lax.all_gather(own_features, "seq", axis=0, tiled=True),
        up_weight,
        preferred_element_type=jnp.float32,
    )
    hidden = jax.nn.gelu(lax.psum(partial_sum, "tp")).astype(jnp.bfloat16)
    return lax.psum_scatter(
        jnp.dot(hidden, down_weight, preferred_element_type=jnp.float32),
        "seq",
        scatter_dimension=0,
        tiled=True,
    ).astype(jnp.bfloat16)


def general_body(vq, vk, vv, cq, ak, av, aq, ck, cv, ai, gain, up, down):
    cross_heads = cq.shape[1] // CHEAD
    mixed = video_self(vq, vk, vv)
    gathered_query = lax.all_gather(aq, "seq", axis=0, tiled=True)
    gathered_key = lax.all_gather(ak, "seq", axis=0, tiled=True)
    gathered_value = lax.all_gather(av, "seq", axis=0, tiled=True)
    heard = attend(cq, gathered_key, gathered_value, cross_heads)
    seen = audio_listen(gathered_query, ck, cv, cross_heads)
    mlp = audio_block(ai, seen, gain, up, down)
    return mixed, heard, seen, mlp


def whole():
    return pl.BlockSpec()


def after(value, *others):
    return lax.optimization_barrier((value, *others))[0]


def sds(shape, dtype=BF16):
    return jax.ShapeDtypeStruct(shape, dtype)


def call(kernel, ins, outs, flops=0, moved=0, limit=32):
    return pl.pallas_call(
        kernel,
        out_shape=tuple(outs),
        in_specs=[whole()] * len(ins),
        out_specs=tuple(whole() for _ in outs),
        compiler_params=pltpu.CompilerParams(vmem_limit_bytes=limit * MIB),
        cost_estimate=pl.CostEstimate(flops=flops, bytes_accessed=moved, transcendentals=0),
    )(*ins)


def trade(value, by):
    n = lax.axis_size("seq")
    return lax.ppermute(value, "seq", [(i, i ^ by) for i in range(n)])


def parts3(value):
    first = value.astype(BF16).astype(F32)
    second = (value - first).astype(BF16).astype(F32)
    return first, second, value - first - second


def pack_kernel(n, first, widths, audio_count, kept, q, k, v, *refs):
    audio, refs = refs[:audio_count], refs[audio_count:]
    keep, outs, sem = refs[:kept], refs[kept:-1], refs[-1]
    me = lax.axis_index("seq")
    tokens = q.shape[0]
    group = q.shape[1] // n
    copies = []
    for c, width in enumerate(widths):
        for s in range(n):
            dest = lax.bitwise_xor(me, s)
            at = pl.ds(pl.multiple_of(dest * group + first, LANES), width)
            for i, ref in enumerate((q, k, v)):
                to = outs[c * n + s].at[pl.ds(i * tokens, tokens), :]
                copies.append(pltpu.make_async_copy(ref.at[:, at], to, sem.at[len(copies)]))
                copies[-1].start()
        first += width
    for ref, to in zip(keep, outs[n * len(widths) :]):
        copies.append(pltpu.make_async_copy(ref, to, sem.at[len(copies)]))
        copies[-1].start()
    if audio:
        half = audio[0].shape[1]
        mine = pl.ds(pl.multiple_of(lax.axis_index("tp") * half, LANES), half)
        parts = [ref[...].astype(F32) for ref in audio[:3]] + [audio[3][:, mine].astype(F32)]
        blocks = [part[:, c : c + widths[0]] for part in parts for c in range(0, half, widths[0])]
        extra = jnp.concatenate(blocks, axis=0).astype(BF16)
        for s in range(n):
            outs[s][3 * tokens :, :] = extra
    for copy in copies:
        copy.wait()


def pack(video, audio, keep, n, first, widths, limit, moved):
    tokens = video[0].shape[0]
    extra = 4 * audio[0].size // widths[0] if audio else 0
    shapes = [sds((3 * tokens + extra, w)) for w in widths for _ in range(n)]
    stay = pl.BlockSpec(memory_space=pl.ANY)
    return pl.pallas_call(
        functools.partial(pack_kernel, n, first, widths, len(audio), len(keep)),
        out_shape=tuple(shapes) + tuple(sds(x.shape) for x in keep),
        in_specs=[stay] * 3 + [whole()] * len(audio) + [stay] * len(keep),
        out_specs=(whole(),) * (len(shapes) + len(keep)),
        scratch_shapes=[pltpu.SemaphoreType.DMA((3 * len(shapes) + len(keep),))],
        compiler_params=pltpu.CompilerParams(vmem_limit_bytes=limit * MIB),
        cost_estimate=pl.CostEstimate(flops=0, bytes_accessed=moved, transcendentals=0),
    )(*video, *audio, *keep)


def audio_rows(tails, part, pair, rows, pairs):
    per = tails[0].shape[1] // LANES
    at, side = (part * pairs + pair) // per * rows, pair % per * LANES
    return jnp.concatenate([t[at : at + rows, side : side + LANES] for t in tails], axis=0)


def attend_heads(pieces, tokens, put):
    scale = LOG2E / math.sqrt(VHEAD)
    for h in range(pieces[0].shape[1] // VHEAD):
        cols = slice(h * VHEAD, (h + 1) * VHEAD)
        keys = jnp.concatenate([p[tokens : 2 * tokens, cols] for p in pieces], axis=0)
        values = jnp.concatenate([p[2 * tokens : 3 * tokens, cols] for p in pieces], axis=0)
        for s, p in enumerate(pieces):
            t = lax.dot_general(p[0:tokens, cols], keys, NT, preferred_element_type=F32) * scale
            w = jnp.exp2(t - jnp.max(t, axis=1, keepdims=True))
            total = jnp.sum(w, axis=1, keepdims=True)
            o = jnp.dot(w.astype(BF16), values, preferred_element_type=F32)
            put(s, h, (o / total).astype(BF16))


def middle_kernel(n, counts, *refs):
    inputs, last, outs, sem = refs[: -2 * n - 1], refs[-2 * n - 1 : -n - 1], refs[-n - 1 : -1], refs[-1]
    tokens = last[0].shape[0] // 3
    top = pl.ds(0, 3 * tokens)
    copies = [
        pltpu.make_async_copy(last[s], outs[s].at[top, :], sem.at[s]) for s in range(n)
    ]
    for copy in copies:
        copy.start()
    head = 0
    for c, count in enumerate(counts):
        first = head * VHEAD

        def put(s, h, rows, first=first):
            at = first + h * VHEAD
            low, side = (at // outs[0].shape[1]) * tokens + 3 * tokens, at % outs[0].shape[1]
            outs[s][low : low + tokens, side : side + VHEAD] = rows

        attend_heads(inputs[c * n : (c + 1) * n], tokens, put)
        head += count
    for copy in copies:
        copy.wait()


def middle(chunks, last, n, moved):
    counts = [c[0].shape[1] // VHEAD for c in chunks]
    tokens = last[0].shape[0] // 3
    width = last[0].shape[1]
    tall = 3 * tokens + -(-sum(counts) * VHEAD // width) * tokens
    pieces = [p for c in chunks for p in c]
    return pl.pallas_call(
        functools.partial(middle_kernel, n, counts),
        out_shape=(sds((tall, width)),) * n,
        in_specs=[whole()] * len(pieces) + [pl.BlockSpec(memory_space=pl.ANY)] * n,
        out_specs=(whole(),) * n,
        scratch_shapes=[pltpu.SemaphoreType.DMA((n,))],
        compiler_params=pltpu.CompilerParams(vmem_limit_bytes=16 * MIB),
        cost_estimate=pl.CostEstimate(flops=0, bytes_accessed=moved, transcendentals=0),
    )(*pieces, *last)


def last_kernel(n, tokens, *refs):
    pieces, sums, outs = refs[:n], refs[n : 2 * n], refs[2 * n :]
    width = outs[0].shape[1]

    def put(s, h, rows):
        outs[s][:tokens, h * VHEAD : (h + 1) * VHEAD] = rows

    for s in range(n):
        part = sums[s][...].astype(F32)
        blocks = [part[:, c : c + width] for c in range(0, part.shape[1], width)]
        outs[s][tokens:, :] = jnp.concatenate(blocks, axis=0).astype(BF16)
    attend_heads(pieces, tokens, put)


def unpack_kernel(n, heads, tokens, *refs):
    middles, lasts, own = refs[:n], refs[n : 2 * n], refs[2 * n]
    out, mlp, sem = refs[2 * n + 1 :]
    me = lax.axis_index("seq")
    width = lasts[0].shape[1]
    group = heads * VHEAD
    copies = []

    def start(source, owner, first, size):
        at = pl.ds(pl.multiple_of(owner * group + first, LANES), size)
        copies.append(pltpu.make_async_copy(source, out.at[:, at], sem.at[len(copies)]))
        copies[-1].start()

    early = group - width
    for s in range(n):
        for c in range(0, early, width):
            rows = pl.ds(3 * tokens + c // width * tokens, tokens)
            size = min(width, early - c)
            start(middles[s].at[rows, pl.ds(0, size)], lax.bitwise_xor(me, s), c, size)
        start(lasts[s].at[pl.ds(0, tokens), :], lax.bitwise_xor(me, s), early, width)
    rows, columns = own.shape
    tails = [lasts[s][tokens:, :].astype(F32) for s in range(1, n)]
    for c in range(columns // width):
        total = own[:, c * width : (c + 1) * width]
        for tail in tails:
            total = total + tail[c * rows : (c + 1) * rows]
        mlp[:, c * width : (c + 1) * width] = total.astype(BF16)
    for copy in copies:
        copy.wait()


def unpack(middles, lasts, own, n, heads, tokens):
    count = n * (-(-(heads * VHEAD - lasts[0].shape[1]) // lasts[0].shape[1]) + 1)
    return pl.pallas_call(
        functools.partial(unpack_kernel, n, heads, tokens),
        out_shape=(sds((tokens, n * heads * VHEAD)), sds(own.shape)),
        in_specs=[pl.BlockSpec(memory_space=pltpu.VMEM)] * (2 * n + 1),
        out_specs=(pl.BlockSpec(memory_space=pl.ANY), whole()),
        scratch_shapes=[pltpu.SemaphoreType.DMA((count,))],
        compiler_params=pltpu.CompilerParams(vmem_limit_bytes=16 * MIB),
    )(*middles, *lasts, own)


def low_half(shape):
    return lax.broadcasted_iota(jnp.int32, shape, 1) < CHEAD


def listen_kernel(n, tokens, rows, *refs):
    pieces, keys, values, out = refs[:n], refs[n], refs[n + 1], refs[n + 2]
    columns = keys.shape[1]
    pairs = columns // LANES
    tails = [p[3 * tokens :, :].astype(F32) for p in pieces]
    count = n * rows
    scale = LOG2E / math.sqrt(CHEAD)
    low = low_half((count, LANES))
    lane = lax.broadcasted_iota(jnp.int32, (count, LANES), 1)
    stats = jnp.zeros((count, LANES), F32)
    heads = columns // CHEAD
    for pair in range(pairs):
        cols = slice(pair * LANES, (pair + 1) * LANES)
        qp = audio_rows(tails, 0, pair, rows, pairs)
        both = jnp.concatenate([jnp.where(low, qp, 0.0), jnp.where(low, 0.0, qp)], axis=0)
        s = lax.dot_general(both.astype(BF16), keys[:, cols], NT, preferred_element_type=F32)
        s = s * scale
        peak = jnp.max(s, axis=1, keepdims=True)
        w = jnp.exp2(s - peak)
        total = jnp.sum(w, axis=1, keepdims=True)
        o = jnp.dot(w.astype(BF16), values[:, cols], preferred_element_type=F32) / total
        out[:, cols] = jnp.where(low, o[:count], o[count:]).astype(BF16)
        for i in range(2):
            head = 2 * pair + i
            sel = slice(i * count, (i + 1) * count)
            for j, part in enumerate(parts3(peak[sel]) + parts3(total[sel])):
                stats = jnp.where(lane == j * heads + head, part, stats)
    out[:, columns:] = stats.astype(BF16)


def combine_kernel(n, tokens, rows, *refs):
    got, pieces = refs[:n], refs[n : 2 * n]
    gain, up = refs[2 * n], refs[2 * n + 1]
    own_sum, sent_sum, seen, x_ref = refs[2 * n + 2 :]

    @pl.when(pl.program_id(0) == 0)
    def _():
        columns = seen.shape[1]
        heads = columns // CHEAD
        peaks, totals, parts = [], [], []
        for s in range(n):
            whole = got[s][...].astype(F32)
            if s:
                whole = jnp.concatenate([whole[(i ^ s) * rows :][:rows] for i in range(n)], axis=0)
            whole, stats = whole[:, :columns], whole[:, columns:]
            piece = [stats[:, j * heads : (j + 1) * heads] for j in range(6)]
            peaks.append(piece[0] + piece[1] + piece[2])
            totals.append(piece[3] + piece[4] + piece[5])
            parts.append(whole)
        top = functools.reduce(jnp.maximum, peaks)
        weight = [t * jnp.exp2(p - top) for t, p in zip(totals, peaks)]
        every = functools.reduce(jnp.add, weight)
        weight = [w / every for w in weight]
        tails = [p[3 * tokens :, :].astype(F32) for p in pieces]
        low = low_half((n * rows, LANES))
        square = jnp.zeros((n * rows, 1), F32)
        for pair in range(columns // LANES):
            cols = slice(pair * LANES, (pair + 1) * LANES)
            o = jnp.zeros((n * rows, LANES), F32)
            for w, part in zip(weight, parts):
                a, b = w[:, 2 * pair : 2 * pair + 1], w[:, 2 * pair + 1 : 2 * pair + 2]
                o = o + jnp.where(low, a, b) * part[:, cols]
            o = o.astype(BF16)
            seen[:, cols] = o[:rows]
            residual = audio_rows(tails, 3, pair, rows, columns // LANES) + o.astype(F32)
            square = square + jnp.sum(residual * residual, axis=1, keepdims=True)
            at = pl.ds(pl.multiple_of(lax.axis_index("tp") * columns + pair * LANES, LANES), LANES)
            x_ref[:, cols] = (residual * gain[:, at]).astype(BF16)
        lane = lax.broadcasted_iota(jnp.int32, (n * rows, LANES), 1)
        first, second, third = parts3(square)
        spread = jnp.where(lane == 0, first, jnp.where(lane == 1, second, third))
        spread = jnp.where(lane < 3, spread, 0.0)
        own_sum[0, :, :LANES] = spread
        sent_sum[0, :, :LANES] = spread.astype(BF16)

    @pl.when(pl.program_id(0) > 0)
    def _():
        product = jnp.dot(x_ref[...], up[...], preferred_element_type=F32)
        own_sum[0] = product
        sent_sum[0] = product.astype(BF16)


def combine(got, pieces, gain, up, tokens, rows, block):
    n = len(got)
    columns, units = up.shape
    steps = units // block + 1
    held = lambda ref: pl.BlockSpec(ref.shape, lambda i: (0,) * ref.ndim)
    moved = pl.BlockSpec((1, n * rows, block), lambda i: (i, 0, 0))
    return pl.pallas_call(
        functools.partial(combine_kernel, n, tokens, rows),
        grid=(steps,),
        out_shape=(
            sds((steps, n * rows, block), F32),
            sds((steps, n * rows, block)),
            sds((rows, columns)),
        ),
        in_specs=[held(r) for r in (*got, *pieces, gain)]
        + [pl.BlockSpec((columns, block), lambda i: (0, jnp.maximum(i - 1, 0)))],
        out_specs=(moved, moved, pl.BlockSpec((rows, columns), lambda i: (0, 0))),
        scratch_shapes=[pltpu.VMEM((n * rows, columns), BF16)],
        compiler_params=pltpu.CompilerParams(vmem_limit_bytes=32 * MIB),
        cost_estimate=pl.CostEstimate(
            flops=0, bytes_accessed=0 * MIB, transcendentals=0
        ),
    )(*got, *pieces, gain, up)


def finish_kernel(n, features, own, other, down, *refs):
    outs, hidden = refs[:n], refs[n]
    rows = outs[0].shape[0]

    @pl.when(pl.program_id(0) == 0)
    def _():
        square = own[0, :, :LANES] + other[0, :, :LANES].astype(F32)
        square = jnp.sum(square, axis=1, keepdims=True)
        scale = lax.rsqrt(square / features + 1e-6)
        block = own.shape[2]
        for i in range(1, own.shape[0]):
            total = (own[i] + other[i].astype(F32)) * scale
            hidden[:, (i - 1) * block : i * block] = jax.nn.gelu(total).astype(BF16)

    product = jnp.dot(hidden[...], down[...], preferred_element_type=F32)
    for s in range(n):
        outs[s][...] = product[s * rows : (s + 1) * rows].astype(outs[s].dtype)


def finish(own, other, down, n, rows, features, block):
    units, columns = down.shape
    held = lambda ref: pl.BlockSpec(ref.shape, lambda i: (0,) * ref.ndim)
    return pl.pallas_call(
        functools.partial(finish_kernel, n, features),
        grid=(columns // block,),
        out_shape=(sds((rows, columns), F32),) + (sds((rows, columns)),) * (n - 1),
        in_specs=[held(own), held(other), pl.BlockSpec((units, block), lambda i: (0, i))],
        out_specs=(pl.BlockSpec((rows, block), lambda i: (0, i)),) * n,
        scratch_shapes=[pltpu.VMEM((n * rows, units), BF16)],
        compiler_params=pltpu.CompilerParams(vmem_limit_bytes=32 * MIB),
        cost_estimate=pl.CostEstimate(
            flops=0, bytes_accessed=0 * MIB, transcendentals=0
        ),
    )(own, other, down)


def heard_kernel(n, tokens, rows, q, *refs):
    pieces, out = refs[:n], refs[n]
    pairs = q.shape[1] // LANES
    tails = [p[3 * tokens :, :].astype(F32) for p in pieces]
    count = n * rows
    low = low_half((count, LANES))
    scale = LOG2E / math.sqrt(CHEAD)

    def both(part, pair):
        x = audio_rows(tails, part, pair, rows, pairs)
        return jnp.concatenate([jnp.where(low, x, 0.0), jnp.where(low, 0.0, x)], axis=0).astype(BF16)

    for pair in range(pairs):
        cols = slice(pair * LANES, (pair + 1) * LANES)
        s = lax.dot_general(both(1, pair), q[:, cols], NT, preferred_element_type=F32) * scale
        probs = []
        for i in range(2):
            t = s[i * count : (i + 1) * count]
            w = jnp.exp2(t - jnp.max(t, axis=0, keepdims=True))
            probs.append(w / jnp.sum(w, axis=0, keepdims=True))
        w = jnp.concatenate(probs, axis=0).astype(BF16)
        out[:, cols] = lax.dot_general(w, both(2, pair), TN, preferred_element_type=F32).astype(BF16)


def short_body(vq, vk, vv, cq, ak, av, aq, ck, cv, ai, gain, up, down):
    n = lax.axis_size("seq")
    tokens = vq.shape[0]
    rows, columns = aq.shape
    features = ai.shape[1]
    heads = vq.shape[1] // n // VHEAD
    widths = [c * VHEAD for c in (1, 1, heads - 2)]
    video = (vq, vk, vv)

    def send(own, *first):
        return [own[0]] + [trade(after(own[s], *first), s) for s in range(1, n)]

    wait = 16 * MIB
    packed = pack(video, (aq, ak, av, ai), (), n, 0, widths[:1], 60, 6 * vq.size)
    chunk_0 = send(packed)
    packed = pack(video, (), (packed[0], ck, cv), n, widths[0], widths[1:], 16, wait)
    *packed, chunk_0[0], ck, cv = packed
    chunk_1 = send(packed[:n])
    (share,) = call(
        functools.partial(listen_kernel, n, tokens, rows),
        (*chunk_0, ck, cv),
        [sds((n * rows, columns + LANES))],
        moved=4 * vq.size,
        limit=16,
    )
    shares = send([share] * n)
    chunk_2 = send(middle([chunk_0, chunk_1], packed[n:], n, MIB), *shares[1:])
    (heard,) = call(
        functools.partial(heard_kernel, n, tokens, rows),
        (cq, *chunk_0),
        [sds(cq.shape)],
        moved=1 * MIB,
        limit=16,
    )
    gain = after(gain.reshape(1, -1), heard)
    own_sum, sent_sum, seen = combine(shares, chunk_0, gain, up, tokens, rows, 512)
    other_sum = lax.ppermute(sent_sum, "tp", [(0, 1), (1, 0)])
    results = finish(own_sum, other_sum, down, n, rows, features, 512)
    ends = call(
        functools.partial(last_kernel, n, tokens),
        (*chunk_2, *results),
        [sds((tokens + rows * columns // widths[2], widths[2]))] * n,
        limit=16,
    )
    ends = [ends[0]] + [trade(ends[s], s) for s in range(1, n)]
    mixed, mlp = unpack(chunk_2, ends, results[0], n, heads, tokens)
    return mixed, heard, seen, mlp


def fits(vq, cq, aq, up, down):
    n = lax.axis_size("seq")
    heads = vq.shape[1] // VHEAD
    return (
        n in (2, 4, 8)
        and lax.axis_size("tp") == 2
        and heads % n == 0
        and heads // n > 2
        and vq.shape[0] == LANES
        and n * vq.shape[0] <= 1024
        and aq.shape[0] % 8 == 0
        and n * aq.shape[0] <= 64
        and 6 * (aq.shape[1] // CHEAD) <= LANES
        and aq.shape[1] % VHEAD == 0
        and up.shape[1] % 512 == 0
        and down.shape[1] % 512 == 0
    )


def body(*args):
    *arrays, gain, up, down = args
    arrays = [a[0] for a in arrays]
    path = short_body if fits(arrays[0], arrays[3], arrays[6], up, down) else general_body
    return tuple(out[None] for out in path(*arrays, gain, up, down))


def solution(mesh):
    rows = P(("clips", "dp"), "seq", "tp")
    placed = (rows,) * 9 + (P(("clips", "dp"), "seq", None), P(), P("tp", "seq"), P("seq", "tp"))
    return jax.shard_map(
        body, mesh=mesh, in_specs=placed, out_specs=(rows,) * 4, check_vma=False
    )
```

```python
import functools
import math

import jax
import jax.numpy as jnp
from jax import lax
from jax.experimental import pallas as pl
from jax.experimental.pallas import tpu as pltpu
from jax.sharding import PartitionSpec as P

VHEAD = 128
CHEAD = 64
LANES = 128
F32 = jnp.float32
BF16 = jnp.bfloat16
LOG2E = math.log2(math.e)
MIB = 1024 * 1024
NT = (((1,), (1,)), ((), ()))
TN = (((0,), (0,)), ((), ()))


def attend_rows(queries, keys_in, values_in, head_count):
    head_size = queries.shape[1] // head_count
    query_heads = queries.reshape(queries.shape[0], head_count, head_size)
    key_heads = keys_in.reshape(keys_in.shape[0], head_count, head_size)
    value_heads = values_in.reshape(values_in.shape[0], head_count, head_size)
    scores = jnp.einsum(
        "qhd,khd->qhk", query_heads, key_heads, preferred_element_type=jnp.float32
    ) / math.sqrt(head_size)
    peak_value = jnp.max(scores, axis=2, keepdims=True)
    weights = jnp.exp(scores - peak_value)
    totals = jnp.sum(weights, axis=2)
    weighted = jnp.einsum(
        "qhk,khd->qhd",
        weights.astype(jnp.bfloat16),
        value_heads,
        preferred_element_type=jnp.float32,
    )
    result = weighted / totals[:, :, None]
    return result.reshape(queries.shape[0], head_count * head_size).astype(jnp.bfloat16)


def attend(queries, keys_in, values_in, head_count):
    row_total = queries.shape[0]
    block_rows = 512 if row_total % 512 == 0 else row_total
    pieces = queries.reshape(row_total // block_rows, block_rows, queries.shape[1])
    result = lax.map(
        lambda row_piece: attend_rows(row_piece, keys_in, values_in, head_count), pieces
    )
    return result.reshape(row_total, queries.shape[1])


def video_self(queries, keys_in, values_in):
    seq_count = lax.axis_size("seq")
    local_heads = queries.shape[1] // VHEAD
    dest_heads = max(local_heads // seq_count, 1)
    blocks = seq_count * dest_heads // local_heads
    groups = local_heads // dest_heads
    group_width = dest_heads * VHEAD
    token_count = queries.shape[0]
    block_tokens = token_count // blocks

    def spread(tensor):
        shaped = tensor.reshape(token_count, groups, group_width).transpose(1, 0, 2)
        shaped = jnp.broadcast_to(shaped[:, None], (groups, blocks, token_count, group_width))
        return shaped.reshape(seq_count, token_count, group_width)

    shaped = queries.reshape(blocks, block_tokens, groups, group_width).transpose(2, 0, 1, 3)
    own_queries = lax.all_to_all(
        shaped.reshape(seq_count, block_tokens, group_width),
        "seq",
        split_axis=0,
        concat_axis=0,
        tiled=True,
    )
    keys_all = lax.all_to_all(spread(keys_in), "seq", split_axis=0, concat_axis=0, tiled=True)
    values_all = lax.all_to_all(spread(values_in), "seq", split_axis=0, concat_axis=0, tiled=True)
    keys_all = keys_all.reshape(-1, group_width)
    values_all = values_all.reshape(-1, group_width)
    own_queries = own_queries.reshape(-1, group_width)
    attended = attend(own_queries, keys_all, values_all, dest_heads)
    returned = lax.all_to_all(
        attended.reshape(seq_count, block_tokens, group_width),
        "seq",
        split_axis=0,
        concat_axis=0,
        tiled=True,
    )
    returned = returned.reshape(groups, blocks, block_tokens, group_width).transpose(1, 2, 0, 3)
    return returned.reshape(token_count, groups * group_width)


def audio_listen(queries, keys_in, values_in, head_count):
    head_size = queries.shape[1] // head_count
    query_heads = queries.reshape(queries.shape[0], head_count, head_size)
    key_heads = keys_in.reshape(keys_in.shape[0], head_count, head_size)
    value_heads = values_in.reshape(values_in.shape[0], head_count, head_size)
    scores = jnp.einsum(
        "qhd,khd->qhk", query_heads, key_heads, preferred_element_type=jnp.float32
    ) / math.sqrt(head_size)
    local_peak = jnp.max(scores, axis=2)
    peak_value = lax.pmax(local_peak, "seq")
    weights = jnp.exp(scores - peak_value[:, :, None])
    totals = jnp.sum(weights, axis=2)
    weighted = jnp.einsum(
        "qhk,khd->qhd",
        weights.astype(jnp.bfloat16),
        value_heads,
        preferred_element_type=jnp.float32,
    )
    weighted = weighted.reshape(queries.shape[0], head_count * head_size)
    totals = lax.psum_scatter(totals, "seq", scatter_dimension=0, tiled=True)
    weighted = lax.psum_scatter(weighted, "seq", scatter_dimension=0, tiled=True)
    return (weighted / jnp.repeat(totals, head_size, axis=1)).astype(jnp.bfloat16)


def audio_block(audio_rows, audio_seen, norm_gain, up_weight, down_weight):
    features = lax.all_gather(audio_seen, "tp", axis=1, tiled=True)
    residual = audio_rows.astype(jnp.float32) + features.astype(jnp.float32)
    scale_factor = lax.rsqrt(jnp.mean(residual * residual, axis=1, keepdims=True) + 1e-06)
    normed = (residual * scale_factor * norm_gain).astype(jnp.bfloat16)
    slice_width = up_weight.shape[0]
    own_features = lax.dynamic_slice_in_dim(
        normed, lax.axis_index("tp") * slice_width, slice_width, 1
    )
    partial_sum = jnp.dot(
        lax.all_gather(own_features, "seq", axis=0, tiled=True),
        up_weight,
        preferred_element_type=jnp.float32,
    )
    hidden = jax.nn.gelu(lax.psum(partial_sum, "tp")).astype(jnp.bfloat16)
    return lax.psum_scatter(
        jnp.dot(hidden, down_weight, preferred_element_type=jnp.float32),
        "seq",
        scatter_dimension=0,
        tiled=True,
    ).astype(jnp.bfloat16)


def general_body(vq, vk, vv, cq, ak, av, aq, ck, cv, ai, gain, up, down):
    cross_heads = cq.shape[1] // CHEAD
    mixed = video_self(vq, vk, vv)
    gathered_query = lax.all_gather(aq, "seq", axis=0, tiled=True)
    gathered_key = lax.all_gather(ak, "seq", axis=0, tiled=True)
    gathered_value = lax.all_gather(av, "seq", axis=0, tiled=True)
    heard = attend(cq, gathered_key, gathered_value, cross_heads)
    seen = audio_listen(gathered_query, ck, cv, cross_heads)
    mlp = audio_block(ai, seen, gain, up, down)
    return mixed, heard, seen, mlp


def whole():
    return pl.BlockSpec()


def after(value, *others):
    return lax.optimization_barrier((value, *others))[0]


def sds(shape, dtype=BF16):
    return jax.ShapeDtypeStruct(shape, dtype)


def call(kernel, ins, outs, flops=0, moved=0, limit=32):
    return pl.pallas_call(
        kernel,
        out_shape=tuple(outs),
        in_specs=[whole()] * len(ins),
        out_specs=tuple(whole() for _ in outs),
        compiler_params=pltpu.CompilerParams(vmem_limit_bytes=limit * MIB),
        cost_estimate=pl.CostEstimate(flops=flops, bytes_accessed=moved, transcendentals=0),
    )(*ins)


def trade(value, by):
    n = lax.axis_size("seq")
    return lax.ppermute(value, "seq", [(i, i ^ by) for i in range(n)])


def parts3(value):
    first = value.astype(BF16).astype(F32)
    second = (value - first).astype(BF16).astype(F32)
    return first, second, value - first - second


def pack_kernel(n, first, widths, audio_count, kept, q, k, v, *refs):
    count = n * len(widths)
    audio, refs = refs[:audio_count], refs[audio_count:]
    keep, refs = refs[:kept], refs[kept:]
    outs, passed, refs = refs[:count], refs[count : count + kept], refs[count + kept :]
    built = refs[:count] if audio else outs
    lines, sem, audio_sem, out_sem = refs[-3 - audio_count : -3], refs[-3], refs[-2], refs[-1]
    me = lax.axis_index("seq")
    tokens = q.shape[0]
    group = q.shape[1] // n
    fetches = [pltpu.make_async_copy(ref, to, audio_sem.at[i]) for i, (ref, to) in enumerate(zip(audio, lines))]
    for copy in fetches:
        copy.start()
    copies, arrivals = [], []
    for c, width in enumerate(widths):
        for s in range(n):
            at = pl.ds(pl.multiple_of(lax.bitwise_xor(me, s) * group + first, LANES), width)
            for i, ref in enumerate((q, k, v)):
                to = built[c * n + s].at[pl.ds(i * tokens, tokens), :]
                arrivals.append(pltpu.make_async_copy(ref.at[:, at], to, sem.at[len(arrivals)]))
                arrivals[-1].start()
        first += width
    for i, (ref, to) in enumerate(zip(keep, passed)):
        copies.append(pltpu.make_async_copy(ref, to, out_sem.at[count + i]))
        copies[-1].start()
    if audio:
        for copy in fetches:
            copy.wait()
        half = lines[0].shape[1]
        mine = pl.ds(pl.multiple_of(lax.axis_index("tp") * half, LANES), half)
        parts = [ref[...].astype(F32) for ref in lines[:3]] + [lines[3][:, mine].astype(F32)]
        blocks = [part[:, c : c + widths[0]] for part in parts for c in range(0, half, widths[0])]
        extra = jnp.concatenate(blocks, axis=0).astype(BF16)
        for s in range(n):
            built[s][3 * tokens :, :] = extra
    for i in range(count):
        for copy in arrivals[3 * i : 3 * i + 3]:
            copy.wait()
        if audio:
            copies.append(pltpu.make_async_copy(built[i], outs[i], out_sem.at[i]))
            copies[-1].start()
    for copy in copies:
        copy.wait()


def pack(video, audio, keep, n, first, widths, limit, moved):
    tokens = video[0].shape[0]
    extra = 4 * audio[0].size // widths[0] if audio else 0
    shapes = [(3 * tokens + extra, w) for w in widths for _ in range(n)]
    stay = pl.BlockSpec(memory_space=pl.ANY)
    dma = pltpu.SemaphoreType.DMA
    return pl.pallas_call(
        functools.partial(pack_kernel, n, first, widths, len(audio), len(keep)),
        out_shape=tuple(sds(x) for x in shapes) + tuple(sds(x.shape) for x in keep),
        in_specs=[stay] * (3 + len(audio) + len(keep)),
        out_specs=(stay if audio else whole(),) * (len(shapes) + len(keep)),
        scratch_shapes=[pltpu.VMEM(x, BF16) for x in shapes if audio]
        + [pltpu.VMEM(x.shape, BF16) for x in audio]
        + [dma((3 * len(shapes),)), dma((max(len(audio), 1),)), dma((len(shapes) + len(keep),))],
        compiler_params=pltpu.CompilerParams(vmem_limit_bytes=limit * MIB),
        cost_estimate=pl.CostEstimate(flops=0, bytes_accessed=moved, transcendentals=0),
    )(*video, *audio, *keep)


def audio_rows(tails, part, pair, rows, pairs):
    per = tails[0].shape[1] // LANES
    at, side = (part * pairs + pair) // per * rows, pair % per * LANES
    return jnp.concatenate([t[at : at + rows, side : side + LANES] for t in tails], axis=0)


def attend_heads(pieces, tokens, put):
    scale = LOG2E / math.sqrt(VHEAD)
    for h in range(pieces[0].shape[1] // VHEAD):
        cols = slice(h * VHEAD, (h + 1) * VHEAD)
        keys = jnp.concatenate([p[tokens : 2 * tokens, cols] for p in pieces], axis=0)
        values = jnp.concatenate([p[2 * tokens : 3 * tokens, cols] for p in pieces], axis=0)
        for s, p in enumerate(pieces):
            t = lax.dot_general(p[0:tokens, cols], keys, NT, preferred_element_type=F32) * scale
            w = jnp.exp2(t - jnp.max(t, axis=1, keepdims=True))
            total = jnp.sum(w, axis=1, keepdims=True)
            o = jnp.dot(w.astype(BF16), values, preferred_element_type=F32)
            put(s, h, (o / total).astype(BF16))


def middle_kernel(n, counts, *refs):
    inputs, last, outs, sem = refs[: -2 * n - 1], refs[-2 * n - 1 : -n - 1], refs[-n - 1 : -1], refs[-1]
    tokens = last[0].shape[0] // 3
    top = pl.ds(0, 3 * tokens)
    copies = [
        pltpu.make_async_copy(last[s], outs[s].at[top, :], sem.at[s]) for s in range(n)
    ]
    for copy in copies:
        copy.start()
    head = 0
    for c, count in enumerate(counts):
        first = head * VHEAD

        def put(s, h, rows, first=first):
            at = first + h * VHEAD
            low, side = (at // outs[0].shape[1]) * tokens + 3 * tokens, at % outs[0].shape[1]
            outs[s][low : low + tokens, side : side + VHEAD] = rows

        attend_heads(inputs[c * n : (c + 1) * n], tokens, put)
        head += count
    for copy in copies:
        copy.wait()


def middle(chunks, last, n, moved):
    counts = [c[0].shape[1] // VHEAD for c in chunks]
    tokens = last[0].shape[0] // 3
    width = last[0].shape[1]
    tall = 3 * tokens + -(-sum(counts) * VHEAD // width) * tokens
    pieces = [p for c in chunks for p in c]
    return pl.pallas_call(
        functools.partial(middle_kernel, n, counts),
        out_shape=(sds((tall, width)),) * n,
        in_specs=[whole()] * len(pieces) + [pl.BlockSpec(memory_space=pl.ANY)] * n,
        out_specs=(whole(),) * n,
        scratch_shapes=[pltpu.SemaphoreType.DMA((n,))],
        compiler_params=pltpu.CompilerParams(vmem_limit_bytes=16 * MIB),
        cost_estimate=pl.CostEstimate(flops=0, bytes_accessed=moved, transcendentals=0),
    )(*pieces, *last)


def last_kernel(n, tokens, *refs):
    pieces, sums, outs = refs[:n], refs[n : 2 * n], refs[2 * n :]
    width = outs[0].shape[1]

    def put(s, h, rows):
        outs[s][:tokens, h * VHEAD : (h + 1) * VHEAD] = rows

    for s in range(n):
        part = sums[s][...].astype(F32)
        blocks = [part[:, c : c + width] for c in range(0, part.shape[1], width)]
        outs[s][tokens:, :] = jnp.concatenate(blocks, axis=0).astype(BF16)
    attend_heads(pieces, tokens, put)


def unpack_kernel(n, heads, tokens, *refs):
    middles, lasts, own = refs[:n], refs[n : 2 * n][::-1], refs[2 * n]
    out, mlp, line, sem = refs[2 * n + 1 :]
    me = lax.axis_index("seq")
    width = lasts[0].shape[1]
    group = heads * VHEAD
    copies = []

    def start(source, owner, first, size):
        at = pl.ds(pl.multiple_of(owner * group + first, LANES), size)
        copies.append(pltpu.make_async_copy(source, out.at[:, at], sem.at[len(copies)]))
        copies[-1].start()

    early = group - width
    for s in range(n):
        for c in range(0, early, width):
            rows = pl.ds(3 * tokens + c // width * tokens, tokens)
            size = min(width, early - c)
            start(middles[s].at[rows, pl.ds(0, size)], lax.bitwise_xor(me, s), c, size)
        start(lasts[s].at[pl.ds(0, tokens), :], lax.bitwise_xor(me, s), early, width)
    rows, columns = own.shape
    tails = [lasts[s][tokens:, :].astype(F32) for s in range(1, n)]
    for c in range(columns // width):
        total = own[:, c * width : (c + 1) * width]
        for tail in tails:
            total = total + tail[c * rows : (c + 1) * rows]
        line[:, c * width : (c + 1) * width] = total.astype(BF16)
    copies.append(pltpu.make_async_copy(line, mlp, sem.at[len(copies)]))
    copies[-1].start()
    for copy in copies:
        copy.wait()


def unpack(middles, lasts, own, n, heads, tokens):
    count = n * (-(-(heads * VHEAD - lasts[0].shape[1]) // lasts[0].shape[1]) + 1)
    return pl.pallas_call(
        functools.partial(unpack_kernel, n, heads, tokens),
        out_shape=(sds((tokens, n * heads * VHEAD)), sds(own.shape)),
        in_specs=[pl.BlockSpec(memory_space=pltpu.VMEM)] * (2 * n + 1),
        out_specs=(pl.BlockSpec(memory_space=pl.ANY),) * 2,
        scratch_shapes=[pltpu.VMEM(own.shape, BF16), pltpu.SemaphoreType.DMA((count + 1,))],
        compiler_params=pltpu.CompilerParams(vmem_limit_bytes=16 * MIB),
    )(*middles, *lasts[::-1], own)


def low_half(shape):
    return lax.broadcasted_iota(jnp.int32, shape, 1) < CHEAD


def listen_kernel(n, tokens, rows, *refs):
    pieces, keys, values, out = refs[:n][::-1], refs[n], refs[n + 1], refs[n + 2]
    columns = keys.shape[1]
    pairs = columns // LANES
    tails = [p[3 * tokens :, :].astype(F32) for p in pieces]
    count = n * rows
    scale = LOG2E / math.sqrt(CHEAD)
    low = low_half((count, LANES))
    lane = lax.broadcasted_iota(jnp.int32, (count, LANES), 1)
    peaks = jnp.zeros((count, LANES), F32)
    totals = jnp.zeros((count, LANES), F32)
    heads = columns // CHEAD
    for pair in range(pairs):
        cols = slice(pair * LANES, (pair + 1) * LANES)
        qp = audio_rows(tails, 0, pair, rows, pairs)
        both = jnp.concatenate([jnp.where(low, qp, 0.0), jnp.where(low, 0.0, qp)], axis=0)
        s = lax.dot_general(both.astype(BF16), keys[:, cols], NT, preferred_element_type=F32)
        s = s * scale
        peak = jnp.max(s, axis=1, keepdims=True)
        w = jnp.exp2(s - peak)
        total = jnp.sum(w, axis=1, keepdims=True)
        o = jnp.dot(w.astype(BF16), values[:, cols], preferred_element_type=F32) / total
        out[:, cols] = jnp.where(low, o[:count], o[count:]).astype(BF16)
        for i in range(2):
            head = lane == 2 * pair + i
            peaks = jnp.where(head, peak[i * count : (i + 1) * count], peaks)
            totals = jnp.where(head, total[i * count : (i + 1) * count], totals)
    out[:, columns:] = share_stats(peaks[:, :heads], totals[:, :heads])


def read_shares(wholes, columns):
    heads = columns // CHEAD
    peaks, totals, parts = [], [], []
    for whole in wholes:
        parts.append(whole[:, :columns])
        piece = [whole[:, columns + j * heads : columns + (j + 1) * heads] for j in range(6)]
        peaks.append(piece[0] + piece[1] + piece[2])
        totals.append(piece[3] + piece[4] + piece[5])
    top = functools.reduce(jnp.maximum, peaks)
    weight = [t * jnp.exp2(p - top) for t, p in zip(totals, peaks)]
    every = functools.reduce(jnp.add, weight)
    return parts, [w / every for w in weight], top, every


def reorder(whole, order, n):
    rows = whole.shape[0] // n
    return jnp.concatenate([whole[(i ^ order) * rows :][:rows] for i in range(n)], axis=0)


def joint(parts, weight, pair):
    low = low_half((parts[0].shape[0], LANES))
    o = jnp.zeros(low.shape, F32)
    for w, part in zip(weight, parts):
        a, b = w[:, 2 * pair : 2 * pair + 1], w[:, 2 * pair + 1 : 2 * pair + 2]
        o = o + jnp.where(low, a, b) * part[:, pair * LANES : (pair + 1) * LANES]
    return o.astype(BF16)


def share_stats(peaks, totals):
    stats = jnp.concatenate(parts3(peaks) + parts3(totals), axis=1)
    rest = jnp.zeros((stats.shape[0], LANES - stats.shape[1]), F32)
    return jnp.concatenate([stats, rest], axis=1).astype(BF16)


def merge_kernel(n, order, own, other, out):
    columns = out.shape[1] - LANES
    wholes = own[...].astype(F32), reorder(other[...].astype(F32), order, n)
    parts, weight, top, every = read_shares(wholes, columns)
    for pair in range(columns // LANES):
        out[:, pair * LANES : (pair + 1) * LANES] = joint(parts, weight, pair)
    out[:, columns:] = share_stats(top, every)


def append_kernel(n, orders, piece, *refs):
    shares, out, sem = refs[:-2], refs[-2], refs[-1]
    count = shares[0].shape[0]
    columns = shares[0].shape[1] - LANES
    width = out.shape[1]
    base = piece.shape[0]
    copy = pltpu.make_async_copy(piece, out.at[pl.ds(0, base), :], sem)
    copy.start()
    wholes = [reorder(ref[...].astype(F32), order, n) for ref, order in zip(shares, orders)]
    parts, weight, top, every = read_shares(wholes, columns)
    blocks = [joint(parts, weight, pair) for pair in range(columns // LANES)]
    blocks.append(share_stats(top, every))
    for c, block in enumerate(blocks):
        at, side = base + c * LANES // width * count, c * LANES % width
        out[at : at + count, side : side + LANES] = block
    if len(blocks) * LANES % width:
        side = len(blocks) * LANES % width
        out[at : at + count, side:] = jnp.zeros((count, width - side), BF16)
    copy.wait()


def append(n, orders, piece, shares):
    count, columns = shares[0].shape
    width = piece.shape[1]
    tall = piece.shape[0] + -(-columns // width) * count
    return pl.pallas_call(
        functools.partial(append_kernel, n, orders),
        out_shape=sds((tall, width)),
        in_specs=[pl.BlockSpec(memory_space=pl.ANY)] + [whole()] * len(shares),
        out_specs=whole(),
        scratch_shapes=[pltpu.SemaphoreType.DMA],
        compiler_params=pltpu.CompilerParams(vmem_limit_bytes=16 * MIB),
    )(piece, *shares)


def combine_kernel(n, base, tokens, rows, *refs):
    got, pieces, (gain, up) = refs[:2], refs[2 : 2 + n], refs[2 + n : 4 + n]
    own_sum, sent_sum, seen, x_ref = refs[4 + n :]

    @pl.when(pl.program_id(0) == 0)
    def _():
        columns = seen.shape[1]
        wholes = []
        for ref, order in zip(got, (0, 1)):
            blocks = [ref[at : at + n * rows, :] for at in range(base, ref.shape[0], n * rows)]
            wholes.append(reorder(jnp.concatenate(blocks, axis=1).astype(F32), order, n))
        parts, weight, _, _ = read_shares(wholes, columns)
        tails = [p[3 * tokens :, :].astype(F32) for p in pieces]
        square = jnp.zeros((n * rows, 1), F32)
        for pair in range(columns // LANES):
            cols = slice(pair * LANES, (pair + 1) * LANES)
            o = joint(parts, weight, pair)
            seen[:, cols] = o[:rows]
            residual = audio_rows(tails, 3, pair, rows, columns // LANES) + o.astype(F32)
            square = square + jnp.sum(residual * residual, axis=1, keepdims=True)
            at = pl.ds(pl.multiple_of(lax.axis_index("tp") * columns + pair * LANES, LANES), LANES)
            x_ref[:, cols] = (residual * gain[:, at]).astype(BF16)
        lane = lax.broadcasted_iota(jnp.int32, (n * rows, LANES), 1)
        first, second, third = parts3(square)
        spread = jnp.where(lane == 0, first, jnp.where(lane == 1, second, third))
        spread = jnp.where(lane < 3, spread, 0.0)
        own_sum[0, :, :LANES] = spread
        sent_sum[0, :, :LANES] = spread.astype(BF16)

    @pl.when(pl.program_id(0) > 0)
    def _():
        product = jnp.dot(x_ref[...], up[...], preferred_element_type=F32)
        own_sum[0] = product
        sent_sum[0] = product.astype(BF16)


def combine(got, base, pieces, gain, up, tokens, rows, block):
    n = len(pieces)
    columns, units = up.shape
    steps = units // block + 1
    held = lambda ref: pl.BlockSpec(ref.shape, lambda i: (0,) * ref.ndim)
    moved = pl.BlockSpec((1, n * rows, block), lambda i: (i, 0, 0))
    return pl.pallas_call(
        functools.partial(combine_kernel, n, base, tokens, rows),
        grid=(steps,),
        out_shape=(
            sds((steps, n * rows, block), F32),
            sds((steps, n * rows, block)),
            sds((rows, columns)),
        ),
        in_specs=[held(r) for r in (*got, *pieces, gain)]
        + [pl.BlockSpec((columns, block), lambda i: (0, jnp.maximum(i - 1, 0)))],
        out_specs=(moved, moved, pl.BlockSpec((rows, columns), lambda i: (0, 0))),
        scratch_shapes=[pltpu.VMEM((n * rows, columns), BF16)],
        compiler_params=pltpu.CompilerParams(vmem_limit_bytes=32 * MIB),
        cost_estimate=pl.CostEstimate(
            flops=0, bytes_accessed=0 * MIB, transcendentals=0
        ),
    )(*got, *pieces, gain, up)


def finish_kernel(n, features, own, other, down, *refs):
    outs, hidden = refs[:n], refs[n]
    rows = outs[0].shape[0]

    @pl.when(pl.program_id(0) == 0)
    def _():
        square = own[0, :, :LANES] + other[0, :, :LANES].astype(F32)
        square = jnp.sum(square, axis=1, keepdims=True)
        scale = lax.rsqrt(square / features + 1e-6)
        block = own.shape[2]
        for i in range(1, own.shape[0]):
            total = (own[i] + other[i].astype(F32)) * scale
            hidden[:, (i - 1) * block : i * block] = jax.nn.gelu(total).astype(BF16)

    product = jnp.dot(hidden[...], down[...], preferred_element_type=F32)
    for s in range(n):
        outs[s][...] = product[s * rows : (s + 1) * rows].astype(outs[s].dtype)


def finish(own, other, down, n, rows, features, block):
    units, columns = down.shape
    held = lambda ref: pl.BlockSpec(ref.shape, lambda i: (0,) * ref.ndim)
    return pl.pallas_call(
        functools.partial(finish_kernel, n, features),
        grid=(columns // block,),
        out_shape=(sds((rows, columns), F32),) + (sds((rows, columns)),) * (n - 1),
        in_specs=[held(own), held(other), pl.BlockSpec((units, block), lambda i: (0, i))],
        out_specs=(pl.BlockSpec((rows, block), lambda i: (0, i)),) * n,
        scratch_shapes=[pltpu.VMEM((n * rows, units), BF16)],
        compiler_params=pltpu.CompilerParams(vmem_limit_bytes=32 * MIB),
        cost_estimate=pl.CostEstimate(
            flops=0, bytes_accessed=0 * MIB, transcendentals=0
        ),
    )(own, other, down)


def heard_kernel(n, tokens, rows, q, *refs):
    pieces, out = refs[:n], refs[n]
    pairs = q.shape[1] // LANES
    tails = [p[3 * tokens :, :].astype(F32) for p in pieces]
    count = n * rows
    low = low_half((count, LANES))
    scale = LOG2E / math.sqrt(CHEAD)

    def both(part, pair):
        x = audio_rows(tails, part, pair, rows, pairs)
        return jnp.concatenate([jnp.where(low, x, 0.0), jnp.where(low, 0.0, x)], axis=0).astype(BF16)

    for pair in range(pairs):
        cols = slice(pair * LANES, (pair + 1) * LANES)
        s = lax.dot_general(both(1, pair), q[:, cols], NT, preferred_element_type=F32) * scale
        probs = []
        for i in range(2):
            t = s[i * count : (i + 1) * count]
            w = jnp.exp2(t - jnp.max(t, axis=0, keepdims=True))
            probs.append(w / jnp.sum(w, axis=0, keepdims=True))
        w = jnp.concatenate(probs, axis=0).astype(BF16)
        out[:, cols] = lax.dot_general(w, both(2, pair), TN, preferred_element_type=F32).astype(BF16)


def short_body(vq, vk, vv, cq, ak, av, aq, ck, cv, ai, gain, up, down):
    n = lax.axis_size("seq")
    tokens = vq.shape[0]
    rows, columns = aq.shape
    features = ai.shape[1]
    heads = vq.shape[1] // n // VHEAD
    widths = [c * VHEAD for c in (1, 1, heads - 2)]
    video = (vq, vk, vv)

    def send(own, *first):
        return [own[0]] + [trade(after(own[s], *first), s) for s in range(1, n)]

    wait = 16 * MIB
    packed = pack(video, (aq, ak, av, ai), (), n, 0, widths[:1], 60, 6 * vq.size)
    chunk_0 = send(packed)
    packed = pack(video, (), (packed[0], ck, cv), n, widths[0], widths[1:], 16, wait)
    *packed, chunk_0[0], ck, cv = packed
    chunk_1 = send(packed[:n])
    (share,) = call(
        functools.partial(listen_kernel, n, tokens, rows),
        (*chunk_0[::-1], ck, cv),
        [sds((n * rows, columns + LANES))],
        moved=4 * vq.size,
        limit=16,
    )
    order = n // 2
    while order > 2:
        (share,) = call(
            functools.partial(merge_kernel, n, order),
            (share, trade(share, order)),
            [sds(share.shape)],
            limit=16,
        )
        order //= 2
    shares = [share, trade(share, 2)] if n > 2 else [share]
    built = middle([chunk_0, chunk_1], packed[n:], n, MIB)
    below = append(n, (0, 2), built[1], shares)
    chunk_2 = [built[0], trade(below, 1)]
    chunk_2 += [trade(after(built[s], shares[1]), s) for s in range(2, n)]
    (heard,) = call(
        functools.partial(heard_kernel, n, tokens, rows),
        (cq, *chunk_0),
        [sds(cq.shape)],
        moved=1 * MIB,
        limit=16,
    )
    gain = after(gain.reshape(1, -1), heard)
    own_sum, sent_sum, seen = combine((below, chunk_2[1]), built[1].shape[0], chunk_0, gain, up, tokens, rows, 512)
    other_sum = lax.ppermute(sent_sum, "tp", [(0, 1), (1, 0)])
    results = finish(own_sum, other_sum, down, n, rows, features, 512)
    ends = call(
        functools.partial(last_kernel, n, tokens),
        (*chunk_2, *results),
        [sds((tokens + rows * columns // widths[2], widths[2]))] * n,
        limit=16,
    )
    ends = [ends[0]] + [trade(ends[s], s) for s in range(1, n)]
    mixed, mlp = unpack(chunk_2, ends, results[0], n, heads, tokens)
    return mixed, heard, seen, mlp


def fits(vq, cq, aq, up, down):
    n = lax.axis_size("seq")
    heads = vq.shape[1] // VHEAD
    return (
        n in (2, 4, 8)
        and lax.axis_size("tp") == 2
        and heads % n == 0
        and heads // n > 2
        and vq.shape[0] == LANES
        and n * vq.shape[0] <= 1024
        and aq.shape[0] % 8 == 0
        and n * aq.shape[0] <= 64
        and 6 * (aq.shape[1] // CHEAD) < LANES
        and aq.shape[1] % VHEAD == 0
        and up.shape[1] % 512 == 0
        and down.shape[1] % 512 == 0
    )


def body(*args):
    *arrays, gain, up, down = args
    arrays = [a[0] for a in arrays]
    path = short_body if fits(arrays[0], arrays[3], arrays[6], up, down) else general_body
    return tuple(out[None] for out in path(*arrays, gain, up, down))


def solution(mesh):
    rows = P(("clips", "dp"), "seq", "tp")
    placed = (rows,) * 9 + (P(("clips", "dp"), "seq", None), P(), P("tp", "seq"), P("seq", "tp"))
    return jax.shard_map(
        body, mesh=mesh, in_specs=placed, out_specs=(rows,) * 4, check_vma=False
    )
```

```python
import functools
import math

import jax
import jax.numpy as jnp
from jax import lax
from jax.experimental import pallas as pl
from jax.experimental.pallas import tpu as pltpu
from jax.sharding import PartitionSpec as P

VHEAD = 128
CHEAD = 64
LANES = 128
F32 = jnp.float32
BF16 = jnp.bfloat16
LOG2E = math.log2(math.e)
MIB = 1024 * 1024
NT = (((1,), (1,)), ((), ()))
TN = (((0,), (0,)), ((), ()))


def attend_rows(queries, keys_in, values_in, head_count):
    head_size = queries.shape[1] // head_count
    query_heads = queries.reshape(queries.shape[0], head_count, head_size)
    key_heads = keys_in.reshape(keys_in.shape[0], head_count, head_size)
    value_heads = values_in.reshape(values_in.shape[0], head_count, head_size)
    scores = jnp.einsum(
        "qhd,khd->qhk", query_heads, key_heads, preferred_element_type=jnp.float32
    ) / math.sqrt(head_size)
    peak_value = jnp.max(scores, axis=2, keepdims=True)
    weights = jnp.exp(scores - peak_value)
    totals = jnp.sum(weights, axis=2)
    weighted = jnp.einsum(
        "qhk,khd->qhd",
        weights.astype(jnp.bfloat16),
        value_heads,
        preferred_element_type=jnp.float32,
    )
    result = weighted / totals[:, :, None]
    return result.reshape(queries.shape[0], head_count * head_size).astype(jnp.bfloat16)


def attend(queries, keys_in, values_in, head_count):
    row_total = queries.shape[0]
    block_rows = 512 if row_total % 512 == 0 else row_total
    pieces = queries.reshape(row_total // block_rows, block_rows, queries.shape[1])
    result = lax.map(
        lambda row_piece: attend_rows(row_piece, keys_in, values_in, head_count), pieces
    )
    return result.reshape(row_total, queries.shape[1])


def video_self(queries, keys_in, values_in):
    seq_count = lax.axis_size("seq")
    local_heads = queries.shape[1] // VHEAD
    dest_heads = max(local_heads // seq_count, 1)
    blocks = seq_count * dest_heads // local_heads
    groups = local_heads // dest_heads
    group_width = dest_heads * VHEAD
    token_count = queries.shape[0]
    block_tokens = token_count // blocks

    def spread(tensor):
        shaped = tensor.reshape(token_count, groups, group_width).transpose(1, 0, 2)
        shaped = jnp.broadcast_to(shaped[:, None], (groups, blocks, token_count, group_width))
        return shaped.reshape(seq_count, token_count, group_width)

    shaped = queries.reshape(blocks, block_tokens, groups, group_width).transpose(2, 0, 1, 3)
    own_queries = lax.all_to_all(
        shaped.reshape(seq_count, block_tokens, group_width),
        "seq",
        split_axis=0,
        concat_axis=0,
        tiled=True,
    )
    keys_all = lax.all_to_all(spread(keys_in), "seq", split_axis=0, concat_axis=0, tiled=True)
    values_all = lax.all_to_all(spread(values_in), "seq", split_axis=0, concat_axis=0, tiled=True)
    keys_all = keys_all.reshape(-1, group_width)
    values_all = values_all.reshape(-1, group_width)
    own_queries = own_queries.reshape(-1, group_width)
    attended = attend(own_queries, keys_all, values_all, dest_heads)
    returned = lax.all_to_all(
        attended.reshape(seq_count, block_tokens, group_width),
        "seq",
        split_axis=0,
        concat_axis=0,
        tiled=True,
    )
    returned = returned.reshape(groups, blocks, block_tokens, group_width).transpose(1, 2, 0, 3)
    return returned.reshape(token_count, groups * group_width)


def audio_listen(queries, keys_in, values_in, head_count):
    head_size = queries.shape[1] // head_count
    query_heads = queries.reshape(queries.shape[0], head_count, head_size)
    key_heads = keys_in.reshape(keys_in.shape[0], head_count, head_size)
    value_heads = values_in.reshape(values_in.shape[0], head_count, head_size)
    scores = jnp.einsum(
        "qhd,khd->qhk", query_heads, key_heads, preferred_element_type=jnp.float32
    ) / math.sqrt(head_size)
    local_peak = jnp.max(scores, axis=2)
    peak_value = lax.pmax(local_peak, "seq")
    weights = jnp.exp(scores - peak_value[:, :, None])
    totals = jnp.sum(weights, axis=2)
    weighted = jnp.einsum(
        "qhk,khd->qhd",
        weights.astype(jnp.bfloat16),
        value_heads,
        preferred_element_type=jnp.float32,
    )
    weighted = weighted.reshape(queries.shape[0], head_count * head_size)
    totals = lax.psum_scatter(totals, "seq", scatter_dimension=0, tiled=True)
    weighted = lax.psum_scatter(weighted, "seq", scatter_dimension=0, tiled=True)
    return (weighted / jnp.repeat(totals, head_size, axis=1)).astype(jnp.bfloat16)


def audio_block(audio_rows, audio_seen, norm_gain, up_weight, down_weight):
    features = lax.all_gather(audio_seen, "tp", axis=1, tiled=True)
    residual = audio_rows.astype(jnp.float32) + features.astype(jnp.float32)
    scale_factor = lax.rsqrt(jnp.mean(residual * residual, axis=1, keepdims=True) + 1e-06)
    normed = (residual * scale_factor * norm_gain).astype(jnp.bfloat16)
    slice_width = up_weight.shape[0]
    own_features = lax.dynamic_slice_in_dim(
        normed, lax.axis_index("tp") * slice_width, slice_width, 1
    )
    partial_sum = jnp.dot(
        lax.all_gather(own_features, "seq", axis=0, tiled=True),
        up_weight,
        preferred_element_type=jnp.float32,
    )
    hidden = jax.nn.gelu(lax.psum(partial_sum, "tp")).astype(jnp.bfloat16)
    return lax.psum_scatter(
        jnp.dot(hidden, down_weight, preferred_element_type=jnp.float32),
        "seq",
        scatter_dimension=0,
        tiled=True,
    ).astype(jnp.bfloat16)


def general_body(vq, vk, vv, cq, ak, av, aq, ck, cv, ai, gain, up, down):
    cross_heads = cq.shape[1] // CHEAD
    mixed = video_self(vq, vk, vv)
    gathered_query = lax.all_gather(aq, "seq", axis=0, tiled=True)
    gathered_key = lax.all_gather(ak, "seq", axis=0, tiled=True)
    gathered_value = lax.all_gather(av, "seq", axis=0, tiled=True)
    heard = attend(cq, gathered_key, gathered_value, cross_heads)
    seen = audio_listen(gathered_query, ck, cv, cross_heads)
    mlp = audio_block(ai, seen, gain, up, down)
    return mixed, heard, seen, mlp


def whole():
    return pl.BlockSpec()


def after(value, *others):
    return lax.optimization_barrier((value, *others))[0]


def sds(shape, dtype=BF16):
    return jax.ShapeDtypeStruct(shape, dtype)


def call(kernel, ins, outs, flops=0, moved=0, limit=32):
    return pl.pallas_call(
        kernel,
        out_shape=tuple(outs),
        in_specs=[whole()] * len(ins),
        out_specs=tuple(whole() for _ in outs),
        compiler_params=pltpu.CompilerParams(vmem_limit_bytes=limit * MIB),
        cost_estimate=pl.CostEstimate(flops=flops, bytes_accessed=moved, transcendentals=0),
    )(*ins)


def trade(value, by):
    n = lax.axis_size("seq")
    return lax.ppermute(value, "seq", [(i, i ^ by) for i in range(n)])


def parts3(value):
    first = value.astype(BF16).astype(F32)
    second = (value - first).astype(BF16).astype(F32)
    return first, second, value - first - second


def pack_kernel(n, first, widths, audio_count, kept, q, k, v, *refs):
    count = n * len(widths)
    audio, refs = refs[:audio_count], refs[audio_count:]
    keep, refs = refs[:kept], refs[kept:]
    outs, passed, refs = refs[:count], refs[count : count + kept], refs[count + kept :]
    built = refs[:count] if audio else outs
    lines, sem, audio_sem, out_sem = refs[-3 - audio_count : -3], refs[-3], refs[-2], refs[-1]
    me = lax.axis_index("seq")
    tokens = q.shape[0]
    group = q.shape[1] // n
    fetches = [pltpu.make_async_copy(ref, to, audio_sem.at[i]) for i, (ref, to) in enumerate(zip(audio, lines))]
    for copy in fetches:
        copy.start()
    copies, arrivals = [], []
    for c, width in enumerate(widths):
        for s in range(n):
            at = pl.ds(pl.multiple_of(lax.bitwise_xor(me, s) * group + first, LANES), width)
            for i, ref in enumerate((q, k, v)):
                to = built[c * n + s].at[pl.ds(i * tokens, tokens), :]
                arrivals.append(pltpu.make_async_copy(ref.at[:, at], to, sem.at[len(arrivals)]))
                arrivals[-1].start()
        first += width
    for i, (ref, to) in enumerate(zip(keep, passed)):
        copies.append(pltpu.make_async_copy(ref, to, out_sem.at[count + i]))
        copies[-1].start()
    if audio:
        for copy in fetches:
            copy.wait()
        half = lines[0].shape[1]
        mine = pl.ds(pl.multiple_of(lax.axis_index("tp") * half, LANES), half)
        parts = [ref[...].astype(F32) for ref in lines[:3]] + [lines[3][:, mine].astype(F32)]
        blocks = [part[:, c : c + widths[0]] for part in parts for c in range(0, half, widths[0])]
        extra = jnp.concatenate(blocks, axis=0).astype(BF16)
        for s in range(n):
            built[s][3 * tokens :, :] = extra
    for i in range(count):
        for copy in arrivals[3 * i : 3 * i + 3]:
            copy.wait()
        if audio:
            copies.append(pltpu.make_async_copy(built[i], outs[i], out_sem.at[i]))
            copies[-1].start()
    for copy in copies:
        copy.wait()


def pack(video, audio, keep, n, first, widths, limit, moved):
    tokens = video[0].shape[0]
    extra = 4 * audio[0].size // widths[0] if audio else 0
    shapes = [(3 * tokens + extra, w) for w in widths for _ in range(n)]
    stay = pl.BlockSpec(memory_space=pl.ANY)
    dma = pltpu.SemaphoreType.DMA
    return pl.pallas_call(
        functools.partial(pack_kernel, n, first, widths, len(audio), len(keep)),
        out_shape=tuple(sds(x) for x in shapes) + tuple(sds(x.shape) for x in keep),
        in_specs=[stay] * (3 + len(audio) + len(keep)),
        out_specs=(stay if audio else whole(),) * (len(shapes) + len(keep)),
        scratch_shapes=[pltpu.VMEM(x, BF16) for x in shapes if audio]
        + [pltpu.VMEM(x.shape, BF16) for x in audio]
        + [dma((3 * len(shapes),)), dma((max(len(audio), 1),)), dma((len(shapes) + len(keep),))],
        compiler_params=pltpu.CompilerParams(vmem_limit_bytes=limit * MIB),
        cost_estimate=pl.CostEstimate(flops=0, bytes_accessed=moved, transcendentals=0),
    )(*video, *audio, *keep)


def audio_rows(tails, part, pair, rows, pairs):
    per = tails[0].shape[1] // LANES
    at, side = (part * pairs + pair) // per * rows, pair % per * LANES
    return jnp.concatenate([t[at : at + rows, side : side + LANES] for t in tails], axis=0)


def attend_heads(pieces, tokens, put):
    scale = LOG2E / math.sqrt(VHEAD)
    for h in range(pieces[0].shape[1] // VHEAD):
        cols = slice(h * VHEAD, (h + 1) * VHEAD)
        keys = jnp.concatenate([p[tokens : 2 * tokens, cols] for p in pieces], axis=0)
        values = jnp.concatenate([p[2 * tokens : 3 * tokens, cols] for p in pieces], axis=0)
        values = jnp.concatenate([values, jnp.ones_like(values)], axis=1)
        for s, p in enumerate(pieces):
            t = lax.dot_general(p[0:tokens, cols], keys, NT, preferred_element_type=F32)
            w = jnp.exp2((t - jnp.max(t, axis=1, keepdims=True)) * scale)
            o = jnp.dot(w.astype(BF16), values, preferred_element_type=F32)
            put(s, h, (o[:, :VHEAD] / o[:, VHEAD:]).astype(BF16))


def first_kernel(n, tokens, *refs):
    pieces, outs = refs[:n], refs[n:]

    def put(s, h, rows):
        outs[s][:, h * VHEAD : (h + 1) * VHEAD] = rows

    attend_heads(pieces, tokens, put)


def middle_kernel(n, *refs):
    pieces, before, last = refs[:n], refs[n : 2 * n], refs[2 * n : 3 * n]
    outs, sem = refs[3 * n : -1], refs[-1]
    tokens = last[0].shape[0] // 3
    early, width = before[0].shape[1], outs[0].shape[1]
    copies = []
    for s in range(n):
        top, below = pl.ds(0, 3 * tokens), pl.ds(3 * tokens, tokens)
        copies.append(pltpu.make_async_copy(last[s], outs[s].at[top, :], sem.at[2 * s]))
        to = outs[s].at[below, pl.ds(0, early)]
        copies.append(pltpu.make_async_copy(before[s], to, sem.at[2 * s + 1]))
    for copy in copies:
        copy.start()

    def put(s, h, rows):
        at = early + h * VHEAD
        outs[s][3 * tokens :, at : at + VHEAD] = rows

    attend_heads(pieces, tokens, put)
    for copy in copies:
        copy.wait()


def middle(chunk, before, last, n, moved):
    tokens = last[0].shape[0] // 3
    stay = pl.BlockSpec(memory_space=pl.ANY)
    return pl.pallas_call(
        functools.partial(middle_kernel, n),
        out_shape=(sds((4 * tokens, last[0].shape[1])),) * n,
        in_specs=[whole()] * n + [stay] * (2 * n),
        out_specs=(whole(),) * n,
        scratch_shapes=[pltpu.SemaphoreType.DMA((2 * n,))],
        compiler_params=pltpu.CompilerParams(vmem_limit_bytes=16 * MIB),
        cost_estimate=pl.CostEstimate(flops=0, bytes_accessed=moved, transcendentals=0),
    )(*chunk, *before, *last)


def last_kernel(n, tokens, *refs):
    pieces, sums, outs = refs[:n], refs[n : 2 * n], refs[2 * n :]
    width = outs[0].shape[1]

    def put(s, h, rows):
        outs[s][:tokens, h * VHEAD : (h + 1) * VHEAD] = rows

    for s in range(n):
        part = sums[s][...].astype(F32)
        blocks = [part[:, c : c + width] for c in range(0, part.shape[1], width)]
        outs[s][tokens:, :] = jnp.concatenate(blocks, axis=0).astype(BF16)
    attend_heads(pieces, tokens, put)


def unpack_kernel(n, heads, tokens, *refs):
    middles, lasts, own = refs[:n], refs[n : 2 * n][::-1], refs[2 * n]
    out, mlp, line, sem = refs[2 * n + 1 :]
    me = lax.axis_index("seq")
    width = lasts[0].shape[1]
    group = heads * VHEAD
    copies = []

    def start(source, owner, first, size):
        at = pl.ds(pl.multiple_of(owner * group + first, LANES), size)
        copies.append(pltpu.make_async_copy(source, out.at[:, at], sem.at[len(copies)]))
        copies[-1].start()

    early = group - width
    for s in range(n):
        for c in range(0, early, width):
            rows = pl.ds(3 * tokens + c // width * tokens, tokens)
            size = min(width, early - c)
            start(middles[s].at[rows, pl.ds(0, size)], lax.bitwise_xor(me, s), c, size)
        start(lasts[s].at[pl.ds(0, tokens), :], lax.bitwise_xor(me, s), early, width)
    rows, columns = own.shape
    tails = [lasts[s][tokens:, :].astype(F32) for s in range(1, n)]
    for c in range(columns // width):
        total = own[:, c * width : (c + 1) * width]
        for tail in tails:
            total = total + tail[c * rows : (c + 1) * rows]
        line[:, c * width : (c + 1) * width] = total.astype(BF16)
    copies.append(pltpu.make_async_copy(line, mlp, sem.at[len(copies)]))
    copies[-1].start()
    for copy in copies:
        copy.wait()


def unpack(middles, lasts, own, n, heads, tokens):
    count = n * (-(-(heads * VHEAD - lasts[0].shape[1]) // lasts[0].shape[1]) + 1)
    return pl.pallas_call(
        functools.partial(unpack_kernel, n, heads, tokens),
        out_shape=(sds((tokens, n * heads * VHEAD)), sds(own.shape)),
        in_specs=[pl.BlockSpec(memory_space=pltpu.VMEM)] * (2 * n + 1),
        out_specs=(pl.BlockSpec(memory_space=pl.ANY),) * 2,
        scratch_shapes=[pltpu.VMEM(own.shape, BF16), pltpu.SemaphoreType.DMA((count + 1,))],
        compiler_params=pltpu.CompilerParams(vmem_limit_bytes=16 * MIB),
    )(*middles, *lasts[::-1], own)


def low_half(shape):
    return lax.broadcasted_iota(jnp.int32, shape, 1) < CHEAD


def listen_kernel(n, tokens, rows, *refs):
    pieces, keys, values, out = refs[:n][::-1], refs[n], refs[n + 1], refs[n + 2]
    columns = keys.shape[1]
    pairs = columns // LANES
    tails = [p[3 * tokens :, :].astype(F32) for p in pieces]
    count = n * rows
    scale = LOG2E / math.sqrt(CHEAD)
    low = low_half((count, LANES))
    lane = lax.broadcasted_iota(jnp.int32, (count, LANES), 1)
    peaks = jnp.zeros((count, LANES), F32)
    totals = jnp.zeros((count, LANES), F32)
    heads = columns // CHEAD
    for pair in range(pairs):
        cols = slice(pair * LANES, (pair + 1) * LANES)
        qp = audio_rows(tails, 0, pair, rows, pairs)
        both = jnp.concatenate([jnp.where(low, qp, 0.0), jnp.where(low, 0.0, qp)], axis=0)
        s = lax.dot_general(both.astype(BF16), keys[:, cols], NT, preferred_element_type=F32)
        s = s * scale
        peak = jnp.max(s, axis=1, keepdims=True)
        w = jnp.exp2(s - peak)
        wide = jnp.concatenate([values[:, cols], jnp.ones_like(values[:, cols])], axis=1)
        o = jnp.dot(w.astype(BF16), wide, preferred_element_type=F32)
        o, total = o[:, :LANES] / o[:, LANES:], o[:, LANES:]
        out[:, cols] = jnp.where(low, o[:count], o[count:]).astype(BF16)
        for i in range(2):
            head = lane == 2 * pair + i
            peaks = jnp.where(head, peak[i * count : (i + 1) * count], peaks)
            totals = jnp.where(head, total[i * count : (i + 1) * count], totals)
    out[:, columns:] = share_stats(peaks[:, :heads], totals[:, :heads])


def read_shares(wholes, columns):
    heads = columns // CHEAD
    peaks, totals, parts = [], [], []
    for whole in wholes:
        parts.append(whole[:, :columns])
        piece = [whole[:, columns + j * heads : columns + (j + 1) * heads] for j in range(6)]
        peaks.append(piece[0] + piece[1] + piece[2])
        totals.append(piece[3] + piece[4] + piece[5])
    top = functools.reduce(jnp.maximum, peaks)
    weight = [t * jnp.exp2(p - top) for t, p in zip(totals, peaks)]
    every = functools.reduce(jnp.add, weight)
    return parts, [w / every for w in weight], top, every


def reorder(whole, order, n):
    rows = whole.shape[0] // n
    return jnp.concatenate([whole[(i ^ order) * rows :][:rows] for i in range(n)], axis=0)


def joint(parts, weight, pair):
    low = low_half((parts[0].shape[0], LANES))
    o = jnp.zeros(low.shape, F32)
    for w, part in zip(weight, parts):
        a, b = w[:, 2 * pair : 2 * pair + 1], w[:, 2 * pair + 1 : 2 * pair + 2]
        o = o + jnp.where(low, a, b) * part[:, pair * LANES : (pair + 1) * LANES]
    return o.astype(BF16)


def share_stats(peaks, totals):
    stats = jnp.concatenate(parts3(peaks) + parts3(totals), axis=1)
    rest = jnp.zeros((stats.shape[0], LANES - stats.shape[1]), F32)
    return jnp.concatenate([stats, rest], axis=1).astype(BF16)


def merge_kernel(n, order, own, other, out):
    columns = out.shape[1] - LANES
    wholes = own[...].astype(F32), reorder(other[...].astype(F32), order, n)
    parts, weight, top, every = read_shares(wholes, columns)
    for pair in range(columns // LANES):
        out[:, pair * LANES : (pair + 1) * LANES] = joint(parts, weight, pair)
    out[:, columns:] = share_stats(top, every)


def append_kernel(n, orders, piece, *refs):
    shares, out, sem = refs[:-2], refs[-2], refs[-1]
    count = shares[0].shape[0]
    columns = shares[0].shape[1] - LANES
    width = out.shape[1]
    base = piece.shape[0]
    copy = pltpu.make_async_copy(piece, out.at[pl.ds(0, base), :], sem)
    copy.start()
    wholes = [reorder(ref[...].astype(F32), order, n) for ref, order in zip(shares, orders)]
    parts, weight, top, every = read_shares(wholes, columns)
    blocks = [joint(parts, weight, pair) for pair in range(columns // LANES)]
    blocks.append(share_stats(top, every))
    for c, block in enumerate(blocks):
        at, side = base + c * LANES // width * count, c * LANES % width
        out[at : at + count, side : side + LANES] = block
    if len(blocks) * LANES % width:
        side = len(blocks) * LANES % width
        out[at : at + count, side:] = jnp.zeros((count, width - side), BF16)
    copy.wait()


def append(n, orders, piece, shares):
    count, columns = shares[0].shape
    width = piece.shape[1]
    tall = piece.shape[0] + -(-columns // width) * count
    return pl.pallas_call(
        functools.partial(append_kernel, n, orders),
        out_shape=sds((tall, width)),
        in_specs=[pl.BlockSpec(memory_space=pl.ANY)] + [whole()] * len(shares),
        out_specs=whole(),
        scratch_shapes=[pltpu.SemaphoreType.DMA],
        compiler_params=pltpu.CompilerParams(vmem_limit_bytes=16 * MIB),
    )(piece, *shares)


def combine_kernel(n, base, tokens, rows, *refs):
    got, pieces, (gain, up) = refs[:2], refs[2 : 2 + n], refs[2 + n : 4 + n]
    own_sum, sent_sum, seen, x_ref = refs[4 + n :]

    @pl.when(pl.program_id(0) == 0)
    def _():
        columns = seen.shape[1]
        wholes = []
        for ref, order in zip(got, (0, 1)):
            blocks = [ref[at : at + n * rows, :] for at in range(base, ref.shape[0], n * rows)]
            wholes.append(reorder(jnp.concatenate(blocks, axis=1).astype(F32), order, n))
        parts, weight, _, _ = read_shares(wholes, columns)
        tails = [p[3 * tokens :, :].astype(F32) for p in pieces]
        square = jnp.zeros((n * rows, 1), F32)
        for pair in range(columns // LANES):
            cols = slice(pair * LANES, (pair + 1) * LANES)
            o = joint(parts, weight, pair)
            seen[:, cols] = o[:rows]
            residual = audio_rows(tails, 3, pair, rows, columns // LANES) + o.astype(F32)
            square = square + jnp.sum(residual * residual, axis=1, keepdims=True)
            at = pl.ds(pl.multiple_of(lax.axis_index("tp") * columns + pair * LANES, LANES), LANES)
            x_ref[:, cols] = (residual * gain[:, at]).astype(BF16)
        lane = lax.broadcasted_iota(jnp.int32, (n * rows, LANES), 1)
        first, second, third = parts3(square)
        spread = jnp.where(lane == 0, first, jnp.where(lane == 1, second, third))
        spread = jnp.where(lane < 3, spread, 0.0)
        own_sum[0, :, :LANES] = spread
        sent_sum[0, :, :LANES] = spread.astype(BF16)

    @pl.when(pl.program_id(0) > 0)
    def _():
        product = jnp.dot(x_ref[...], up[...], preferred_element_type=F32)
        own_sum[0] = product
        sent_sum[0] = product.astype(BF16)


def combine(got, base, pieces, gain, up, tokens, rows, block):
    n = len(pieces)
    columns, units = up.shape
    steps = units // block + 1
    held = lambda ref: pl.BlockSpec(ref.shape, lambda i: (0,) * ref.ndim)
    moved = pl.BlockSpec((1, n * rows, block), lambda i: (i, 0, 0))
    return pl.pallas_call(
        functools.partial(combine_kernel, n, base, tokens, rows),
        grid=(steps,),
        out_shape=(
            sds((steps, n * rows, block), F32),
            sds((steps, n * rows, block)),
            sds((rows, columns)),
        ),
        in_specs=[held(r) for r in (*got, *pieces, gain)]
        + [pl.BlockSpec((columns, block), lambda i: (0, jnp.maximum(i - 1, 0)))],
        out_specs=(moved, moved, pl.BlockSpec((rows, columns), lambda i: (0, 0))),
        scratch_shapes=[pltpu.VMEM((n * rows, columns), BF16)],
        compiler_params=pltpu.CompilerParams(vmem_limit_bytes=32 * MIB),
        cost_estimate=pl.CostEstimate(
            flops=0, bytes_accessed=0 * MIB, transcendentals=0
        ),
    )(*got, *pieces, gain, up)


def finish_kernel(n, features, own, other, down, *refs):
    outs, hidden = refs[:n], refs[n]
    rows = outs[0].shape[0]

    @pl.when(pl.program_id(0) == 0)
    def _():
        square = own[0, :, :LANES] + other[0, :, :LANES].astype(F32)
        square = jnp.sum(square, axis=1, keepdims=True)
        scale = lax.rsqrt(square / features + 1e-6)
        block = own.shape[2]
        for i in range(1, own.shape[0]):
            total = (own[i] + other[i].astype(F32)) * scale
            hidden[:, (i - 1) * block : i * block] = jax.nn.gelu(total).astype(BF16)

    product = jnp.dot(hidden[...], down[...], preferred_element_type=F32)
    for s in range(n):
        outs[s][...] = product[s * rows : (s + 1) * rows].astype(outs[s].dtype)


def finish(own, other, down, n, rows, features, block):
    units, columns = down.shape
    held = lambda ref: pl.BlockSpec(ref.shape, lambda i: (0,) * ref.ndim)
    return pl.pallas_call(
        functools.partial(finish_kernel, n, features),
        grid=(columns // block,),
        out_shape=(sds((rows, columns), F32),) + (sds((rows, columns)),) * (n - 1),
        in_specs=[held(own), held(other), pl.BlockSpec((units, block), lambda i: (0, i))],
        out_specs=(pl.BlockSpec((rows, block), lambda i: (0, i)),) * n,
        scratch_shapes=[pltpu.VMEM((n * rows, units), BF16)],
        compiler_params=pltpu.CompilerParams(vmem_limit_bytes=32 * MIB),
        cost_estimate=pl.CostEstimate(
            flops=0, bytes_accessed=0 * MIB, transcendentals=0
        ),
    )(own, other, down)


def heard_kernel(n, tokens, rows, q, *refs):
    pieces, out = refs[:n], refs[n]
    pairs = q.shape[1] // LANES
    tails = [p[3 * tokens :, :].astype(F32) for p in pieces]
    count = n * rows
    low = low_half((count, LANES))
    scale = LOG2E / math.sqrt(CHEAD)

    def both(part, pair):
        x = audio_rows(tails, part, pair, rows, pairs)
        return jnp.concatenate([jnp.where(low, x, 0.0), jnp.where(low, 0.0, x)], axis=0).astype(BF16)

    for pair in range(pairs):
        cols = slice(pair * LANES, (pair + 1) * LANES)
        s = lax.dot_general(both(1, pair), q[:, cols], NT, preferred_element_type=F32) * scale
        probs = []
        for i in range(2):
            t = s[i * count : (i + 1) * count]
            w = jnp.exp2(t - jnp.max(t, axis=0, keepdims=True))
            probs.append(w / jnp.sum(w, axis=0, keepdims=True))
        w = jnp.concatenate(probs, axis=0).astype(BF16)
        out[:, cols] = lax.dot_general(w, both(2, pair), TN, preferred_element_type=F32).astype(BF16)


def short_body(vq, vk, vv, cq, ak, av, aq, ck, cv, ai, gain, up, down):
    n = lax.axis_size("seq")
    tokens = vq.shape[0]
    rows, columns = aq.shape
    features = ai.shape[1]
    heads = vq.shape[1] // n // VHEAD
    widths = [c * VHEAD for c in (1, 1, heads - 2)]
    video = (vq, vk, vv)

    def send(own, *first):
        return [own[0]] + [trade(after(own[s], *first), s) for s in range(1, n)]

    wait = 16 * MIB
    packed = pack(video, (aq, ak, av, ai), (), n, 0, widths[:1], 60, 6 * vq.size)
    chunk_0 = send(packed)
    packed = pack(video, (), (packed[0], ck, cv), n, widths[0], widths[1:], 16, wait)
    *packed, chunk_0[0], ck, cv = packed
    chunk_1 = send(packed[:n])
    (share,) = call(
        functools.partial(listen_kernel, n, tokens, rows),
        (*chunk_0[::-1], ck, cv),
        [sds((n * rows, columns + LANES))],
        moved=4 * vq.size,
        limit=16,
    )
    order = n // 2
    while order > 2:
        (share,) = call(
            functools.partial(merge_kernel, n, order),
            (share, trade(share, order)),
            [sds(share.shape)],
            limit=16,
        )
        order //= 2
    shares = [share, trade(share, 2)] if n > 2 else [share]
    first = call(
        functools.partial(first_kernel, n, tokens),
        (after(chunk_0[0], share), *chunk_0[1:]),
        [sds((tokens, widths[0]))] * n,
        limit=16,
    )
    built = middle(chunk_1, first, packed[n:], n, MIB)
    below = append(n, (0, 2), built[1], shares)
    chunk_2 = [built[0], trade(below, 1)]
    chunk_2 += [trade(built[s], s) for s in range(2, n)]
    (heard,) = call(
        functools.partial(heard_kernel, n, tokens, rows),
        (cq, *chunk_0),
        [sds(cq.shape)],
        moved=1 * MIB,
        limit=16,
    )
    gain = after(gain.reshape(1, -1), heard)
    own_sum, sent_sum, seen = combine((below, chunk_2[1]), built[1].shape[0], chunk_0, gain, up, tokens, rows, 512)
    other_sum = lax.ppermute(sent_sum, "tp", [(0, 1), (1, 0)])
    results = finish(own_sum, other_sum, down, n, rows, features, 512)
    ends = call(
        functools.partial(last_kernel, n, tokens),
        (*chunk_2, *results),
        [sds((tokens + rows * columns // widths[2], widths[2]))] * n,
        limit=16,
    )
    ends = [ends[0]] + [trade(ends[s], s) for s in range(1, n)]
    mixed, mlp = unpack(chunk_2, ends, results[0], n, heads, tokens)
    return mixed, heard, seen, mlp


def fits(vq, cq, aq, up, down):
    n = lax.axis_size("seq")
    heads = vq.shape[1] // VHEAD
    return (
        n in (2, 4, 8)
        and lax.axis_size("tp") == 2
        and heads % n == 0
        and heads // n == 4
        and vq.shape[0] == LANES
        and n * vq.shape[0] <= 1024
        and aq.shape[0] % 8 == 0
        and n * aq.shape[0] <= 64
        and 6 * (aq.shape[1] // CHEAD) < LANES
        and aq.shape[1] % VHEAD == 0
        and up.shape[1] % 512 == 0
        and down.shape[1] % 512 == 0
    )


def body(*args):
    *arrays, gain, up, down = args
    arrays = [a[0] for a in arrays]
    path = short_body if fits(arrays[0], arrays[3], arrays[6], up, down) else general_body
    return tuple(out[None] for out in path(*arrays, gain, up, down))


def solution(mesh):
    rows = P(("clips", "dp"), "seq", "tp")
    placed = (rows,) * 9 + (P(("clips", "dp"), "seq", None), P(), P("tp", "seq"), P("seq", "tp"))
    return jax.shard_map(
        body, mesh=mesh, in_specs=placed, out_specs=(rows,) * 4, check_vma=False
    )
```

```python
import functools
import math

import jax
import jax.numpy as jnp
from jax import lax
from jax.experimental import pallas as pl
from jax.experimental.pallas import tpu as pltpu
from jax.sharding import PartitionSpec as P

VHEAD = 128
CHEAD = 64
LANES = 128
F32 = jnp.float32
BF16 = jnp.bfloat16
LOG2E = math.log2(math.e)
MIB = 1024 * 1024
NT = (((1,), (1,)), ((), ()))
TN = (((0,), (0,)), ((), ()))


def attend_rows(queries, keys_in, values_in, head_count):
    head_size = queries.shape[1] // head_count
    query_heads = queries.reshape(queries.shape[0], head_count, head_size)
    key_heads = keys_in.reshape(keys_in.shape[0], head_count, head_size)
    value_heads = values_in.reshape(values_in.shape[0], head_count, head_size)
    scores = jnp.einsum(
        "qhd,khd->qhk", query_heads, key_heads, preferred_element_type=jnp.float32
    ) / math.sqrt(head_size)
    peak_value = jnp.max(scores, axis=2, keepdims=True)
    weights = jnp.exp(scores - peak_value)
    totals = jnp.sum(weights, axis=2)
    weighted = jnp.einsum(
        "qhk,khd->qhd",
        weights.astype(jnp.bfloat16),
        value_heads,
        preferred_element_type=jnp.float32,
    )
    result = weighted / totals[:, :, None]
    return result.reshape(queries.shape[0], head_count * head_size).astype(jnp.bfloat16)


def attend(queries, keys_in, values_in, head_count):
    row_total = queries.shape[0]
    block_rows = 512 if row_total % 512 == 0 else row_total
    pieces = queries.reshape(row_total // block_rows, block_rows, queries.shape[1])
    result = lax.map(
        lambda row_piece: attend_rows(row_piece, keys_in, values_in, head_count), pieces
    )
    return result.reshape(row_total, queries.shape[1])


def video_self(queries, keys_in, values_in):
    seq_count = lax.axis_size("seq")
    local_heads = queries.shape[1] // VHEAD
    dest_heads = max(local_heads // seq_count, 1)
    blocks = seq_count * dest_heads // local_heads
    groups = local_heads // dest_heads
    group_width = dest_heads * VHEAD
    token_count = queries.shape[0]
    block_tokens = token_count // blocks

    def spread(tensor):
        shaped = tensor.reshape(token_count, groups, group_width).transpose(1, 0, 2)
        shaped = jnp.broadcast_to(shaped[:, None], (groups, blocks, token_count, group_width))
        return shaped.reshape(seq_count, token_count, group_width)

    shaped = queries.reshape(blocks, block_tokens, groups, group_width).transpose(2, 0, 1, 3)
    own_queries = lax.all_to_all(
        shaped.reshape(seq_count, block_tokens, group_width),
        "seq",
        split_axis=0,
        concat_axis=0,
        tiled=True,
    )
    keys_all = lax.all_to_all(spread(keys_in), "seq", split_axis=0, concat_axis=0, tiled=True)
    values_all = lax.all_to_all(spread(values_in), "seq", split_axis=0, concat_axis=0, tiled=True)
    keys_all = keys_all.reshape(-1, group_width)
    values_all = values_all.reshape(-1, group_width)
    own_queries = own_queries.reshape(-1, group_width)
    attended = attend(own_queries, keys_all, values_all, dest_heads)
    returned = lax.all_to_all(
        attended.reshape(seq_count, block_tokens, group_width),
        "seq",
        split_axis=0,
        concat_axis=0,
        tiled=True,
    )
    returned = returned.reshape(groups, blocks, block_tokens, group_width).transpose(1, 2, 0, 3)
    return returned.reshape(token_count, groups * group_width)


def audio_listen(queries, keys_in, values_in, head_count):
    head_size = queries.shape[1] // head_count
    query_heads = queries.reshape(queries.shape[0], head_count, head_size)
    key_heads = keys_in.reshape(keys_in.shape[0], head_count, head_size)
    value_heads = values_in.reshape(values_in.shape[0], head_count, head_size)
    scores = jnp.einsum(
        "qhd,khd->qhk", query_heads, key_heads, preferred_element_type=jnp.float32
    ) / math.sqrt(head_size)
    local_peak = jnp.max(scores, axis=2)
    peak_value = lax.pmax(local_peak, "seq")
    weights = jnp.exp(scores - peak_value[:, :, None])
    totals = jnp.sum(weights, axis=2)
    weighted = jnp.einsum(
        "qhk,khd->qhd",
        weights.astype(jnp.bfloat16),
        value_heads,
        preferred_element_type=jnp.float32,
    )
    weighted = weighted.reshape(queries.shape[0], head_count * head_size)
    totals = lax.psum_scatter(totals, "seq", scatter_dimension=0, tiled=True)
    weighted = lax.psum_scatter(weighted, "seq", scatter_dimension=0, tiled=True)
    return (weighted / jnp.repeat(totals, head_size, axis=1)).astype(jnp.bfloat16)


def audio_block(audio_rows, audio_seen, norm_gain, up_weight, down_weight):
    features = lax.all_gather(audio_seen, "tp", axis=1, tiled=True)
    residual = audio_rows.astype(jnp.float32) + features.astype(jnp.float32)
    scale_factor = lax.rsqrt(jnp.mean(residual * residual, axis=1, keepdims=True) + 1e-06)
    normed = (residual * scale_factor * norm_gain).astype(jnp.bfloat16)
    slice_width = up_weight.shape[0]
    own_features = lax.dynamic_slice_in_dim(
        normed, lax.axis_index("tp") * slice_width, slice_width, 1
    )
    partial_sum = jnp.dot(
        lax.all_gather(own_features, "seq", axis=0, tiled=True),
        up_weight,
        preferred_element_type=jnp.float32,
    )
    hidden = jax.nn.gelu(lax.psum(partial_sum, "tp")).astype(jnp.bfloat16)
    return lax.psum_scatter(
        jnp.dot(hidden, down_weight, preferred_element_type=jnp.float32),
        "seq",
        scatter_dimension=0,
        tiled=True,
    ).astype(jnp.bfloat16)


def general_body(vq, vk, vv, cq, ak, av, aq, ck, cv, ai, gain, up, down):
    cross_heads = cq.shape[1] // CHEAD
    mixed = video_self(vq, vk, vv)
    gathered_query = lax.all_gather(aq, "seq", axis=0, tiled=True)
    gathered_key = lax.all_gather(ak, "seq", axis=0, tiled=True)
    gathered_value = lax.all_gather(av, "seq", axis=0, tiled=True)
    heard = attend(cq, gathered_key, gathered_value, cross_heads)
    seen = audio_listen(gathered_query, ck, cv, cross_heads)
    mlp = audio_block(ai, seen, gain, up, down)
    return mixed, heard, seen, mlp


def whole():
    return pl.BlockSpec()


def after(value, *others):
    return lax.optimization_barrier((value, *others))[0]


def sds(shape, dtype=BF16):
    return jax.ShapeDtypeStruct(shape, dtype)


def call(kernel, ins, outs, flops=0, moved=0, limit=32):
    return pl.pallas_call(
        kernel,
        out_shape=tuple(outs),
        in_specs=[whole()] * len(ins),
        out_specs=tuple(whole() for _ in outs),
        compiler_params=pltpu.CompilerParams(vmem_limit_bytes=limit * MIB),
        cost_estimate=pl.CostEstimate(flops=flops, bytes_accessed=moved, transcendentals=0),
    )(*ins)


def trade(value, by):
    n = lax.axis_size("seq")
    return lax.ppermute(value, "seq", [(i, i ^ by) for i in range(n)])


def parts3(value):
    first = value.astype(BF16).astype(F32)
    second = (value - first).astype(BF16).astype(F32)
    return first, second, value - first - second


def pack_kernel(n, first, widths, audio_count, kept, staged, columns, q, k, v, *refs):
    count = n * len(widths)
    audio, refs = refs[:audio_count], refs[audio_count:]
    keep, refs = refs[:kept], refs[kept:]
    outs, passed, refs = refs[:count], refs[count : count + kept], refs[count + kept :]
    built = refs[:count] if staged else outs
    lines, sem, audio_sem, out_sem = refs[-3 - audio_count : -3], refs[-3], refs[-2], refs[-1]
    me = lax.axis_index("seq")
    tokens = q.shape[0]
    group = q.shape[1] // n
    fetches = [pltpu.make_async_copy(ref, to, audio_sem.at[i]) for i, (ref, to) in enumerate(zip(audio, lines))]
    for copy in fetches:
        copy.start()
    copies, arrivals = [], []
    for c, width in enumerate(widths):
        for s in range(n):
            at = pl.ds(pl.multiple_of(lax.bitwise_xor(me, s) * group + first, LANES), width)
            for i, ref in enumerate((q, k, v)):
                to = built[c * n + s].at[pl.ds(i * tokens, tokens), :]
                arrivals.append(pltpu.make_async_copy(ref.at[:, at], to, sem.at[len(arrivals)]))
                arrivals[-1].start()
        first += width
    for i, (ref, to) in enumerate(zip(keep, passed)):
        copies.append(pltpu.make_async_copy(ref, to, out_sem.at[count + i]))
        copies[-1].start()
    if audio:
        for copy in fetches:
            copy.wait()
        parts = []
        for ref in lines:
            mine = slice(None)
            if ref.shape[1] > columns:
                mine = pl.ds(pl.multiple_of(lax.axis_index("tp") * columns, LANES), columns)
            parts.append(ref[:, mine].astype(F32))
        blocks = [part[:, c : c + widths[0]] for part in parts for c in range(0, columns, widths[0])]
        extra = jnp.concatenate(blocks, axis=0).astype(BF16)
        for s in range(n):
            if built[s].shape[0] > 3 * tokens:
                built[s][3 * tokens :, :] = extra
    for i in range(count):
        for copy in arrivals[3 * i : 3 * i + 3]:
            copy.wait()
        if staged:
            copies.append(pltpu.make_async_copy(built[i], outs[i], out_sem.at[i]))
            copies[-1].start()
    for copy in copies:
        copy.wait()


def pack(video, audio, spots, keep, n, first, widths, limit, moved, staged):
    columns = audio[0].shape[1] if audio else 0
    lines = audio[0].size // widths[0] if audio else 0
    tokens = video[0].shape[0]
    extra = len(audio) * lines
    shapes = [(3 * tokens + (extra if s in spots else 0), w) for w in widths for s in range(n)]
    stay = pl.BlockSpec(memory_space=pl.ANY)
    dma = pltpu.SemaphoreType.DMA
    return pl.pallas_call(
        functools.partial(pack_kernel, n, first, widths, len(audio), len(keep), staged, columns),
        out_shape=tuple(sds(x) for x in shapes) + tuple(sds(x.shape) for x in keep),
        in_specs=[stay] * (3 + len(audio) + len(keep)),
        out_specs=(stay if staged else whole(),) * (len(shapes) + len(keep)),
        scratch_shapes=[pltpu.VMEM(x, BF16) for x in shapes if staged]
        + [pltpu.VMEM(x.shape, BF16) for x in audio]
        + [dma((3 * len(shapes),)), dma((max(len(audio), 1),)), dma((len(shapes) + len(keep),))],
        compiler_params=pltpu.CompilerParams(vmem_limit_bytes=limit * MIB),
        cost_estimate=pl.CostEstimate(flops=0, bytes_accessed=moved, transcendentals=0),
    )(*video, *audio, *keep)


def audio_rows(tails, part, pair, rows, pairs):
    per = tails[0].shape[1] // LANES
    at, side = (part * pairs + pair) // per * rows, pair % per * LANES
    return jnp.concatenate([t[at : at + rows, side : side + LANES] for t in tails], axis=0)


def attend_heads(pieces, tokens, put):
    scale = LOG2E / math.sqrt(VHEAD)
    for h in range(pieces[0].shape[1] // VHEAD):
        cols = slice(h * VHEAD, (h + 1) * VHEAD)
        keys = jnp.concatenate([p[tokens : 2 * tokens, cols] for p in pieces], axis=0)
        values = jnp.concatenate([p[2 * tokens : 3 * tokens, cols] for p in pieces], axis=0)
        values = jnp.concatenate([values, jnp.ones_like(values)], axis=1)
        for s, p in enumerate(pieces):
            t = lax.dot_general(p[0:tokens, cols], keys, NT, preferred_element_type=F32)
            w = jnp.exp2((t - jnp.max(t, axis=1, keepdims=True)) * scale)
            o = jnp.dot(w.astype(BF16), values, preferred_element_type=F32)
            put(s, h, (o[:, :VHEAD] / o[:, VHEAD:]).astype(BF16))


def first_kernel(n, tokens, *refs):
    pieces, outs = refs[:n], refs[n:]

    def put(s, h, rows):
        outs[s][:, h * VHEAD : (h + 1) * VHEAD] = rows

    attend_heads(pieces, tokens, put)


def middle_kernel(n, *refs):
    pieces, before, last = refs[:n], refs[n : 2 * n], refs[2 * n : 3 * n]
    outs, sem = refs[3 * n : -1], refs[-1]
    tokens = last[0].shape[0] // 3
    early, width = before[0].shape[1], outs[0].shape[1]
    copies = []
    for s in range(n):
        top, below = pl.ds(0, 3 * tokens), pl.ds(3 * tokens, tokens)
        copies.append(pltpu.make_async_copy(last[s], outs[s].at[top, :], sem.at[2 * s]))
        to = outs[s].at[below, pl.ds(0, early)]
        copies.append(pltpu.make_async_copy(before[s], to, sem.at[2 * s + 1]))
    for copy in copies:
        copy.start()

    def put(s, h, rows):
        at = early + h * VHEAD
        low, side = (3 + at // width) * tokens, at % width
        outs[s][low : low + tokens, side : side + VHEAD] = rows

    attend_heads(pieces, tokens, put)
    for copy in copies:
        copy.wait()


def middle(chunk, before, last, n, moved):
    tokens = last[0].shape[0] // 3
    width = last[0].shape[1]
    tall = tokens * (3 + (before[0].shape[1] + chunk[0].shape[1]) // width)
    stay = pl.BlockSpec(memory_space=pl.ANY)
    return pl.pallas_call(
        functools.partial(middle_kernel, n),
        out_shape=(sds((tall, width)),) * n,
        in_specs=[whole()] * n + [stay] * (2 * n),
        out_specs=(whole(),) * n,
        scratch_shapes=[pltpu.SemaphoreType.DMA((2 * n,))],
        compiler_params=pltpu.CompilerParams(vmem_limit_bytes=16 * MIB),
        cost_estimate=pl.CostEstimate(flops=0, bytes_accessed=moved, transcendentals=0),
    )(*chunk, *before, *last)


def last_kernel(n, tokens, *refs):
    pieces, sums, outs = refs[:n], refs[n : 2 * n], refs[2 * n :]
    width = outs[0].shape[1]

    def put(s, h, rows):
        outs[s][:tokens, h * VHEAD : (h + 1) * VHEAD] = rows

    for s in range(n):
        part = sums[s][...].astype(F32)
        blocks = [part[:, c : c + width] for c in range(0, part.shape[1], width)]
        outs[s][tokens:, :] = jnp.concatenate(blocks, axis=0).astype(BF16)
    attend_heads(pieces, tokens, put)


def unpack_kernel(n, heads, tokens, *refs):
    middles, lasts, own = refs[:n], refs[n : 2 * n][::-1], refs[2 * n]
    out, mlp, line, sem = refs[2 * n + 1 :]
    me = lax.axis_index("seq")
    width = lasts[0].shape[1]
    group = heads * VHEAD
    copies = []

    def start(source, owner, first, size):
        at = pl.ds(pl.multiple_of(owner * group + first, LANES), size)
        copies.append(pltpu.make_async_copy(source, out.at[:, at], sem.at[len(copies)]))
        copies[-1].start()

    early = group - width
    for s in range(n):
        for c in range(0, early, width):
            rows = pl.ds(3 * tokens + c // width * tokens, tokens)
            size = min(width, early - c)
            start(middles[s].at[rows, pl.ds(0, size)], lax.bitwise_xor(me, s), c, size)
        start(lasts[s].at[pl.ds(0, tokens), :], lax.bitwise_xor(me, s), early, width)
    rows, columns = own.shape
    tails = [lasts[s][tokens:, :].astype(F32) for s in range(1, n)]
    for c in range(columns // width):
        total = own[:, c * width : (c + 1) * width]
        for tail in tails:
            total = total + tail[c * rows : (c + 1) * rows]
        line[:, c * width : (c + 1) * width] = total.astype(BF16)
    copies.append(pltpu.make_async_copy(line, mlp, sem.at[len(copies)]))
    copies[-1].start()
    for copy in copies:
        copy.wait()


def unpack(middles, lasts, own, n, heads, tokens):
    count = n * (-(-(heads * VHEAD - lasts[0].shape[1]) // lasts[0].shape[1]) + 1)
    return pl.pallas_call(
        functools.partial(unpack_kernel, n, heads, tokens),
        out_shape=(sds((tokens, n * heads * VHEAD)), sds(own.shape)),
        in_specs=[pl.BlockSpec(memory_space=pltpu.VMEM)] * (2 * n + 1),
        out_specs=(pl.BlockSpec(memory_space=pl.ANY),) * 2,
        scratch_shapes=[pltpu.VMEM(own.shape, BF16), pltpu.SemaphoreType.DMA((count + 1,))],
        compiler_params=pltpu.CompilerParams(vmem_limit_bytes=16 * MIB),
    )(*middles, *lasts[::-1], own)


def low_half(shape):
    return lax.broadcasted_iota(jnp.int32, shape, 1) < CHEAD


def listen_kernel(n, tokens, rows, *refs):
    pieces, keys, values, out = refs[:n][::-1], refs[n], refs[n + 1], refs[n + 2]
    columns = keys.shape[1]
    pairs = columns // LANES
    tails = [p[3 * tokens :, :].astype(F32) for p in pieces]
    count = n * rows
    scale = LOG2E / math.sqrt(CHEAD)
    low = low_half((count, LANES))
    lane = lax.broadcasted_iota(jnp.int32, (count, LANES), 1)
    peaks = jnp.zeros((count, LANES), F32)
    totals = jnp.zeros((count, LANES), F32)
    heads = columns // CHEAD
    for pair in range(pairs):
        cols = slice(pair * LANES, (pair + 1) * LANES)
        qp = audio_rows(tails, 0, pair, rows, pairs)
        both = jnp.concatenate([jnp.where(low, qp, 0.0), jnp.where(low, 0.0, qp)], axis=0)
        s = lax.dot_general(both.astype(BF16), keys[:, cols], NT, preferred_element_type=F32)
        s = s * scale
        peak = jnp.max(s, axis=1, keepdims=True)
        w = jnp.exp2(s - peak)
        wide = jnp.concatenate([values[:, cols], jnp.ones_like(values[:, cols])], axis=1)
        o = jnp.dot(w.astype(BF16), wide, preferred_element_type=F32)
        o, total = o[:, :LANES] / o[:, LANES:], o[:, LANES:]
        out[:, cols] = jnp.where(low, o[:count], o[count:]).astype(BF16)
        for i in range(2):
            head = lane == 2 * pair + i
            peaks = jnp.where(head, peak[i * count : (i + 1) * count], peaks)
            totals = jnp.where(head, total[i * count : (i + 1) * count], totals)
    out[:, columns:] = share_stats(peaks[:, :heads], totals[:, :heads])


def read_shares(wholes, columns):
    heads = columns // CHEAD
    peaks, totals, parts = [], [], []
    for whole in wholes:
        parts.append(whole[:, :columns])
        piece = [whole[:, columns + j * heads : columns + (j + 1) * heads] for j in range(6)]
        peaks.append(piece[0] + piece[1] + piece[2])
        totals.append(piece[3] + piece[4] + piece[5])
    top = functools.reduce(jnp.maximum, peaks)
    weight = [t * jnp.exp2(p - top) for t, p in zip(totals, peaks)]
    every = functools.reduce(jnp.add, weight)
    return parts, [w / every for w in weight], top, every


def reorder(whole, order, n):
    rows = whole.shape[0] // n
    return jnp.concatenate([whole[(i ^ order) * rows :][:rows] for i in range(n)], axis=0)


def joint(parts, weight, pair):
    low = low_half((parts[0].shape[0], LANES))
    o = jnp.zeros(low.shape, F32)
    for w, part in zip(weight, parts):
        a, b = w[:, 2 * pair : 2 * pair + 1], w[:, 2 * pair + 1 : 2 * pair + 2]
        o = o + jnp.where(low, a, b) * part[:, pair * LANES : (pair + 1) * LANES]
    return o.astype(BF16)


def share_stats(peaks, totals):
    stats = jnp.concatenate(parts3(peaks) + parts3(totals), axis=1)
    rest = jnp.zeros((stats.shape[0], LANES - stats.shape[1]), F32)
    return jnp.concatenate([stats, rest], axis=1).astype(BF16)


def merge_kernel(n, order, tokens, own, other, mine, second, out):
    count, columns = own.shape[0], own.shape[1] - LANES
    wholes = own[...].astype(F32), reorder(other[...].astype(F32), order, n)
    parts, weight, top, every = read_shares(wholes, columns)
    for pair in range(columns // LANES):
        out[:, pair * LANES : (pair + 1) * LANES] = joint(parts, weight, pair)
    out[:, columns : columns + LANES] = share_stats(top, every)
    at = columns + LANES
    for ref in (mine, second):
        for row in range(3 * tokens, ref.shape[0], count):
            out[:, at : at + LANES] = ref[row : row + count, :]
            at += LANES


def combine_kernel(n, tokens, rows, *refs):
    got, pieces, (gain, up) = refs[:2], refs[2 : 2 + n], refs[2 + n : 4 + n]
    own_sum, sent_sum, seen, x_ref = refs[4 + n :]

    @pl.when(pl.program_id(0) == 0)
    def _():
        columns = seen.shape[1]
        wholes = []
        for ref, order in zip(got, (0, 1)):
            wholes.append(reorder(ref[:, : columns + LANES].astype(F32), order, n))
        parts, weight, _, _ = read_shares(wholes, columns)
        tails = [p[3 * tokens :, :].astype(F32) for p in pieces]
        square = jnp.zeros((n * rows, 1), F32)
        for pair in range(columns // LANES):
            cols = slice(pair * LANES, (pair + 1) * LANES)
            o = joint(parts, weight, pair)
            seen[:, cols] = o[:rows]
            residual = audio_rows(tails, 1, pair, rows, columns // LANES) + o.astype(F32)
            square = square + jnp.sum(residual * residual, axis=1, keepdims=True)
            at = pl.ds(pl.multiple_of(lax.axis_index("tp") * columns + pair * LANES, LANES), LANES)
            x_ref[:, cols] = (residual * gain[:, at]).astype(BF16)
        lane = lax.broadcasted_iota(jnp.int32, (n * rows, LANES), 1)
        first, second, third = parts3(square)
        spread = jnp.where(lane == 0, first, jnp.where(lane == 1, second, third))
        spread = jnp.where(lane < 3, spread, 0.0)
        own_sum[0, :, :LANES] = spread
        sent_sum[0, :, :LANES] = spread.astype(BF16)

    @pl.when(pl.program_id(0) > 0)
    def _():
        product = jnp.dot(x_ref[...], up[...], preferred_element_type=F32)
        own_sum[0] = product
        sent_sum[0] = product.astype(BF16)


def combine(got, pieces, gain, up, tokens, rows, block):
    n = len(pieces)
    columns, units = up.shape
    steps = units // block + 1
    held = lambda ref: pl.BlockSpec(ref.shape, lambda i: (0,) * ref.ndim)
    moved = pl.BlockSpec((1, n * rows, block), lambda i: (i, 0, 0))
    return pl.pallas_call(
        functools.partial(combine_kernel, n, tokens, rows),
        grid=(steps,),
        out_shape=(
            sds((steps, n * rows, block), F32),
            sds((steps, n * rows, block)),
            sds((rows, columns)),
        ),
        in_specs=[held(r) for r in (*got, *pieces, gain)]
        + [pl.BlockSpec((columns, block), lambda i: (0, jnp.maximum(i - 1, 0)))],
        out_specs=(moved, moved, pl.BlockSpec((rows, columns), lambda i: (0, 0))),
        scratch_shapes=[pltpu.VMEM((n * rows, columns), BF16)],
        compiler_params=pltpu.CompilerParams(vmem_limit_bytes=32 * MIB),
        cost_estimate=pl.CostEstimate(
            flops=0, bytes_accessed=0 * MIB, transcendentals=0
        ),
    )(*got, *pieces, gain, up)


def finish_kernel(n, features, own, other, down, *refs):
    outs, hidden = refs[:n], refs[n]
    rows = outs[0].shape[0]

    @pl.when(pl.program_id(0) == 0)
    def _():
        square = own[0, :, :LANES] + other[0, :, :LANES].astype(F32)
        square = jnp.sum(square, axis=1, keepdims=True)
        scale = lax.rsqrt(square / features + 1e-6)
        block = own.shape[2]
        for i in range(1, own.shape[0]):
            total = (own[i] + other[i].astype(F32)) * scale
            hidden[:, (i - 1) * block : i * block] = jax.nn.gelu(total).astype(BF16)

    product = jnp.dot(hidden[...], down[...], preferred_element_type=F32)
    for s in range(n):
        outs[s][...] = product[s * rows : (s + 1) * rows].astype(outs[s].dtype)


def finish(own, other, down, n, rows, features, block):
    units, columns = down.shape
    held = lambda ref: pl.BlockSpec(ref.shape, lambda i: (0,) * ref.ndim)
    return pl.pallas_call(
        functools.partial(finish_kernel, n, features),
        grid=(columns // block,),
        out_shape=(sds((rows, columns), F32),) + (sds((rows, columns)),) * (n - 1),
        in_specs=[held(own), held(other), pl.BlockSpec((units, block), lambda i: (0, i))],
        out_specs=(pl.BlockSpec((rows, block), lambda i: (0, i)),) * n,
        scratch_shapes=[pltpu.VMEM((n * rows, units), BF16)],
        compiler_params=pltpu.CompilerParams(vmem_limit_bytes=32 * MIB),
        cost_estimate=pl.CostEstimate(
            flops=0, bytes_accessed=0 * MIB, transcendentals=0
        ),
    )(own, other, down)


def heard_kernel(n, tokens, rows, q, own, second, first, out):
    pairs = q.shape[1] // LANES
    at = first.shape[1] - 2 * (own.shape[0] - 3 * tokens) // first.shape[0] * LANES
    half = (first.shape[1] - at) // 2
    far = [
        jnp.concatenate([first[:, c : c + LANES] for c in range(start, start + half, LANES)], axis=0)
        for start in (at, at + half)
    ]
    tails = [own[3 * tokens :, :], far[0], second[3 * tokens :, :], far[1]]
    tails = [tail.astype(F32) for tail in tails]
    count = n * rows
    low = low_half((count, LANES))
    scale = LOG2E / math.sqrt(CHEAD)

    def both(part, pair):
        x = audio_rows(tails, part, pair, rows, pairs)
        return jnp.concatenate([jnp.where(low, x, 0.0), jnp.where(low, 0.0, x)], axis=0).astype(BF16)

    for pair in range(pairs):
        cols = slice(pair * LANES, (pair + 1) * LANES)
        s = lax.dot_general(both(0, pair), q[:, cols], NT, preferred_element_type=F32) * scale
        probs = []
        for i in range(2):
            t = s[i * count : (i + 1) * count]
            w = jnp.exp2(t - jnp.max(t, axis=0, keepdims=True))
            probs.append(w / jnp.sum(w, axis=0, keepdims=True))
        w = jnp.concatenate(probs, axis=0).astype(BF16)
        out[:, cols] = lax.dot_general(w, both(1, pair), TN, preferred_element_type=F32).astype(BF16)


def short_body(vq, vk, vv, cq, ak, av, aq, ck, cv, ai, gain, up, down):
    n = lax.axis_size("seq")
    tokens = vq.shape[0]
    rows, columns = aq.shape
    features = ai.shape[1]
    heads = vq.shape[1] // n // VHEAD
    widths = [c * VHEAD for c in (1, 1, heads - 2)]
    video = (vq, vk, vv)

    def send(own, *first):
        return [own[0]] + [trade(after(own[s], *first), s) for s in range(1, n)]

    wait = 16 * MIB
    packed = pack(video, (aq, ai), range(n), (), n, 0, widths[:1], 60, 6 * vq.size, True)
    chunk_0 = send(packed)
    packed = pack(video, (ak, av), (0, 2), (), n, widths[0], widths[1:2], 60, wait, True)
    chunk_1 = send(packed)
    keep = (chunk_0[0], chunk_1[0], ck, cv)
    packed = pack(video, (), (), keep, n, widths[0] + widths[1], widths[2:], 16, wait, False)
    *packed, chunk_0[0], chunk_1[0], ck, cv = packed
    (share,) = call(
        functools.partial(listen_kernel, n, tokens, rows),
        (*chunk_0[::-1], ck, cv),
        [sds((n * rows, columns + LANES))],
        moved=4 * vq.size,
        limit=16,
    )
    order = n // 2
    while order > 2:
        (share,) = call(
            functools.partial(merge_kernel, n, order),
            (share, trade(share, order)),
            [sds(share.shape)],
            limit=16,
        )
        order //= 2
    shares = [share, trade(share, 2)] if n > 2 else [share]
    first = call(
        functools.partial(first_kernel, n, tokens),
        (after(chunk_0[0], share), *chunk_0[1:]),
        [sds((tokens, widths[0]))] * n,
        limit=16,
    )
    built = middle(chunk_1, first, packed, n, MIB)
    wide = share.shape[1] + 4 * rows * columns // share.shape[0]
    (share,) = call(
        functools.partial(merge_kernel, n, 2, tokens),
        (after(shares[0], built[0]), shares[1], chunk_1[0], chunk_1[2]),
        [sds((share.shape[0], wide))],
        limit=16,
    )
    below = trade(share, 1)
    chunk_2 = [built[0]] + [trade(after(built[s], below), s) for s in range(1, 2)]
    chunk_2 += [trade(after(built[s], share), s) for s in range(2, n)]
    (heard,) = call(
        functools.partial(heard_kernel, n, tokens, rows),
        (cq, chunk_1[0], chunk_1[2], below),
        [sds(cq.shape)],
        moved=0,
        limit=16,
    )
    gain = after(gain.reshape(1, -1), heard)
    own_sum, sent_sum, seen = combine((share, below), chunk_0, gain, up, tokens, rows, 512)
    other_sum = lax.ppermute(sent_sum, "tp", [(0, 1), (1, 0)])
    results = finish(own_sum, other_sum, down, n, rows, features, 512)
    ends = call(
        functools.partial(last_kernel, n, tokens),
        (*chunk_2, *results),
        [sds((tokens + rows * columns // widths[2], widths[2]))] * n,
        limit=16,
    )
    ends = [ends[0]] + [trade(ends[s], s) for s in range(1, n)]
    mixed, mlp = unpack(chunk_2, ends, results[0], n, heads, tokens)
    return mixed, heard, seen, mlp


def fits(vq, cq, aq, up, down):
    n = lax.axis_size("seq")
    heads = vq.shape[1] // VHEAD
    return (
        n == 4
        and lax.axis_size("tp") == 2
        and heads % n == 0
        and heads // n == 4
        and vq.shape[0] == LANES
        and n * vq.shape[0] <= 1024
        and aq.shape[0] % 8 == 0
        and n * aq.shape[0] <= 64
        and 6 * (aq.shape[1] // CHEAD) < LANES
        and aq.shape[1] % VHEAD == 0
        and up.shape[1] % 512 == 0
        and down.shape[1] % 512 == 0
    )


def body(*args):
    *arrays, gain, up, down = args
    arrays = [a[0] for a in arrays]
    path = short_body if fits(arrays[0], arrays[3], arrays[6], up, down) else general_body
    return tuple(out[None] for out in path(*arrays, gain, up, down))


def solution(mesh):
    rows = P(("clips", "dp"), "seq", "tp")
    placed = (rows,) * 9 + (P(("clips", "dp"), "seq", None), P(), P("tp", "seq"), P("seq", "tp"))
    return jax.shard_map(
        body, mesh=mesh, in_specs=placed, out_specs=(rows,) * 4, check_vma=False
    )
```

```python
import functools
import math

import jax
import jax.numpy as jnp
from jax import lax
from jax.experimental import pallas as pl
from jax.experimental.pallas import tpu as pltpu
from jax.sharding import PartitionSpec as P

VHEAD = 128
CHEAD = 64
LANES = 128
F32 = jnp.float32
BF16 = jnp.bfloat16
LOG2E = math.log2(math.e)
MIB = 1024 * 1024
NT = (((1,), (1,)), ((), ()))
TN = (((0,), (0,)), ((), ()))


def attend_rows(queries, keys_in, values_in, head_count):
    head_size = queries.shape[1] // head_count
    query_heads = queries.reshape(queries.shape[0], head_count, head_size)
    key_heads = keys_in.reshape(keys_in.shape[0], head_count, head_size)
    value_heads = values_in.reshape(values_in.shape[0], head_count, head_size)
    scores = jnp.einsum(
        "qhd,khd->qhk", query_heads, key_heads, preferred_element_type=jnp.float32
    ) / math.sqrt(head_size)
    peak_value = jnp.max(scores, axis=2, keepdims=True)
    weights = jnp.exp(scores - peak_value)
    totals = jnp.sum(weights, axis=2)
    weighted = jnp.einsum(
        "qhk,khd->qhd",
        weights.astype(jnp.bfloat16),
        value_heads,
        preferred_element_type=jnp.float32,
    )
    result = weighted / totals[:, :, None]
    return result.reshape(queries.shape[0], head_count * head_size).astype(jnp.bfloat16)


def attend(queries, keys_in, values_in, head_count):
    row_total = queries.shape[0]
    block_rows = 512 if row_total % 512 == 0 else row_total
    pieces = queries.reshape(row_total // block_rows, block_rows, queries.shape[1])
    result = lax.map(
        lambda row_piece: attend_rows(row_piece, keys_in, values_in, head_count), pieces
    )
    return result.reshape(row_total, queries.shape[1])


def video_self(queries, keys_in, values_in):
    seq_count = lax.axis_size("seq")
    local_heads = queries.shape[1] // VHEAD
    dest_heads = max(local_heads // seq_count, 1)
    blocks = seq_count * dest_heads // local_heads
    groups = local_heads // dest_heads
    group_width = dest_heads * VHEAD
    token_count = queries.shape[0]
    block_tokens = token_count // blocks

    def spread(tensor):
        shaped = tensor.reshape(token_count, groups, group_width).transpose(1, 0, 2)
        shaped = jnp.broadcast_to(shaped[:, None], (groups, blocks, token_count, group_width))
        return shaped.reshape(seq_count, token_count, group_width)

    shaped = queries.reshape(blocks, block_tokens, groups, group_width).transpose(2, 0, 1, 3)
    own_queries = lax.all_to_all(
        shaped.reshape(seq_count, block_tokens, group_width),
        "seq",
        split_axis=0,
        concat_axis=0,
        tiled=True,
    )
    keys_all = lax.all_to_all(spread(keys_in), "seq", split_axis=0, concat_axis=0, tiled=True)
    values_all = lax.all_to_all(spread(values_in), "seq", split_axis=0, concat_axis=0, tiled=True)
    keys_all = keys_all.reshape(-1, group_width)
    values_all = values_all.reshape(-1, group_width)
    own_queries = own_queries.reshape(-1, group_width)
    attended = attend(own_queries, keys_all, values_all, dest_heads)
    returned = lax.all_to_all(
        attended.reshape(seq_count, block_tokens, group_width),
        "seq",
        split_axis=0,
        concat_axis=0,
        tiled=True,
    )
    returned = returned.reshape(groups, blocks, block_tokens, group_width).transpose(1, 2, 0, 3)
    return returned.reshape(token_count, groups * group_width)


def audio_listen(queries, keys_in, values_in, head_count):
    head_size = queries.shape[1] // head_count
    query_heads = queries.reshape(queries.shape[0], head_count, head_size)
    key_heads = keys_in.reshape(keys_in.shape[0], head_count, head_size)
    value_heads = values_in.reshape(values_in.shape[0], head_count, head_size)
    scores = jnp.einsum(
        "qhd,khd->qhk", query_heads, key_heads, preferred_element_type=jnp.float32
    ) / math.sqrt(head_size)
    local_peak = jnp.max(scores, axis=2)
    peak_value = lax.pmax(local_peak, "seq")
    weights = jnp.exp(scores - peak_value[:, :, None])
    totals = jnp.sum(weights, axis=2)
    weighted = jnp.einsum(
        "qhk,khd->qhd",
        weights.astype(jnp.bfloat16),
        value_heads,
        preferred_element_type=jnp.float32,
    )
    weighted = weighted.reshape(queries.shape[0], head_count * head_size)
    totals = lax.psum_scatter(totals, "seq", scatter_dimension=0, tiled=True)
    weighted = lax.psum_scatter(weighted, "seq", scatter_dimension=0, tiled=True)
    return (weighted / jnp.repeat(totals, head_size, axis=1)).astype(jnp.bfloat16)


def audio_block(audio_rows, audio_seen, norm_gain, up_weight, down_weight):
    features = lax.all_gather(audio_seen, "tp", axis=1, tiled=True)
    residual = audio_rows.astype(jnp.float32) + features.astype(jnp.float32)
    scale_factor = lax.rsqrt(jnp.mean(residual * residual, axis=1, keepdims=True) + 1e-06)
    normed = (residual * scale_factor * norm_gain).astype(jnp.bfloat16)
    slice_width = up_weight.shape[0]
    own_features = lax.dynamic_slice_in_dim(
        normed, lax.axis_index("tp") * slice_width, slice_width, 1
    )
    partial_sum = jnp.dot(
        lax.all_gather(own_features, "seq", axis=0, tiled=True),
        up_weight,
        preferred_element_type=jnp.float32,
    )
    hidden = jax.nn.gelu(lax.psum(partial_sum, "tp")).astype(jnp.bfloat16)
    return lax.psum_scatter(
        jnp.dot(hidden, down_weight, preferred_element_type=jnp.float32),
        "seq",
        scatter_dimension=0,
        tiled=True,
    ).astype(jnp.bfloat16)


def general_body(vq, vk, vv, cq, ak, av, aq, ck, cv, ai, gain, up, down):
    cross_heads = cq.shape[1] // CHEAD
    mixed = video_self(vq, vk, vv)
    gathered_query = lax.all_gather(aq, "seq", axis=0, tiled=True)
    gathered_key = lax.all_gather(ak, "seq", axis=0, tiled=True)
    gathered_value = lax.all_gather(av, "seq", axis=0, tiled=True)
    heard = attend(cq, gathered_key, gathered_value, cross_heads)
    seen = audio_listen(gathered_query, ck, cv, cross_heads)
    mlp = audio_block(ai, seen, gain, up, down)
    return mixed, heard, seen, mlp


def whole():
    return pl.BlockSpec()


def after(value, *others):
    return lax.optimization_barrier((value, *others))[0]


def sds(shape, dtype=BF16):
    return jax.ShapeDtypeStruct(shape, dtype)


def call(kernel, ins, outs, flops=0, moved=0, limit=32):
    return pl.pallas_call(
        kernel,
        out_shape=tuple(outs),
        in_specs=[whole()] * len(ins),
        out_specs=tuple(whole() for _ in outs),
        compiler_params=pltpu.CompilerParams(vmem_limit_bytes=limit * MIB),
        cost_estimate=pl.CostEstimate(flops=flops, bytes_accessed=moved, transcendentals=0),
    )(*ins)


def trade(value, by):
    n = lax.axis_size("seq")
    return lax.ppermute(value, "seq", [(i, i ^ by) for i in range(n)])


def parts3(value):
    first = value.astype(BF16).astype(F32)
    second = (value - first).astype(BF16).astype(F32)
    return first, second, value - first - second


def pack_kernel(n, first, widths, audio_count, kept, staged, columns, q, k, v, *refs):
    count = n * len(widths)
    audio, refs = refs[:audio_count], refs[audio_count:]
    keep, refs = refs[:kept], refs[kept:]
    outs, passed, refs = refs[:count], refs[count : count + kept], refs[count + kept :]
    built = refs[:count] if staged else outs
    sem, out_sem = refs[-2], refs[-1]
    me = lax.axis_index("seq")
    tokens = q.shape[0]
    group = q.shape[1] // n
    copies, arrivals = [], []
    for c, width in enumerate(widths):
        for s in range(n):
            at = pl.ds(pl.multiple_of(lax.bitwise_xor(me, s) * group + first, LANES), width)
            for i, ref in enumerate((q, k, v)):
                to = built[c * n + s].at[pl.ds(i * tokens, tokens), :]
                arrivals.append(pltpu.make_async_copy(ref.at[:, at], to, sem.at[len(arrivals)]))
                arrivals[-1].start()
        first += width
    for i, (ref, to) in enumerate(zip(keep, passed)):
        copies.append(pltpu.make_async_copy(ref, to, out_sem.at[count + i]))
        copies[-1].start()
    if audio:
        parts = []
        for ref in audio:
            mine = slice(None)
            if ref.shape[1] > columns:
                mine = pl.ds(pl.multiple_of(lax.axis_index("tp") * columns, LANES), columns)
            parts.append(ref[:, mine].astype(F32))
        blocks = [part[:, c : c + widths[0]] for part in parts for c in range(0, columns, widths[0])]
        extra = jnp.concatenate(blocks, axis=0).astype(BF16)
        for s in range(n):
            if built[s].shape[0] > 3 * tokens:
                built[s][3 * tokens :, :] = extra
    for i in range(count):
        for copy in arrivals[3 * i : 3 * i + 3]:
            copy.wait()
        if staged:
            copies.append(pltpu.make_async_copy(built[i], outs[i], out_sem.at[i]))
            copies[-1].start()
    for copy in copies:
        copy.wait()


def pack(video, audio, spots, keep, n, first, widths, limit, moved, staged):
    columns = audio[0].shape[1] if audio else 0
    lines = audio[0].size // widths[0] if audio else 0
    tokens = video[0].shape[0]
    extra = len(audio) * lines
    shapes = [(3 * tokens + (extra if s in spots else 0), w) for w in widths for s in range(n)]
    stay = pl.BlockSpec(memory_space=pl.ANY)
    dma = pltpu.SemaphoreType.DMA
    return pl.pallas_call(
        functools.partial(pack_kernel, n, first, widths, len(audio), len(keep), staged, columns),
        out_shape=tuple(sds(x) for x in shapes) + tuple(sds(x.shape) for x in keep),
        in_specs=[stay] * 3 + [whole()] * len(audio) + [stay] * len(keep),
        out_specs=(stay if staged else whole(),) * (len(shapes) + len(keep)),
        scratch_shapes=[pltpu.VMEM(x, BF16) for x in shapes if staged]
        + [dma((3 * len(shapes),)), dma((len(shapes) + len(keep),))],
        compiler_params=pltpu.CompilerParams(vmem_limit_bytes=limit * MIB),
        cost_estimate=pl.CostEstimate(flops=0, bytes_accessed=moved, transcendentals=0),
    )(*video, *audio, *keep)


def audio_rows(tails, part, pair, rows, pairs):
    per = tails[0].shape[1] // LANES
    at, side = (part * pairs + pair) // per * rows, pair % per * LANES
    return jnp.concatenate([t[at : at + rows, side : side + LANES] for t in tails], axis=0)


def attend_heads(pieces, tokens, put):
    scale = LOG2E / math.sqrt(VHEAD)
    for h in range(pieces[0].shape[1] // VHEAD):
        cols = slice(h * VHEAD, (h + 1) * VHEAD)
        keys = jnp.concatenate([p[tokens : 2 * tokens, cols] for p in pieces], axis=0)
        values = jnp.concatenate([p[2 * tokens : 3 * tokens, cols] for p in pieces], axis=0)
        values = jnp.concatenate([values, jnp.ones_like(values)], axis=1)
        for s, p in enumerate(pieces):
            t = lax.dot_general(p[0:tokens, cols], keys, NT, preferred_element_type=F32)
            w = jnp.exp2((t - jnp.max(t, axis=1, keepdims=True)) * scale)
            o = jnp.dot(w.astype(BF16), values, preferred_element_type=F32)
            put(s, h, (o[:, :VHEAD] / o[:, VHEAD:]).astype(BF16))


def first_kernel(n, tokens, *refs):
    pieces, outs = refs[:n], refs[n:]

    def put(s, h, rows):
        outs[s][:, h * VHEAD : (h + 1) * VHEAD] = rows

    attend_heads(pieces, tokens, put)


def middle_kernel(n, *refs):
    pieces, before, last = refs[:n], refs[n : 2 * n], refs[2 * n : 3 * n]
    outs, sem = refs[3 * n : -1], refs[-1]
    tokens = last[0].shape[0] // 3
    early, width = before[0].shape[1], outs[0].shape[1]
    copies = []
    for s in range(n):
        top, below = pl.ds(0, 3 * tokens), pl.ds(3 * tokens, tokens)
        copies.append(pltpu.make_async_copy(last[s], outs[s].at[top, :], sem.at[2 * s]))
        to = outs[s].at[below, pl.ds(0, early)]
        copies.append(pltpu.make_async_copy(before[s], to, sem.at[2 * s + 1]))
    for copy in copies:
        copy.start()

    def put(s, h, rows):
        at = early + h * VHEAD
        low, side = (3 + at // width) * tokens, at % width
        outs[s][low : low + tokens, side : side + VHEAD] = rows

    attend_heads(pieces, tokens, put)
    for copy in copies:
        copy.wait()


def middle(chunk, before, last, n, moved):
    tokens = last[0].shape[0] // 3
    width = last[0].shape[1]
    tall = tokens * (3 + (before[0].shape[1] + chunk[0].shape[1]) // width)
    stay = pl.BlockSpec(memory_space=pl.ANY)
    return pl.pallas_call(
        functools.partial(middle_kernel, n),
        out_shape=(sds((tall, width)),) * n,
        in_specs=[whole()] * n + [stay] * (2 * n),
        out_specs=(whole(),) * n,
        scratch_shapes=[pltpu.SemaphoreType.DMA((2 * n,))],
        compiler_params=pltpu.CompilerParams(vmem_limit_bytes=16 * MIB),
        cost_estimate=pl.CostEstimate(flops=0, bytes_accessed=moved, transcendentals=0),
    )(*chunk, *before, *last)


def last_kernel(n, tokens, *refs):
    pieces, sums, outs = refs[:n], refs[n : 2 * n], refs[2 * n :]
    width = outs[0].shape[1]

    def put(s, h, rows):
        outs[s][:tokens, h * VHEAD : (h + 1) * VHEAD] = rows

    for s in range(n):
        part = sums[s][...].astype(F32)
        blocks = [part[:, c : c + width] for c in range(0, part.shape[1], width)]
        outs[s][tokens:, :] = jnp.concatenate(blocks, axis=0).astype(BF16)
    attend_heads(pieces, tokens, put)


def unpack_kernel(n, heads, tokens, *refs):
    middles, lasts, own = refs[:n], refs[n : 2 * n][::-1], refs[2 * n]
    out, mlp, sem = refs[2 * n + 1 :]
    me = lax.axis_index("seq")
    width = lasts[0].shape[1]
    group = heads * VHEAD
    copies = []

    def start(source, owner, first, size):
        at = pl.ds(pl.multiple_of(owner * group + first, LANES), size)
        copies.append(pltpu.make_async_copy(source, out.at[:, at], sem.at[len(copies)]))
        copies[-1].start()

    early = group - width
    for s in range(n):
        for c in range(0, early, width):
            rows = pl.ds(3 * tokens + c // width * tokens, tokens)
            size = min(width, early - c)
            start(middles[s].at[rows, pl.ds(0, size)], lax.bitwise_xor(me, s), c, size)
        start(lasts[s].at[pl.ds(0, tokens), :], lax.bitwise_xor(me, s), early, width)
    rows, columns = own.shape
    tails = [lasts[s][tokens:, :].astype(F32) for s in range(1, n)]
    for c in range(columns // width):
        total = own[:, c * width : (c + 1) * width]
        for tail in tails:
            total = total + tail[c * rows : (c + 1) * rows]
        mlp[:, c * width : (c + 1) * width] = total.astype(BF16)
    for copy in copies:
        copy.wait()


def unpack(middles, lasts, own, n, heads, tokens):
    count = n * (-(-(heads * VHEAD - lasts[0].shape[1]) // lasts[0].shape[1]) + 1)
    return pl.pallas_call(
        functools.partial(unpack_kernel, n, heads, tokens),
        out_shape=(sds((tokens, n * heads * VHEAD)), sds(own.shape)),
        in_specs=[pl.BlockSpec(memory_space=pltpu.VMEM)] * (2 * n + 1),
        out_specs=(pl.BlockSpec(memory_space=pl.ANY), whole()),
        scratch_shapes=[pltpu.SemaphoreType.DMA((count,))],
        compiler_params=pltpu.CompilerParams(vmem_limit_bytes=16 * MIB),
    )(*middles, *lasts[::-1], own)


def low_half(shape):
    return lax.broadcasted_iota(jnp.int32, shape, 1) < CHEAD


def listen_kernel(n, tokens, rows, *refs):
    pieces, keys, values, out = refs[:n][::-1], refs[n], refs[n + 1], refs[n + 2]
    columns = keys.shape[1]
    pairs = columns // LANES
    tails = [p[3 * tokens :, :].astype(F32) for p in pieces]
    count = n * rows
    scale = LOG2E / math.sqrt(CHEAD)
    low = low_half((count, LANES))
    lane = lax.broadcasted_iota(jnp.int32, (count, LANES), 1)
    peaks = jnp.zeros((count, LANES), F32)
    totals = jnp.zeros((count, LANES), F32)
    heads = columns // CHEAD
    for pair in range(pairs):
        cols = slice(pair * LANES, (pair + 1) * LANES)
        qp = audio_rows(tails, 0, pair, rows, pairs)
        both = jnp.concatenate([jnp.where(low, qp, 0.0), jnp.where(low, 0.0, qp)], axis=0)
        s = lax.dot_general(both.astype(BF16), keys[:, cols], NT, preferred_element_type=F32)
        s = s * scale
        peak = jnp.max(s, axis=1, keepdims=True)
        w = jnp.exp2(s - peak)
        wide = jnp.concatenate([values[:, cols], jnp.ones_like(values[:, cols])], axis=1)
        o = jnp.dot(w.astype(BF16), wide, preferred_element_type=F32)
        o, total = o[:, :LANES] / o[:, LANES:], o[:, LANES:]
        out[:, cols] = jnp.where(low, o[:count], o[count:]).astype(BF16)
        for i in range(2):
            head = lane == 2 * pair + i
            peaks = jnp.where(head, peak[i * count : (i + 1) * count], peaks)
            totals = jnp.where(head, total[i * count : (i + 1) * count], totals)
    out[:, columns:] = share_stats(peaks[:, :heads], totals[:, :heads])


def read_shares(wholes, columns):
    heads = columns // CHEAD
    peaks, totals, parts = [], [], []
    for whole in wholes:
        parts.append(whole[:, :columns])
        piece = [whole[:, columns + j * heads : columns + (j + 1) * heads] for j in range(6)]
        peaks.append(piece[0] + piece[1] + piece[2])
        totals.append(piece[3] + piece[4] + piece[5])
    top = functools.reduce(jnp.maximum, peaks)
    weight = [t * jnp.exp2(p - top) for t, p in zip(totals, peaks)]
    every = functools.reduce(jnp.add, weight)
    return parts, [w / every for w in weight], top, every


def reorder(whole, order, n):
    rows = whole.shape[0] // n
    return jnp.concatenate([whole[(i ^ order) * rows :][:rows] for i in range(n)], axis=0)


def joint(parts, weight, pair):
    low = low_half((parts[0].shape[0], LANES))
    o = jnp.zeros(low.shape, F32)
    for w, part in zip(weight, parts):
        a, b = w[:, 2 * pair : 2 * pair + 1], w[:, 2 * pair + 1 : 2 * pair + 2]
        o = o + jnp.where(low, a, b) * part[:, pair * LANES : (pair + 1) * LANES]
    return o.astype(BF16)


def share_stats(peaks, totals):
    stats = jnp.concatenate(parts3(peaks) + parts3(totals), axis=1)
    rest = jnp.zeros((stats.shape[0], LANES - stats.shape[1]), F32)
    return jnp.concatenate([stats, rest], axis=1).astype(BF16)


def merge_kernel(n, order, tokens, own, other, mine, second, out):
    count, columns = own.shape[0], own.shape[1] - LANES
    wholes = own[...].astype(F32), reorder(other[...].astype(F32), order, n)
    parts, weight, top, every = read_shares(wholes, columns)
    for pair in range(columns // LANES):
        out[:, pair * LANES : (pair + 1) * LANES] = joint(parts, weight, pair)
    out[:, columns : columns + LANES] = share_stats(top, every)
    at = columns + LANES
    for ref in (mine, second):
        for row in range(3 * tokens, ref.shape[0], count):
            out[:, at : at + LANES] = ref[row : row + count, :]
            at += LANES


def combine_kernel(n, tokens, rows, *refs):
    got, pieces, (gain, up) = refs[:2], refs[2 : 2 + n], refs[2 + n : 4 + n]
    own_sum, sent_sum, seen, x_ref = refs[4 + n :]

    @pl.when(pl.program_id(0) == 0)
    def _():
        columns = seen.shape[1]
        wholes = []
        for ref, order in zip(got, (0, 1)):
            wholes.append(reorder(ref[:, : columns + LANES].astype(F32), order, n))
        parts, weight, _, _ = read_shares(wholes, columns)
        tails = [p[3 * tokens :, :].astype(F32) for p in pieces]
        square = jnp.zeros((n * rows, 1), F32)
        for pair in range(columns // LANES):
            cols = slice(pair * LANES, (pair + 1) * LANES)
            o = joint(parts, weight, pair)
            seen[:, cols] = o[:rows]
            residual = audio_rows(tails, 1, pair, rows, columns // LANES) + o.astype(F32)
            square = square + jnp.sum(residual * residual, axis=1, keepdims=True)
            at = pl.ds(pl.multiple_of(lax.axis_index("tp") * columns + pair * LANES, LANES), LANES)
            x_ref[:, cols] = (residual * gain[:, at]).astype(BF16)
        lane = lax.broadcasted_iota(jnp.int32, (n * rows, LANES), 1)
        first, second, third = parts3(square)
        spread = jnp.where(lane == 0, first, jnp.where(lane == 1, second, third))
        spread = jnp.where(lane < 3, spread, 0.0)
        own_sum[0, :, :LANES] = spread
        sent_sum[0, :, :LANES] = spread.astype(BF16)

    @pl.when(pl.program_id(0) > 0)
    def _():
        product = jnp.dot(x_ref[...], up[...], preferred_element_type=F32)
        own_sum[0] = product
        sent_sum[0] = product.astype(BF16)


def combine(got, pieces, gain, up, tokens, rows, block):
    n = len(pieces)
    columns, units = up.shape
    steps = units // block + 1
    held = lambda ref: pl.BlockSpec(ref.shape, lambda i: (0,) * ref.ndim)
    moved = pl.BlockSpec((1, n * rows, block), lambda i: (i, 0, 0))
    return pl.pallas_call(
        functools.partial(combine_kernel, n, tokens, rows),
        grid=(steps,),
        out_shape=(
            sds((steps, n * rows, block), F32),
            sds((steps, n * rows, block)),
            sds((rows, columns)),
        ),
        in_specs=[held(r) for r in (*got, *pieces, gain)]
        + [pl.BlockSpec((columns, block), lambda i: (0, jnp.maximum(i - 1, 0)))],
        out_specs=(moved, moved, pl.BlockSpec((rows, columns), lambda i: (0, 0))),
        scratch_shapes=[pltpu.VMEM((n * rows, columns), BF16)],
        compiler_params=pltpu.CompilerParams(vmem_limit_bytes=32 * MIB),
        cost_estimate=pl.CostEstimate(
            flops=0, bytes_accessed=0 * MIB, transcendentals=0
        ),
    )(*got, *pieces, gain, up)


def finish_kernel(n, features, own, other, down, *refs):
    outs, hidden = refs[:n], refs[n]
    rows = outs[0].shape[0]

    @pl.when(pl.program_id(0) == 0)
    def _():
        square = own[0, :, :LANES] + other[0, :, :LANES].astype(F32)
        square = jnp.sum(square, axis=1, keepdims=True)
        scale = lax.rsqrt(square / features + 1e-6)
        block = own.shape[2]
        for i in range(1, own.shape[0]):
            total = (own[i] + other[i].astype(F32)) * scale
            hidden[:, (i - 1) * block : i * block] = jax.nn.gelu(total).astype(BF16)

    product = jnp.dot(hidden[...], down[...], preferred_element_type=F32)
    for s in range(n):
        outs[s][...] = product[s * rows : (s + 1) * rows].astype(outs[s].dtype)


def finish(own, other, down, n, rows, features, block):
    units, columns = down.shape
    held = lambda ref: pl.BlockSpec(ref.shape, lambda i: (0,) * ref.ndim)
    return pl.pallas_call(
        functools.partial(finish_kernel, n, features),
        grid=(columns // block,),
        out_shape=(sds((rows, columns), F32),) + (sds((rows, columns)),) * (n - 1),
        in_specs=[held(own), held(other), pl.BlockSpec((units, block), lambda i: (0, i))],
        out_specs=(pl.BlockSpec((rows, block), lambda i: (0, i)),) * n,
        scratch_shapes=[pltpu.VMEM((n * rows, units), BF16)],
        compiler_params=pltpu.CompilerParams(vmem_limit_bytes=32 * MIB),
        cost_estimate=pl.CostEstimate(
            flops=0, bytes_accessed=0 * MIB, transcendentals=0
        ),
    )(own, other, down)


def heard_kernel(n, tokens, rows, q, own, second, first, out):
    pairs = q.shape[1] // LANES
    at = first.shape[1] - 2 * (own.shape[0] - 3 * tokens) // first.shape[0] * LANES
    half = (first.shape[1] - at) // 2
    far = [
        jnp.concatenate([first[:, c : c + LANES] for c in range(start, start + half, LANES)], axis=0)
        for start in (at, at + half)
    ]
    tails = [own[3 * tokens :, :], far[0], second[3 * tokens :, :], far[1]]
    tails = [tail.astype(F32) for tail in tails]
    count = n * rows
    low = low_half((count, LANES))
    scale = LOG2E / math.sqrt(CHEAD)

    def both(part, pair):
        x = audio_rows(tails, part, pair, rows, pairs)
        return jnp.concatenate([jnp.where(low, x, 0.0), jnp.where(low, 0.0, x)], axis=0).astype(BF16)

    for pair in range(pairs):
        cols = slice(pair * LANES, (pair + 1) * LANES)
        s = lax.dot_general(both(0, pair), q[:, cols], NT, preferred_element_type=F32) * scale
        probs = []
        for i in range(2):
            t = s[i * count : (i + 1) * count]
            w = jnp.exp2(t - jnp.max(t, axis=0, keepdims=True))
            probs.append(w / jnp.sum(w, axis=0, keepdims=True))
        w = jnp.concatenate(probs, axis=0).astype(BF16)
        out[:, cols] = lax.dot_general(w, both(1, pair), TN, preferred_element_type=F32).astype(BF16)


def short_body(vq, vk, vv, cq, ak, av, aq, ck, cv, ai, gain, up, down):
    n = lax.axis_size("seq")
    tokens = vq.shape[0]
    rows, columns = aq.shape
    features = ai.shape[1]
    heads = vq.shape[1] // n // VHEAD
    widths = [c * VHEAD for c in (1, 1, heads - 2)]
    video = (vq, vk, vv)

    def send(own, *first):
        return [own[0]] + [trade(after(own[s], *first), s) for s in range(1, n)]

    wait = 16 * MIB
    packed = pack(video, (aq, ai), range(n), (), n, 0, widths[:1], 60, 6 * vq.size, True)
    chunk_0 = send(packed)
    packed = pack(video, (ak, av), (0, 2), (), n, widths[0], widths[1:2], 60, wait, True)
    chunk_1 = send(packed)
    keep = (chunk_0[0], chunk_1[0], ck, cv)
    packed = pack(video, (), (), keep, n, widths[0] + widths[1], widths[2:], 16, wait, False)
    *packed, chunk_0[0], chunk_1[0], ck, cv = packed
    (share,) = call(
        functools.partial(listen_kernel, n, tokens, rows),
        (*chunk_0[::-1], ck, cv),
        [sds((n * rows, columns + LANES))],
        moved=4 * vq.size,
        limit=16,
    )
    order = n // 2
    while order > 2:
        (share,) = call(
            functools.partial(merge_kernel, n, order),
            (share, trade(share, order)),
            [sds(share.shape)],
            limit=16,
        )
        order //= 2
    shares = [share, trade(share, 2)] if n > 2 else [share]
    first = call(
        functools.partial(first_kernel, n, tokens),
        (after(chunk_0[0], share), *chunk_0[1:]),
        [sds((tokens, widths[0]))] * n,
        limit=16,
    )
    built = middle(chunk_1, first, packed, n, MIB)
    wide = share.shape[1] + 4 * rows * columns // share.shape[0]
    (share,) = call(
        functools.partial(merge_kernel, n, 2, tokens),
        (after(shares[0], built[0]), shares[1], chunk_1[0], chunk_1[2]),
        [sds((share.shape[0], wide))],
        limit=16,
    )
    below = trade(share, 1)
    chunk_2 = [built[0]] + [trade(after(built[s], below), s) for s in range(1, 2)]
    chunk_2 += [trade(after(built[s], share), s) for s in range(2, n)]
    (heard,) = call(
        functools.partial(heard_kernel, n, tokens, rows),
        (cq, chunk_1[0], chunk_1[2], below),
        [sds(cq.shape)],
        moved=0,
        limit=16,
    )
    gain = after(gain.reshape(1, -1), heard)
    own_sum, sent_sum, seen = combine((share, below), chunk_0, gain, up, tokens, rows, 512)
    other_sum = lax.ppermute(sent_sum, "tp", [(0, 1), (1, 0)])
    results = finish(own_sum, other_sum, down, n, rows, features, 512)
    ends = call(
        functools.partial(last_kernel, n, tokens),
        (*chunk_2, *results),
        [sds((tokens + rows * columns // widths[2], widths[2]))] * n,
        limit=16,
    )
    ends = [ends[0]] + [trade(ends[s], s) for s in range(1, n)]
    mixed, mlp = unpack(chunk_2, ends, results[0], n, heads, tokens)
    return mixed, heard, seen, mlp


def fits(vq, cq, aq, up, down):
    n = lax.axis_size("seq")
    heads = vq.shape[1] // VHEAD
    return (
        n == 4
        and lax.axis_size("tp") == 2
        and heads % n == 0
        and heads // n == 4
        and vq.shape[0] == LANES
        and n * vq.shape[0] <= 1024
        and aq.shape[0] % 8 == 0
        and n * aq.shape[0] <= 64
        and 6 * (aq.shape[1] // CHEAD) < LANES
        and aq.shape[1] % VHEAD == 0
        and up.shape[1] % 512 == 0
        and down.shape[1] % 512 == 0
    )


def body(*args):
    *arrays, gain, up, down = args
    arrays = [a[0] for a in arrays]
    path = short_body if fits(arrays[0], arrays[3], arrays[6], up, down) else general_body
    return tuple(out[None] for out in path(*arrays, gain, up, down))


def solution(mesh):
    rows = P(("clips", "dp"), "seq", "tp")
    placed = (rows,) * 9 + (P(("clips", "dp"), "seq", None), P(), P("tp", "seq"), P("seq", "tp"))
    return jax.shard_map(
        body, mesh=mesh, in_specs=placed, out_specs=(rows,) * 4, check_vma=False
    )
```
